32 devices in a mesh: row: 4 (over x, core), col: 8 (over z, y).
Axes of the slice: x: 2, y: 2, z: 4, core: 2. Of those that a mesh axis runs over, the one named last changes fastest.
Arguments:
- density: bfloat16 [1024, 3, 256], P(('row', 'col')), may hold values from -6 to 6
- coords: bfloat16 [1024, 3, 256], P(('row', 'col')), may hold values from 0 to 1
- basis: bfloat16 [1024, 32, 768], P(('row', 'col')), may hold values from -0.21875 to 0.21875
- transfer: float32 [1024, 32, 32], P(('row', 'col')), may hold values from -1 to 1
- parent: int32 [1024], replicated, may hold values from 0 to 255
- near_pairs: int32 [2, 4096], P(None, ('row', 'col')), may hold values from 0 to 1023, as said below
- near_count: int32 [32], P(('row', 'col')), may hold values from 16 to 128, as said below
- far_pairs: int32 [2, 2048], P(None, ('row', 'col')), may hold values from 0 to 255
- coupling: float32 [2048, 32, 32], P(('row', 'col')), may hold values from -1 to 1
Outputs:
- velocity: float32 [1024, 3, 256], P(('row', 'col'))
The draws below stay inside these ranges and needn't reach their ends.
Inputs may be any that keep to these rules, and one draw needn't show every extreme that they name: `near_pairs`: let i = j % 128 for slot j of device (r, c), owners in row-major order with 32 clusters each. The first cluster is owned by device (r, i // (128 // 8)) and the second by device (i // (128 // 4), c); the two may be equal. Slots past a device's live count hold valid but unused pairs. `near_count`: the largest live count equals 128 in every draw.
All inputs are finite; a program needn't handle non-finite values.
Results may differ from the reference program's by a relative error of at most 0.0026.
Values may be sent and summed in bfloat16 or wider, within the bound.
A program may use at most 64 MiB of HBM per device.

```python
import math
import jax
import jax.numpy as jnp
from jax import lax

CL = 256
R = 32
CPD = 32
NC = 1024
NPAR = 256
NP_DEV = 128
NF = 2048
N_ROW = 4
N_COL = 8


def draw_near_pairs(key, part):
    key = jax.random.fold_in(key, 7)
    devices = N_ROW * N_COL
    row_span = CPD * N_COL
    slots = jnp.arange(devices * NP_DEV, dtype=jnp.int32)
    owner = slots // NP_DEV
    within_dev = slots % NP_DEV
    owner_row = owner // N_COL
    owner_col = owner % N_COL
    dest_col = within_dev // (NP_DEV // N_COL)
    dest_row = within_dev // (NP_DEV // N_ROW)
    key_first, key_inner = jax.random.split(key, 2)
    first_ids = owner_row * row_span + dest_col * CPD + jax.random.randint(key_first, slots.shape, 0, CPD, dtype=jnp.int32)
    second_ids = dest_row * row_span + owner_col * CPD + jax.random.randint(key_inner, slots.shape, 0, CPD, dtype=jnp.int32)
    return jnp.stack([first_ids, second_ids]).astype(jnp.int32)


def draw_near_count(key, part):
    key = jax.random.fold_in(key, 11)
    devices = N_ROW * N_COL
    key_counts, key_full = jax.random.split(key)
    counts = jax.random.randint(key_counts, (devices,), NP_DEV // 8, NP_DEV // 2 + 1, dtype=jnp.int32)
    fullest = jax.random.randint(key_full, (), 0, devices, dtype=jnp.int32)
    return jnp.where(jnp.arange(devices, dtype=jnp.int32) == fullest, NP_DEV, counts).astype(jnp.int32)


def plant(values, own_key, smallest, high):
    spot = [jax.random.randint(jax.random.fold_in(own_key, axis), (), 0, length) for axis, length in enumerate(values.shape)]
    widest = values.shape.index(max(values.shape))
    next_to = spot[:widest] + [(spot[widest] + 1) % values.shape[widest]] + spot[widest + 1:]
    return values.at[tuple(spot)].set(smallest).at[tuple(next_to)].set(high)


def steps_of(stream_key, extent, cuts, least, top_value):
    gain, own = 1.0, jax.random.fold_in(stream_key, 6)
    for position, shards_of in cuts:
        draws = jnp.exp(jax.random.uniform(jax.random.fold_in(own, position), (shards_of,), jnp.float32, least / len(cuts), top_value / len(cuts)))
        gain = gain * jnp.repeat(draws, extent[position] // shards_of).reshape([-1 if axis == position else 1 for axis in range(len(extent))])
    return gain


def bell_draw(key, extent, scale, reach, pieces=(), kind=jnp.bfloat16):
    factor_of = steps_of(key, extent, pieces, -0.22, 0.18) if pieces else 1.0
    result = jax.random.normal(key, extent, jnp.float32) * scale * factor_of
    return jnp.minimum(jnp.maximum(result, -reach), reach).astype(kind)


def setup_inputs(seed: int = 0) -> dict:
    keys = jax.random.split(jax.random.key(seed), 10)
    return {
        "density": bell_draw(keys[0], (NC, 3, CL), 1.0, 6.0, ((0, 32),)),
        "coords": jnp.clip(1.0 * jax.random.uniform(keys[1], (NC, 3, CL), jnp.float32) ** steps_of(keys[1], (NC, 3, CL), ((0, 32),), -0.2, 0.2), 0.0, 1.0).astype(jnp.bfloat16),
        "basis": bell_draw(keys[2], (NC, R, 3 * CL), (3 * CL) ** -0.5, 0.21875, ((0, 32),)),
        "transfer": bell_draw(keys[3], (NC, R, R), R ** -0.5, 1.0, ((0, 32),), jnp.float32),
        "parent": plant(jax.random.randint(keys[4], (NC,), 0, NPAR), jax.random.fold_in(keys[4], 1), 0, NPAR - 1).astype(jnp.int32),
        "near_pairs": draw_near_pairs(jax.random.fold_in(keys[9], 71), 0),
        "near_count": draw_near_count(jax.random.fold_in(keys[9], 71), 0),
        "far_pairs": plant(jax.random.randint(keys[7], (2, NF), 0, NPAR), jax.random.fold_in(keys[7], 1), 0, NPAR - 1).astype(jnp.int32),
        "coupling": bell_draw(keys[8], (NF, R, R), R ** -0.5, 1.0, ((0, 32),), jnp.float32),
    }


REG_EPS = 0.02
STOKES_SCALE = 1.0 / (8.0 * math.pi)

def stokeslet(near_x, far_x):
    offset = near_x[:, :, :, None] - far_x[:, :, None, :]
    dist_sq = lax.optimization_barrier(jnp.sum(offset * offset, axis=1))
    inv_dist = lax.rsqrt(dist_sq + REG_EPS * REG_EPS)
    inv_cube = inv_dist * inv_dist * inv_dist
    isotropic = (dist_sq + 2.0 * REG_EPS * REG_EPS) * inv_cube
    dyadic = offset[:, :, None] * offset[:, None, :] * inv_cube[:, None, None]
    identity = jnp.eye(3, dtype=jnp.float32)
    return (dyadic + identity[None, :, :, None, None] * isotropic[:, None, None]) * STOKES_SCALE

def near_field(density, coords, near_pairs, near_count):
    accumulated = jnp.zeros((NC, 3, CL), jnp.float32)

    def per_device(accumulated, device):
        live_pairs = near_count[device]

        def per_block(slot_block, accumulated):
            first_slot = (device * NP_DEV + slot_block * 4).astype(jnp.int32)
            glob_a = lax.dynamic_slice_in_dim(near_pairs[0], first_slot, 4)
            glob_b = lax.dynamic_slice_in_dim(near_pairs[1], first_slot, 4)
            within = slot_block * 4 + jnp.arange(4, dtype=jnp.int32) < live_pairs
            row_keep = within.astype(jnp.float32)
            col_keep = (within & (glob_a != glob_b)).astype(jnp.float32)
            kernel_tile = stokeslet(coords[glob_a].astype(jnp.float32), coords[glob_b].astype(jnp.float32))
            kernel_tile = lax.optimization_barrier(kernel_tile.astype(jnp.bfloat16)).astype(jnp.float32)
            source_a = density[glob_a].astype(jnp.float32)
            source_b = density[glob_b].astype(jnp.float32)
            to_first = jnp.einsum('pijxy,pjy->pix', kernel_tile, source_b) * row_keep[:, None, None]
            to_second = jnp.einsum('pijxy,pix->pjy', kernel_tile, source_a) * col_keep[:, None, None]
            return accumulated.at[glob_a].add(to_first).at[glob_b].add(to_second)
        return (lax.fori_loop(0, (live_pairs + 3) // 4, per_block, accumulated), None)
    accumulated, unused = lax.scan(per_device, accumulated, jnp.arange(N_ROW * N_COL, dtype=jnp.int32))
    return accumulated

def far_field(density, basis, transfer, parent, far_pairs, coupling):
    highest = lax.Precision.HIGHEST
    basis_wide = basis.astype(jnp.float32)
    moments = jnp.einsum('crk,ck->cr', basis_wide, density.reshape(NC, 3 * CL).astype(jnp.float32), precision=highest)
    lifted = jnp.einsum('crs,cs->cr', transfer, moments, precision=highest)
    parent_moments = jnp.zeros((NPAR, R), jnp.float32).at[parent].add(lifted)
    to_first = jnp.einsum('krs,ks->kr', coupling, parent_moments[far_pairs[1]], precision=highest)
    to_second = jnp.einsum('ksr,ks->kr', coupling, parent_moments[far_pairs[0]], precision=highest)
    parent_locals = jnp.zeros((NPAR, R), jnp.float32).at[far_pairs[0]].add(to_first).at[far_pairs[1]].add(to_second)
    local_coef = jnp.einsum('csr,cs->cr', transfer, parent_locals[parent], precision=highest)
    return jnp.einsum('crk,cr->ck', basis_wide, local_coef, precision=highest).reshape(NC, 3, CL)

def reference(density, coords, basis, transfer, parent, near_pairs, near_count, far_pairs, coupling):
    near = near_field(density, coords, near_pairs, near_count)
    return near + far_field(density, basis, transfer, parent, far_pairs, coupling)
```

```python
import functools
import math

import jax
import jax.numpy as jnp
from jax import lax
from jax.experimental import pallas as pl
from jax.experimental.pallas import tpu as pltpu
from jax.sharding import PartitionSpec as P

REG_EPS = 0.02
STOKES_SCALE = 1.0 / (8.0 * math.pi)
MESH = pl.DeviceIdType.MESH
GROUP = 4
CHUNK = 16


def greet(n_row, n_col, row, col):
    barrier = pltpu.get_barrier_semaphore()
    for k in range(1, n_col):
        pl.semaphore_signal(barrier, inc=1, device_id=(row, lax.rem(col + k, n_col)), device_id_type=MESH)
    for k in range(1, n_row):
        pl.semaphore_signal(barrier, inc=1, device_id=(lax.rem(row + k, n_row), col), device_id_type=MESH)
    pl.semaphore_wait(barrier, n_col + n_row - 2)


def part(ref, index, size):
    return ref.at[pl.ds(pl.multiple_of(index * size, size), size)]


def gather_kernel(n_row, n_col, n_z, tile, ids, lifted, row_tiles, col_tiles, row_ids, col_ids, all_lifted,
                  own_sem, st, rt, sct, rct, si, ri, sci, rci, sl, rl, scl, rcl):
    row, col = lax.axis_index("row"), lax.axis_index("col")
    n_y = n_col // n_z
    z, y = col // n_y, lax.rem(col, n_y)
    rows, id_rows, lift_rows = tile.shape[0], ids.shape[0], lifted.shape[0]
    span = n_col * lift_rows
    own = [
        pltpu.make_async_copy(tile, part(row_tiles, col, rows), own_sem.at[0]),
        pltpu.make_async_copy(tile, part(col_tiles, row, rows), own_sem.at[1]),
        pltpu.make_async_copy(ids, part(row_ids, col, id_rows), own_sem.at[2]),
        pltpu.make_async_copy(ids, part(col_ids, row, id_rows), own_sem.at[3]),
        pltpu.make_async_copy(lifted, part(all_lifted, row * n_col + col, lift_rows), own_sem.at[4]),
    ]
    for copy in own:
        copy.start()
    greet(n_row, n_col, row, col)

    def to_col(src, dst, index, size, sends, recvs, slot, peer):
        return pltpu.make_async_remote_copy(
            src_ref=src, dst_ref=part(dst, index, size), send_sem=sends.at[slot], recv_sem=recvs.at[index],
            device_id=(row, peer), device_id_type=MESH)

    def to_row(src, dst_view, sends, recvs, peer):
        return pltpu.make_async_remote_copy(
            src_ref=src, dst_ref=dst_view, send_sem=sends.at[peer], recv_sem=recvs.at[row],
            device_id=(peer, col), device_id_type=MESH)

    started = []

    def go(copy):
        copy.start()
        started.append(copy)

    for k in range(1, n_col):
        peer = lax.rem(col + k, n_col)
        go(pltpu.make_async_remote_copy(
            src_ref=lifted, dst_ref=part(all_lifted, row * n_col + col, lift_rows),
            send_sem=sl.at[peer], recv_sem=rl.at[col], device_id=(row, peer), device_id_type=MESH))
    for k in range(1, n_z):
        peer = lax.rem(z + k, n_z) * n_y + y
        go(to_col(tile, row_tiles, col, rows, st, rt, k, peer))
    for k in range(1, n_y):
        peer = z * n_y + lax.rem(y + k, n_y)
        go(to_col(tile, row_tiles, col, rows, st, rt, n_z + k, peer))
    for k in range(1, n_row):
        peer = lax.rem(row + k, n_row)
        go(to_row(tile, part(col_tiles, row, rows), sct, rct, peer))
        go(to_row(ids, part(col_ids, row, id_rows), sci, rci, peer))
    for k in range(1, n_col):
        peer = lax.rem(col + k, n_col)
        go(to_col(ids, row_ids, col, id_rows, si, ri, peer, peer))

    own[4].wait()
    for k in range(1, n_col):
        src = lax.rem(col + k, n_col)
        pltpu.make_async_copy(lifted, part(all_lifted, row * n_col + src, lift_rows), rl.at[src]).wait()
    for k in range(1, n_row):
        peer = lax.rem(row + k, n_row)
        mine = part(all_lifted, row, span)
        go(to_row(mine, mine, scl, rcl, peer))

    for k in range(1, n_z):
        src = lax.rem(z + k, n_z) * n_y + y
        pltpu.make_async_copy(tile, part(row_tiles, src, rows), rt.at[src]).wait()
        for j in range(1, n_y):
            peer = z * n_y + lax.rem(y + j, n_y)
            go(to_col(part(row_tiles, src, rows), row_tiles, src, rows, st, rt, n_z + n_y * k + j, peer))
    for j in range(1, n_y):
        for k in range(n_z):
            src = lax.rem(z + k, n_z) * n_y + lax.rem(y + j, n_y)
            pltpu.make_async_copy(tile, part(row_tiles, src, rows), rt.at[src]).wait()
    for k in range(1, n_col):
        src = lax.rem(col + k, n_col)
        pltpu.make_async_copy(ids, part(row_ids, src, id_rows), ri.at[src]).wait()
    for k in range(1, n_row):
        src = lax.rem(row + k, n_row)
        pltpu.make_async_copy(tile, part(col_tiles, src, rows), rct.at[src]).wait()
        pltpu.make_async_copy(ids, part(col_ids, src, id_rows), rci.at[src]).wait()
        view = part(all_lifted, src, span)
        pltpu.make_async_copy(view, view, rcl.at[src]).wait()
    for copy in own[:4]:
        copy.wait()
    for copy in started:
        copy.wait_send()


def gather(n_row, n_col, tile, ids, lifted):
    n_z = 4 if n_col % 4 == 0 else 1
    any_space = pl.BlockSpec(memory_space=pl.ANY)
    dma = pltpu.SemaphoreType.DMA
    sizes = [(5,), (n_z * (n_col // n_z + 1) + n_col,), (n_col,), (n_row,), (n_row,), (n_col,), (n_col,),
             (n_row,), (n_row,), (n_col,), (n_col,), (n_row,), (n_row,)]
    shape = jax.ShapeDtypeStruct
    return pl.pallas_call(
        functools.partial(gather_kernel, n_row, n_col, n_z),
        out_shape=[
            shape((n_col * tile.shape[0], tile.shape[1]), tile.dtype),
            shape((n_row * tile.shape[0], tile.shape[1]), tile.dtype),
            shape((n_col * ids.shape[0], ids.shape[1]), ids.dtype),
            shape((n_row * ids.shape[0], ids.shape[1]), ids.dtype),
            shape((n_row * n_col * lifted.shape[0], lifted.shape[1]), lifted.dtype),
        ],
        in_specs=[any_space] * 3,
        out_specs=[any_space] * 5,
        scratch_shapes=[dma(size) for size in sizes],
        compiler_params=pltpu.CompilerParams(collective_id=1, has_side_effects=True),
        name="gather",
    )(tile, ids, lifted)


def near_kernel(first, second, live, row_tiles, col_tiles, out_first, out_second, row_wide, col_wide, iso, ga, gb):
    block = 256
    for narrow, wide in ((row_tiles, row_wide), (col_tiles, col_wide)):
        @pl.loop(0, narrow.shape[0] // block)
        def _(step):
            at = pl.ds(pl.multiple_of(step * block, block), block)
            wide[at, :] = narrow[at, :].astype(jnp.float32)

    out_first[...] = jnp.zeros_like(out_first)
    out_second[...] = jnp.zeros_like(out_second)
    panels = row_tiles.shape[1]
    count = live[0]
    eps_sq = REG_EPS * REG_EPS
    across = (((1,), (1,)), ((), ()))
    down = (((1,), (0,)), ((), ()))

    def pair(slot, u):
        ta = row_wide[pl.ds(pl.multiple_of(first[slot] * 8, 8), 8), :]
        tb = col_wide[pl.ds(pl.multiple_of(second[slot] * 8, 8), 8), :]
        columns = ta.T
        for chunk in range(panels // CHUNK):
            at = slice(chunk * CHUNK, (chunk + 1) * CHUNK)
            cut = columns[at, :]
            offset = [cut[:, 3 + i:4 + i] - tb[3 + i:4 + i, :] for i in range(3)]
            dist_sq = offset[0] * offset[0] + offset[1] * offset[1] + offset[2] * offset[2]
            inv_dist = lax.rsqrt(dist_sq + eps_sq)
            inv_cube = inv_dist * inv_dist * inv_dist
            qa = offset[0] * tb[0:1, :] + offset[1] * tb[1:2, :] + offset[2] * tb[2:3, :]
            qb = offset[0] * cut[:, 0:1] + offset[1] * cut[:, 1:2] + offset[2] * cut[:, 2:3]
            iso[u, at, :] = ((dist_sq + 2.0 * eps_sq) * inv_cube).astype(jnp.bfloat16)
            ga[u, at, :] = (qa * inv_cube).astype(jnp.bfloat16)
            gb[u, at, :] = (qb * inv_cube).astype(jnp.bfloat16)
        na, nb = ta.astype(jnp.bfloat16), tb.astype(jnp.bfloat16)
        ua = lax.dot_general(nb, iso[u], across, preferred_element_type=jnp.float32)
        va = lax.dot_general(nb, ga[u], across, preferred_element_type=jnp.float32)
        ub = lax.dot_general(na, iso[u], down, preferred_element_type=jnp.float32)
        vb = lax.dot_general(na, gb[u], down, preferred_element_type=jnp.float32)
        to_first = (ua[0:3] + (ta[3:6] * va[6:7] - va[3:6])) * STOKES_SCALE
        to_second = (ub[0:3] + (vb[3:6] - tb[3:6] * vb[6:7])) * STOKES_SCALE
        within = slot < count
        keep_second = within & (live[1 + slot] != 0)
        to_first = jnp.where(within, to_first, 0.0)
        to_second = jnp.where(keep_second, to_second, 0.0)
        for i in range(3):
            out_first[pl.ds(slot, 1), i * panels:(i + 1) * panels] = to_first[i:i + 1]
            out_second[pl.ds(slot, 1), i * panels:(i + 1) * panels] = to_second[i:i + 1]

    def group(step, carry):
        for u in range(GROUP):
            pair(step * GROUP + u, u)
        return carry

    lax.fori_loop(0, (count + GROUP - 1) // GROUP, group, 0)


def near(first, second, live, row_tiles, col_tiles):
    slots, panels = first.shape[0], row_tiles.shape[1]
    smem = pl.BlockSpec(memory_space=pltpu.SMEM)
    vmem = pl.BlockSpec(memory_space=pltpu.VMEM)
    return pl.pallas_call(
        near_kernel,
        out_shape=[jax.ShapeDtypeStruct((slots, 3 * panels), jnp.float32)] * 2,
        in_specs=[smem, smem, smem, vmem, vmem],
        out_specs=[vmem, vmem],
        scratch_shapes=[
            pltpu.VMEM(row_tiles.shape, jnp.float32),
            pltpu.VMEM(col_tiles.shape, jnp.float32),
        ] + [pltpu.VMEM((GROUP, panels, panels), jnp.bfloat16)] * 3,
        compiler_params=pltpu.CompilerParams(vmem_limit_bytes=48 * 1024 * 1024),
        name="near",
    )(first, second, live, row_tiles, col_tiles)


def exchange_kernel(n_row, n_col, out_first, out_second, partial, got_first, got_second, total, f1, f2, acc, red,
                    own_sem, s1, r1, s2, r2, s3, r3, sa, ra, sb, rb):
    row, col = lax.axis_index("row"), lax.axis_index("col")
    ca, cb = out_first.shape[0] // n_col, out_second.shape[0] // n_row
    piece = partial.shape[0] // n_col
    own = [
        pltpu.make_async_copy(part(out_first, col, ca), part(got_first, col, ca), own_sem.at[0]),
        pltpu.make_async_copy(part(out_second, row, cb), part(got_second, row, cb), own_sem.at[1]),
    ]
    for copy in own:
        copy.start()
    f1[pl.ds(col, 1)] = partial[pl.ds(pl.multiple_of(col * piece, piece), piece), :][None]
    greet(n_row, n_col, row, col)
    started = []

    def send(src, dst, sends, recvs, slot, mine, device):
        copy = pltpu.make_async_remote_copy(
            src_ref=src, dst_ref=dst, send_sem=sends.at[slot], recv_sem=recvs.at[mine],
            device_id=device, device_id_type=MESH)
        copy.start()
        started.append(copy)

    for k in range(1, n_col):
        peer = lax.rem(col + k, n_col)
        send(part(partial, peer, piece), f1.at[col], s1, r1, peer, col, (row, peer))
    for k in range(1, n_col):
        peer = lax.rem(col + k, n_col)
        send(part(out_first, peer, ca), part(got_first, col, ca), sa, ra, peer, col, (row, peer))
    for k in range(1, n_row):
        peer = lax.rem(row + k, n_row)
        send(part(out_second, peer, cb), part(got_second, row, cb), sb, rb, peer, row, (peer, col))

    for k in range(1, n_col):
        src = lax.rem(col + k, n_col)
        pltpu.make_async_copy(f1.at[src], f1.at[src], r1.at[src]).wait()
    acc[...] = jnp.sum(f1[...], axis=0)
    f2[pl.ds(row, 1)] = acc[...][None]
    for k in range(1, n_row):
        peer = lax.rem(row + k, n_row)
        send(acc, f2.at[row], s2, r2, peer, row, (peer, col))
    for k in range(1, n_row):
        src = lax.rem(row + k, n_row)
        pltpu.make_async_copy(f2.at[src], f2.at[src], r2.at[src]).wait()
    red[...] = jnp.sum(f2[...], axis=0)
    keep = pltpu.make_async_copy(red, part(total, col, piece), own_sem.at[2])
    keep.start()
    for k in range(1, n_col):
        peer = lax.rem(col + k, n_col)
        send(red, part(total, col, piece), s3, r3, peer, col, (row, peer))
    for k in range(1, n_col):
        src = lax.rem(col + k, n_col)
        pltpu.make_async_copy(red, part(total, src, piece), r3.at[src]).wait()
        view = part(got_first, src, ca)
        pltpu.make_async_copy(view, view, ra.at[src]).wait()
    for k in range(1, n_row):
        src = lax.rem(row + k, n_row)
        view = part(got_second, src, cb)
        pltpu.make_async_copy(view, view, rb.at[src]).wait()
    keep.wait()
    for copy in own:
        copy.wait()
    for copy in started:
        copy.wait_send()


def exchange(n_row, n_col, out_first, out_second, partial):
    any_space = pl.BlockSpec(memory_space=pl.ANY)
    vmem = pl.BlockSpec(memory_space=pltpu.VMEM)
    dma = pltpu.SemaphoreType.DMA
    piece = partial.shape[0] // n_col
    shape = jax.ShapeDtypeStruct
    sizes = [3, n_col, n_col, n_row, n_row, n_col, n_col, n_col, n_col, n_row, n_row]
    return pl.pallas_call(
        functools.partial(exchange_kernel, n_row, n_col),
        out_shape=[shape(out_first.shape, jnp.float32), shape(out_second.shape, jnp.float32),
                   shape(partial.shape, jnp.float32)],
        in_specs=[any_space, any_space, vmem],
        out_specs=[any_space] * 3,
        scratch_shapes=[
            pltpu.VMEM((n_col, piece, 128), jnp.float32),
            pltpu.VMEM((n_row, piece, 128), jnp.float32),
            pltpu.VMEM((piece, 128), jnp.float32),
            pltpu.VMEM((piece, 128), jnp.float32),
        ] + [dma((size,)) for size in sizes],
        compiler_params=pltpu.CompilerParams(collective_id=2, has_side_effects=True),
        name="exchange",
    )(out_first, out_second, partial)


def shards(density, coords, basis, transfer, parent, near_pairs, near_count, far_pairs, coupling):
    highest = lax.Precision.HIGHEST
    per_device, _, panels = density.shape
    rank = basis.shape[1]
    n_row, n_col = lax.axis_size("row"), lax.axis_size("col")
    row, col = lax.axis_index("row"), lax.axis_index("col")
    row_span = per_device * n_col
    row_base = row * row_span
    own_base = row_base + col * per_device
    slots = near_pairs.shape[1]
    parent_total = parent.shape[0] // 4

    tile = jnp.concatenate(
        [density, coords, jnp.ones((per_device, 1, panels), density.dtype),
         jnp.zeros((per_device, 1, panels), density.dtype)], axis=1).reshape(per_device * 8, panels)
    ids = jnp.pad(near_pairs, ((0, 6), (0, 0)))
    flattened = density.reshape(per_device, 3 * panels)
    moments = jnp.einsum("crk,ck->cr", basis, flattened, preferred_element_type=jnp.float32)
    lifted = jnp.einsum("crs,cs->cr", transfer, moments, precision=highest)
    row_tiles, col_tiles, row_ids, col_ids, all_lifted = gather(
        n_row, n_col, tile, ids, lifted.reshape(-1, 128))

    glob_a, glob_b = near_pairs[0], near_pairs[1]
    live = jnp.concatenate([near_count, (glob_a != glob_b).astype(jnp.int32)])
    out_first, out_second = near(
        glob_a - row_base, glob_b // row_span * per_device + glob_b % per_device, live, row_tiles, col_tiles)

    all_lifted = all_lifted.reshape(-1, rank)
    parents = jnp.arange(parent_total, dtype=jnp.int32)
    to_parent = (parents[:, None] == parent[None, :]).astype(jnp.float32)
    parent_moments = jnp.dot(to_parent, all_lifted, precision=highest)
    pick = (far_pairs[:, :, None] == parents).astype(jnp.float32)
    sources = jnp.einsum("dkp,ps->dks", pick, parent_moments, precision=highest)
    to_first = jnp.einsum("krs,ks->kr", coupling, sources[1], precision=highest)
    to_second = jnp.einsum("ksr,ks->kr", coupling, sources[0], precision=highest)
    own_locals = jnp.einsum("dkp,dkr->pr", pick, jnp.stack([to_first, to_second]), precision=highest)

    got_first, got_second, parent_locals = exchange(
        n_row, n_col, out_first, out_second, own_locals.reshape(-1, 128))
    parent_locals = parent_locals.reshape(parent_total, rank)

    own_parent = lax.dynamic_slice_in_dim(parent, own_base, per_device)
    own_pick = (own_parent[:, None] == parents).astype(jnp.float32)
    own_parts = jnp.dot(own_pick, parent_locals, precision=highest)
    local_coef = jnp.einsum("csr,cs->cr", transfer, own_parts, precision=highest)
    far_part = jnp.einsum("crk,cr->ck", basis.astype(jnp.float32), local_coef, precision=highest)

    ca, cb = slots // n_col, slots // n_row
    firsts = lax.dynamic_slice_in_dim(row_ids.reshape(n_col, 8, slots)[:, 0], col * ca, ca, axis=1)
    seconds = lax.dynamic_slice_in_dim(col_ids.reshape(n_row, 8, slots)[:, 1], row * cb, cb, axis=1)
    owners = jnp.concatenate([firsts.reshape(-1), seconds.reshape(-1)]) - own_base
    place = (jnp.arange(per_device, dtype=jnp.int32)[:, None] == owners).astype(jnp.float32)
    near_part = (jnp.dot(place[:, :slots], got_first, precision=highest)
                 + jnp.dot(place[:, slots:], got_second, precision=highest))
    return (near_part + far_part).reshape(per_device, 3, panels)


def solution(mesh):
    placed = (
        P(("row", "col"), None, None),
        P(("row", "col"), None, None),
        P(("row", "col"), None, None),
        P(("row", "col"), None, None),
        P(),
        P(None, ("row", "col")),
        P(("row", "col")),
        P(None, ("row", "col")),
        P(("row", "col"), None, None),
    )
    return jax.shard_map(
        shards, mesh=mesh, in_specs=placed, out_specs=P(("row", "col"), None, None), check_vma=False
    )
```

```python
import functools
import math

import jax
import jax.numpy as jnp
from jax import lax
from jax.experimental import pallas as pl
from jax.experimental.pallas import tpu as pltpu
from jax.sharding import PartitionSpec as P

REG_EPS = 0.02
STOKES_SCALE = 1.0 / (8.0 * math.pi)
MESH = pl.DeviceIdType.MESH
GROUP = 4
CHUNK = 16


def greet(n_row, n_col, row, col):
    barrier = pltpu.get_barrier_semaphore()
    for k in range(1, n_col):
        pl.semaphore_signal(barrier, inc=1, device_id=(row, lax.rem(col + k, n_col)), device_id_type=MESH)
    for k in range(1, n_row):
        pl.semaphore_signal(barrier, inc=1, device_id=(lax.rem(row + k, n_row), col), device_id_type=MESH)
    pl.semaphore_wait(barrier, n_col + n_row - 2)


def part(ref, index, size):
    return ref.at[pl.ds(pl.multiple_of(index * size, size), size)]


def gather_kernel(n_row, n_col, n_z, tile, ids, lifted, row_tiles, col_tiles, row_ids, col_ids, all_lifted,
                  own_sem, st, rt, sct, rct, si, ri, sci, rci, sl, rl, scl, rcl):
    row, col = lax.axis_index("row"), lax.axis_index("col")
    n_y = n_col // n_z
    z, y = col // n_y, lax.rem(col, n_y)
    rows, id_rows, lift_rows = tile.shape[0], ids.shape[0], lifted.shape[0]
    span = n_col * lift_rows
    own = [
        pltpu.make_async_copy(tile, part(row_tiles, col, rows), own_sem.at[0]),
        pltpu.make_async_copy(tile, part(col_tiles, row, rows), own_sem.at[1]),
        pltpu.make_async_copy(ids, part(row_ids, col, id_rows), own_sem.at[2]),
        pltpu.make_async_copy(ids, part(col_ids, row, id_rows), own_sem.at[3]),
        pltpu.make_async_copy(lifted, part(all_lifted, row * n_col + col, lift_rows), own_sem.at[4]),
    ]
    for copy in own:
        copy.start()
    greet(n_row, n_col, row, col)

    def to_col(src, dst, index, size, sends, recvs, slot, peer):
        return pltpu.make_async_remote_copy(
            src_ref=src, dst_ref=part(dst, index, size), send_sem=sends.at[slot], recv_sem=recvs.at[index],
            device_id=(row, peer), device_id_type=MESH)

    def to_row(src, dst_view, sends, recvs, peer):
        return pltpu.make_async_remote_copy(
            src_ref=src, dst_ref=dst_view, send_sem=sends.at[peer], recv_sem=recvs.at[row],
            device_id=(peer, col), device_id_type=MESH)

    started = []

    def go(copy):
        copy.start()
        started.append(copy)

    for k in range(1, n_col):
        peer = lax.rem(col + k, n_col)
        go(pltpu.make_async_remote_copy(
            src_ref=lifted, dst_ref=part(all_lifted, row * n_col + col, lift_rows),
            send_sem=sl.at[peer], recv_sem=rl.at[col], device_id=(row, peer), device_id_type=MESH))
    for k in range(1, n_z):
        peer = lax.rem(z + k, n_z) * n_y + y
        go(to_col(tile, row_tiles, col, rows, st, rt, k, peer))
    for k in range(1, n_y):
        peer = z * n_y + lax.rem(y + k, n_y)
        go(to_col(tile, row_tiles, col, rows, st, rt, n_z + k, peer))
    for k in range(1, n_row):
        peer = lax.rem(row + k, n_row)
        go(to_row(tile, part(col_tiles, row, rows), sct, rct, peer))
        go(to_row(ids, part(col_ids, row, id_rows), sci, rci, peer))
    for k in range(1, n_col):
        peer = lax.rem(col + k, n_col)
        go(to_col(ids, row_ids, col, id_rows, si, ri, peer, peer))

    own[4].wait()
    for k in range(1, n_col):
        src = lax.rem(col + k, n_col)
        pltpu.make_async_copy(lifted, part(all_lifted, row * n_col + src, lift_rows), rl.at[src]).wait()
    for k in range(1, n_row):
        peer = lax.rem(row + k, n_row)
        mine = part(all_lifted, row, span)
        go(to_row(mine, mine, scl, rcl, peer))

    for k in range(1, n_z):
        src = lax.rem(z + k, n_z) * n_y + y
        pltpu.make_async_copy(tile, part(row_tiles, src, rows), rt.at[src]).wait()
        for j in range(1, n_y):
            peer = z * n_y + lax.rem(y + j, n_y)
            go(to_col(part(row_tiles, src, rows), row_tiles, src, rows, st, rt, n_z + n_y * k + j, peer))
    for j in range(1, n_y):
        for k in range(n_z):
            src = lax.rem(z + k, n_z) * n_y + lax.rem(y + j, n_y)
            pltpu.make_async_copy(tile, part(row_tiles, src, rows), rt.at[src]).wait()
    for k in range(1, n_col):
        src = lax.rem(col + k, n_col)
        pltpu.make_async_copy(ids, part(row_ids, src, id_rows), ri.at[src]).wait()
    for k in range(1, n_row):
        src = lax.rem(row + k, n_row)
        pltpu.make_async_copy(tile, part(col_tiles, src, rows), rct.at[src]).wait()
        pltpu.make_async_copy(ids, part(col_ids, src, id_rows), rci.at[src]).wait()
        view = part(all_lifted, src, span)
        pltpu.make_async_copy(view, view, rcl.at[src]).wait()
    for copy in own[:4]:
        copy.wait()
    for copy in started:
        copy.wait_send()


def gather(n_row, n_col, tile, ids, lifted):
    n_z = 4 if n_col % 4 == 0 else 1
    any_space = pl.BlockSpec(memory_space=pl.ANY)
    dma = pltpu.SemaphoreType.DMA
    sizes = [(5,), (n_z * (n_col // n_z + 1) + n_col,), (n_col,), (n_row,), (n_row,), (n_col,), (n_col,),
             (n_row,), (n_row,), (n_col,), (n_col,), (n_row,), (n_row,)]
    shape = jax.ShapeDtypeStruct
    return pl.pallas_call(
        functools.partial(gather_kernel, n_row, n_col, n_z),
        out_shape=[
            shape((n_col * tile.shape[0], tile.shape[1]), tile.dtype),
            shape((n_row * tile.shape[0], tile.shape[1]), tile.dtype),
            shape((n_col * ids.shape[0], ids.shape[1]), ids.dtype),
            shape((n_row * ids.shape[0], ids.shape[1]), ids.dtype),
            shape((n_row * n_col * lifted.shape[0], lifted.shape[1]), lifted.dtype),
        ],
        in_specs=[any_space] * 3,
        out_specs=[any_space] * 5,
        scratch_shapes=[dma(size) for size in sizes],
        compiler_params=pltpu.CompilerParams(collective_id=1, has_side_effects=True),
        name="gather",
    )(tile, ids, lifted)


def near_kernel(first, second, live, row_tiles, col_tiles, out_first, out_second, row_wide, col_wide, radius_sq, inv, cube):
    block = 256
    for narrow, wide in ((row_tiles, row_wide), (col_tiles, col_wide)):
        @pl.loop(0, narrow.shape[0] // block)
        def _(step):
            at = pl.ds(pl.multiple_of(step * block, block), block)
            wide[at, :] = narrow[at, :].astype(jnp.float32)

    out_first[...] = jnp.zeros_like(out_first)
    out_second[...] = jnp.zeros_like(out_second)
    panels = row_tiles.shape[1]
    count = live[0]
    eps_sq = REG_EPS * REG_EPS
    across = (((1,), (1,)), ((), ()))
    down = (((1,), (0,)), ((), ()))

    sub = lax.broadcasted_iota(jnp.int32, (8, panels), 0)
    ones = jnp.ones((1, panels), jnp.float32)

    def split(wide):
        terms = []
        for _ in range(2):
            term = wide.astype(jnp.bfloat16).astype(jnp.float32)
            terms.append(term)
            wide = wide - term
        return terms + [wide]

    def prepare(tile):
        products = [tile * tile[3 + i:4 + i, :] for i in range(3)]
        y_f = products[0][0:1] + products[1][1:2] + products[2][2:3]
        y_y = products[0][3:4] + products[1][4:5] + products[2][5:6]
        blocks = [tile]
        for product in products:
            high = product.astype(jnp.bfloat16).astype(jnp.float32)
            blocks += [high, product - high]
        blocks += split(tile * y_f)
        return jnp.concatenate(blocks, axis=0).astype(jnp.bfloat16), y_y

    def distances(ta, tb, xx, yy, u):
        x_high, x_mid, x_low = split(xx)
        y_high, y_mid, y_low = split(yy + eps_sq)
        left0 = jnp.where(sub == 0, x_high, jnp.where(sub == 1, x_mid, jnp.where(sub == 2, x_low, jnp.where(
            sub < 6, -2.0 * ta, ta))))
        right0 = jnp.where(sub < 3, ones, jnp.where(sub == 6, y_high, tb))
        left1 = jnp.where(sub < 2, ones, 0.0)
        right1 = jnp.where(sub == 0, y_mid, jnp.where(sub == 1, y_low, 0.0))
        left = jnp.concatenate([left0, left1], axis=0).T.astype(jnp.bfloat16)
        right = jnp.concatenate([right0, right1], axis=0).astype(jnp.bfloat16)
        radius_sq[u] = jnp.dot(left, right, preferred_element_type=jnp.float32)

    def combine(near_inv, near_cube, tile):
        x = tile[3:6]
        s = near_cube[0:3]
        value = near_inv[0:3] + eps_sq * s
        last = near_cube[56:64] + near_cube[64:72] + near_cube[72:80]
        dotted = jnp.sum(x * s, axis=0, keepdims=True) - last[6:7]
        value = value + (x * dotted + last[3:6])
        cross = [jnp.sum(x * (near_cube[8 + 16 * i:11 + 16 * i] + near_cube[16 + 16 * i:19 + 16 * i]), axis=0,
                         keepdims=True) for i in range(3)]
        return [(value[i:i + 1] - cross[i]) * STOKES_SCALE for i in range(3)]

    def begin(slot, u):
        ta = row_wide[pl.ds(pl.multiple_of(first[slot] * 8, 8), 8), :]
        tb = col_wide[pl.ds(pl.multiple_of(second[slot] * 8, 8), 8), :]
        ra, xx = prepare(ta)
        rb, yy = prepare(tb)
        distances(ta, tb, xx, yy, u)
        return ta, tb, ra, rb

    def finish(slot, u, ta, tb, ra, rb):
        for chunk in range(panels // CHUNK):
            at = slice(chunk * CHUNK, (chunk + 1) * CHUNK)
            inv_dist = lax.rsqrt(radius_sq[u, at, :])
            inv[u, at, :] = inv_dist.astype(jnp.bfloat16)
            cube[u, at, :] = (inv_dist * inv_dist * inv_dist).astype(jnp.bfloat16)
        product = functools.partial(lax.dot_general, preferred_element_type=jnp.float32)
        to_first = combine(product(rb[0:16], inv[u], across), product(rb, cube[u], across), ta)
        to_second = combine(product(ra[0:16], inv[u], down), product(ra, cube[u], down), tb)
        within = slot < count
        keep_second = within & (live[1 + slot] != 0)
        for i in range(3):
            at = slice(i * panels, (i + 1) * panels)
            out_first[pl.ds(slot, 1), at] = jnp.where(within, to_first[i], 0.0)
            out_second[pl.ds(slot, 1), at] = jnp.where(keep_second, to_second[i], 0.0)

    def group(step, carry):
        held = begin(step * GROUP, 0)
        for u in range(GROUP):
            ahead = begin(step * GROUP + u + 1, u + 1) if u + 1 < GROUP else None
            finish(step * GROUP + u, u, *held)
            held = ahead
        return carry

    lax.fori_loop(0, (count + GROUP - 1) // GROUP, group, 0)


def near(first, second, live, row_tiles, col_tiles):
    slots, panels = first.shape[0], row_tiles.shape[1]
    smem = pl.BlockSpec(memory_space=pltpu.SMEM)
    vmem = pl.BlockSpec(memory_space=pltpu.VMEM)
    return pl.pallas_call(
        near_kernel,
        out_shape=[jax.ShapeDtypeStruct((slots, 3 * panels), jnp.float32)] * 2,
        in_specs=[smem, smem, smem, vmem, vmem],
        out_specs=[vmem, vmem],
        scratch_shapes=[
            pltpu.VMEM(row_tiles.shape, jnp.float32),
            pltpu.VMEM(col_tiles.shape, jnp.float32),
            pltpu.VMEM((GROUP, panels, panels), jnp.float32),
        ] + [pltpu.VMEM((GROUP, panels, panels), jnp.bfloat16)] * 2,
        compiler_params=pltpu.CompilerParams(vmem_limit_bytes=48 * 1024 * 1024),
        name="near",
    )(first, second, live, row_tiles, col_tiles)


def exchange_kernel(n_row, n_col, out_first, out_second, partial, got_first, got_second, total, f1, f2, acc, red,
                    own_sem, s1, r1, s2, r2, s3, r3, sa, ra, sb, rb):
    row, col = lax.axis_index("row"), lax.axis_index("col")
    ca, cb = out_first.shape[0] // n_col, out_second.shape[0] // n_row
    piece = partial.shape[0] // n_col
    own = [
        pltpu.make_async_copy(part(out_first, col, ca), part(got_first, col, ca), own_sem.at[0]),
        pltpu.make_async_copy(part(out_second, row, cb), part(got_second, row, cb), own_sem.at[1]),
    ]
    for copy in own:
        copy.start()
    f1[pl.ds(col, 1)] = partial[pl.ds(pl.multiple_of(col * piece, piece), piece), :][None]
    greet(n_row, n_col, row, col)
    started = []

    def send(src, dst, sends, recvs, slot, mine, device):
        copy = pltpu.make_async_remote_copy(
            src_ref=src, dst_ref=dst, send_sem=sends.at[slot], recv_sem=recvs.at[mine],
            device_id=device, device_id_type=MESH)
        copy.start()
        started.append(copy)

    for k in range(1, n_col):
        peer = lax.rem(col + k, n_col)
        send(part(partial, peer, piece), f1.at[col], s1, r1, peer, col, (row, peer))
    for k in range(1, n_col):
        peer = lax.rem(col + k, n_col)
        send(part(out_first, peer, ca), part(got_first, col, ca), sa, ra, peer, col, (row, peer))
    for k in range(1, n_row):
        peer = lax.rem(row + k, n_row)
        send(part(out_second, peer, cb), part(got_second, row, cb), sb, rb, peer, row, (peer, col))

    for k in range(1, n_col):
        src = lax.rem(col + k, n_col)
        pltpu.make_async_copy(f1.at[src], f1.at[src], r1.at[src]).wait()
    acc[...] = jnp.sum(f1[...], axis=0)
    f2[pl.ds(row, 1)] = acc[...][None]
    for k in range(1, n_row):
        peer = lax.rem(row + k, n_row)
        send(acc, f2.at[row], s2, r2, peer, row, (peer, col))
    for k in range(1, n_row):
        src = lax.rem(row + k, n_row)
        pltpu.make_async_copy(f2.at[src], f2.at[src], r2.at[src]).wait()
    red[...] = jnp.sum(f2[...], axis=0)
    keep = pltpu.make_async_copy(red, part(total, col, piece), own_sem.at[2])
    keep.start()
    for k in range(1, n_col):
        peer = lax.rem(col + k, n_col)
        send(red, part(total, col, piece), s3, r3, peer, col, (row, peer))
    for k in range(1, n_col):
        src = lax.rem(col + k, n_col)
        pltpu.make_async_copy(red, part(total, src, piece), r3.at[src]).wait()
        view = part(got_first, src, ca)
        pltpu.make_async_copy(view, view, ra.at[src]).wait()
    for k in range(1, n_row):
        src = lax.rem(row + k, n_row)
        view = part(got_second, src, cb)
        pltpu.make_async_copy(view, view, rb.at[src]).wait()
    keep.wait()
    for copy in own:
        copy.wait()
    for copy in started:
        copy.wait_send()


def exchange(n_row, n_col, out_first, out_second, partial):
    any_space = pl.BlockSpec(memory_space=pl.ANY)
    vmem = pl.BlockSpec(memory_space=pltpu.VMEM)
    dma = pltpu.SemaphoreType.DMA
    piece = partial.shape[0] // n_col
    shape = jax.ShapeDtypeStruct
    sizes = [3, n_col, n_col, n_row, n_row, n_col, n_col, n_col, n_col, n_row, n_row]
    return pl.pallas_call(
        functools.partial(exchange_kernel, n_row, n_col),
        out_shape=[shape(out_first.shape, jnp.float32), shape(out_second.shape, jnp.float32),
                   shape(partial.shape, jnp.float32)],
        in_specs=[any_space, any_space, vmem],
        out_specs=[any_space] * 3,
        scratch_shapes=[
            pltpu.VMEM((n_col, piece, 128), jnp.float32),
            pltpu.VMEM((n_row, piece, 128), jnp.float32),
            pltpu.VMEM((piece, 128), jnp.float32),
            pltpu.VMEM((piece, 128), jnp.float32),
        ] + [dma((size,)) for size in sizes],
        compiler_params=pltpu.CompilerParams(collective_id=2, has_side_effects=True),
        name="exchange",
    )(out_first, out_second, partial)


def shards(density, coords, basis, transfer, parent, near_pairs, near_count, far_pairs, coupling):
    highest = lax.Precision.HIGHEST
    per_device, _, panels = density.shape
    rank = basis.shape[1]
    n_row, n_col = lax.axis_size("row"), lax.axis_size("col")
    row, col = lax.axis_index("row"), lax.axis_index("col")
    row_span = per_device * n_col
    row_base = row * row_span
    own_base = row_base + col * per_device
    slots = near_pairs.shape[1]
    parent_total = parent.shape[0] // 4

    tile = jnp.concatenate(
        [density, coords, jnp.ones((per_device, 1, panels), density.dtype),
         jnp.zeros((per_device, 1, panels), density.dtype)], axis=1).reshape(per_device * 8, panels)
    ids = jnp.pad(near_pairs, ((0, 6), (0, 0)))
    flattened = density.reshape(per_device, 3 * panels)
    moments = jnp.einsum("crk,ck->cr", basis, flattened, preferred_element_type=jnp.float32)
    lifted = jnp.einsum("crs,cs->cr", transfer, moments, precision=highest)
    row_tiles, col_tiles, row_ids, col_ids, all_lifted = gather(
        n_row, n_col, tile, ids, lifted.reshape(-1, 128))

    glob_a, glob_b = near_pairs[0], near_pairs[1]
    live = jnp.concatenate([near_count, (glob_a != glob_b).astype(jnp.int32)])
    out_first, out_second = near(
        glob_a - row_base, glob_b // row_span * per_device + glob_b % per_device, live, row_tiles, col_tiles)

    all_lifted = all_lifted.reshape(-1, rank)
    parents = jnp.arange(parent_total, dtype=jnp.int32)
    to_parent = (parents[:, None] == parent[None, :]).astype(jnp.float32)
    parent_moments = jnp.dot(to_parent, all_lifted, precision=highest)
    pick = (far_pairs[:, :, None] == parents).astype(jnp.float32)
    sources = jnp.einsum("dkp,ps->dks", pick, parent_moments, precision=highest)
    to_first = jnp.einsum("krs,ks->kr", coupling, sources[1], precision=highest)
    to_second = jnp.einsum("ksr,ks->kr", coupling, sources[0], precision=highest)
    own_locals = jnp.einsum("dkp,dkr->pr", pick, jnp.stack([to_first, to_second]), precision=highest)

    got_first, got_second, parent_locals = exchange(
        n_row, n_col, out_first, out_second, own_locals.reshape(-1, 128))
    parent_locals = parent_locals.reshape(parent_total, rank)

    own_parent = lax.dynamic_slice_in_dim(parent, own_base, per_device)
    own_pick = (own_parent[:, None] == parents).astype(jnp.float32)
    own_parts = jnp.dot(own_pick, parent_locals, precision=highest)
    local_coef = jnp.einsum("csr,cs->cr", transfer, own_parts, precision=highest)
    far_part = jnp.einsum("crk,cr->ck", basis.astype(jnp.float32), local_coef, precision=highest)

    ca, cb = slots // n_col, slots // n_row
    firsts = lax.dynamic_slice_in_dim(row_ids.reshape(n_col, 8, slots)[:, 0], col * ca, ca, axis=1)
    seconds = lax.dynamic_slice_in_dim(col_ids.reshape(n_row, 8, slots)[:, 1], row * cb, cb, axis=1)
    owners = jnp.concatenate([firsts.reshape(-1), seconds.reshape(-1)]) - own_base
    place = (jnp.arange(per_device, dtype=jnp.int32)[:, None] == owners).astype(jnp.float32)
    near_part = (jnp.dot(place[:, :slots], got_first, precision=highest)
                 + jnp.dot(place[:, slots:], got_second, precision=highest))
    return (near_part + far_part).reshape(per_device, 3, panels)


def solution(mesh):
    placed = (
        P(("row", "col"), None, None),
        P(("row", "col"), None, None),
        P(("row", "col"), None, None),
        P(("row", "col"), None, None),
        P(),
        P(None, ("row", "col")),
        P(("row", "col")),
        P(None, ("row", "col")),
        P(("row", "col"), None, None),
    )
    return jax.shard_map(
        shards, mesh=mesh, in_specs=placed, out_specs=P(("row", "col"), None, None), check_vma=False
    )
```

```python
import functools
import math

import jax
import jax.numpy as jnp
from jax import lax
from jax.experimental import pallas as pl
from jax.experimental.pallas import tpu as pltpu
from jax.sharding import PartitionSpec as P

REG_EPS = 0.02
STOKES_SCALE = 1.0 / (8.0 * math.pi)
MESH = pl.DeviceIdType.MESH
GROUP = 4
CHUNK = 16


def greet(n_row, n_col, row, col):
    barrier = pltpu.get_barrier_semaphore()
    for k in range(1, n_col):
        pl.semaphore_signal(barrier, inc=1, device_id=(row, lax.rem(col + k, n_col)), device_id_type=MESH)
    for k in range(1, n_row):
        pl.semaphore_signal(barrier, inc=1, device_id=(lax.rem(row + k, n_row), col), device_id_type=MESH)
    pl.semaphore_wait(barrier, n_col + n_row - 2)


def part(ref, index, size):
    return ref.at[pl.ds(pl.multiple_of(index * size, size), size)]


def gather_kernel(n_row, n_col, n_z, tile, ids, lifted, row_tiles, col_tiles, row_ids, col_ids, all_lifted,
                  own_sem, st, rt, sct, rct, si, ri, sci, rci, sl, rl, scl, rcl):
    row, col = lax.axis_index("row"), lax.axis_index("col")
    n_y = n_col // n_z
    z, y = col // n_y, lax.rem(col, n_y)
    rows, lift_rows = tile.shape[0], lifted.shape[0]
    span = n_col * lift_rows
    own = [
        pltpu.make_async_copy(tile, part(row_tiles, col, rows), own_sem.at[0]),
        pltpu.make_async_copy(tile, part(col_tiles, row, rows), own_sem.at[1]),
        pltpu.make_async_copy(ids, row_ids.at[col], own_sem.at[2]),
        pltpu.make_async_copy(ids, col_ids.at[row], own_sem.at[3]),
        pltpu.make_async_copy(lifted, part(all_lifted, row * n_col + col, lift_rows), own_sem.at[4]),
    ]
    for copy in own:
        copy.start()
    greet(n_row, n_col, row, col)

    def to_col(src, dst, index, size, sends, recvs, slot, peer):
        return pltpu.make_async_remote_copy(
            src_ref=src, dst_ref=part(dst, index, size), send_sem=sends.at[slot], recv_sem=recvs.at[index],
            device_id=(row, peer), device_id_type=MESH)

    def to_row(src, dst_view, sends, recvs, peer):
        return pltpu.make_async_remote_copy(
            src_ref=src, dst_ref=dst_view, send_sem=sends.at[peer], recv_sem=recvs.at[row],
            device_id=(peer, col), device_id_type=MESH)

    started = []

    def go(copy):
        copy.start()
        started.append(copy)

    for k in range(1, n_col):
        peer = lax.rem(col + k, n_col)
        go(pltpu.make_async_remote_copy(
            src_ref=lifted, dst_ref=part(all_lifted, row * n_col + col, lift_rows),
            send_sem=sl.at[peer], recv_sem=rl.at[col], device_id=(row, peer), device_id_type=MESH))
    for k in range(1, n_z):
        peer = lax.rem(z + k, n_z) * n_y + y
        go(to_col(tile, row_tiles, col, rows, st, rt, k, peer))
    for k in range(1, n_y):
        peer = z * n_y + lax.rem(y + k, n_y)
        go(to_col(tile, row_tiles, col, rows, st, rt, n_z + k, peer))
    for k in range(1, n_row):
        peer = lax.rem(row + k, n_row)
        go(to_row(tile, part(col_tiles, row, rows), sct, rct, peer))
        go(to_row(ids, col_ids.at[row], sci, rci, peer))
    for k in range(1, n_col):
        peer = lax.rem(col + k, n_col)
        go(pltpu.make_async_remote_copy(
            src_ref=ids, dst_ref=row_ids.at[col], send_sem=si.at[peer], recv_sem=ri.at[col],
            device_id=(row, peer), device_id_type=MESH))

    own[4].wait()
    for k in range(1, n_col):
        src = lax.rem(col + k, n_col)
        pltpu.make_async_copy(lifted, part(all_lifted, row * n_col + src, lift_rows), rl.at[src]).wait()
    for k in range(1, n_row):
        peer = lax.rem(row + k, n_row)
        mine = part(all_lifted, row, span)
        go(to_row(mine, mine, scl, rcl, peer))

    for k in range(1, n_z):
        src = lax.rem(z + k, n_z) * n_y + y
        pltpu.make_async_copy(tile, part(row_tiles, src, rows), rt.at[src]).wait()
        for j in range(1, n_y):
            peer = z * n_y + lax.rem(y + j, n_y)
            go(to_col(part(row_tiles, src, rows), row_tiles, src, rows, st, rt, n_z + n_y * k + j, peer))
    for j in range(1, n_y):
        for k in range(n_z):
            src = lax.rem(z + k, n_z) * n_y + lax.rem(y + j, n_y)
            pltpu.make_async_copy(tile, part(row_tiles, src, rows), rt.at[src]).wait()
    for k in range(1, n_col):
        src = lax.rem(col + k, n_col)
        pltpu.make_async_copy(ids, row_ids.at[src], ri.at[src]).wait()
    for k in range(1, n_row):
        src = lax.rem(row + k, n_row)
        pltpu.make_async_copy(tile, part(col_tiles, src, rows), rct.at[src]).wait()
        pltpu.make_async_copy(ids, col_ids.at[src], rci.at[src]).wait()
        view = part(all_lifted, src, span)
        pltpu.make_async_copy(view, view, rcl.at[src]).wait()
    for copy in own[:4]:
        copy.wait()
    for copy in started:
        copy.wait_send()


def gather(n_row, n_col, tile, ids, lifted):
    n_z = 4 if n_col % 4 == 0 else 1
    any_space = pl.BlockSpec(memory_space=pl.ANY)
    dma = pltpu.SemaphoreType.DMA
    sizes = [(5,), (n_z * (n_col // n_z + 1) + n_col,), (n_col,), (n_row,), (n_row,), (n_col,), (n_col,),
             (n_row,), (n_row,), (n_col,), (n_col,), (n_row,), (n_row,)]
    shape = jax.ShapeDtypeStruct
    return pl.pallas_call(
        functools.partial(gather_kernel, n_row, n_col, n_z),
        out_shape=[
            shape((n_col * tile.shape[0], tile.shape[1]), tile.dtype),
            shape((n_row * tile.shape[0], tile.shape[1]), tile.dtype),
            shape((n_col,) + ids.shape, ids.dtype),
            shape((n_row,) + ids.shape, ids.dtype),
            shape((n_row * n_col * lifted.shape[0], lifted.shape[1]), lifted.dtype),
        ],
        in_specs=[any_space] * 3,
        out_specs=[any_space] * 5,
        scratch_shapes=[dma(size) for size in sizes],
        compiler_params=pltpu.CompilerParams(collective_id=1, has_side_effects=True),
        name="gather",
    )(tile, ids, lifted)


def split(wide, terms=3):
    out = []
    for _ in range(terms - 1):
        term = wide.astype(jnp.bfloat16).astype(jnp.float32)
        out.append(term)
        wide = wide - term
    return out + [wide]


def select_rows(one_hot, wide):
    return sum(jnp.dot(one_hot, term.astype(jnp.bfloat16), preferred_element_type=jnp.float32)
               for term in split(wide))


def as_one_hot(where_true):
    return jnp.where(where_true, 1.0, 0.0).astype(jnp.bfloat16)


def couple(far, coupling, parents, all_lifted, lifted, moved, own_locals):
    total, rank = own_locals.shape
    pairs = far.shape[1]
    for u in range(4):
        lifted[pl.ds(u, all_lifted.shape[0], stride=4), :] = pltpu.roll(all_lifted[...], (4 - u) % 4 * rank, 1)
    parent_row = lax.broadcasted_iota(jnp.int32, (total, 1), 0)
    moments = select_rows(as_one_hot(parent_row == parents[...]), lifted[:, :rank])
    lane = lax.broadcasted_iota(jnp.int32, (pairs, total), 1).astype(jnp.float32)
    sources = []
    for side in range(2):
        column = jnp.broadcast_to(far[side:side + 1, :].astype(jnp.float32), (8, pairs)).T[:, 0:1]
        sources.append(select_rows(as_one_hot(lane == column), moments))
    turned = sources[0].T
    pair_lane = lax.broadcasted_iota(jnp.int32, (rank, pairs), 1)
    to_first = jnp.zeros((rank, pairs), jnp.float32)
    for k in range(pairs):
        block = coupling[k]
        to_first = jnp.where(pair_lane == k, jnp.sum(block * sources[1][k:k + 1], axis=1, keepdims=True), to_first)
        moved[k:k + 1, :] = jnp.sum(block * turned[:, k:k + 1], axis=0, keepdims=True)
    own_locals[...] = (select_rows(as_one_hot(parent_row == far[0:1, :]), to_first.T)
                       + select_rows(as_one_hot(parent_row == far[1:2, :]), moved[...]))


def placement(row_ids, col_ids, place):
    per_device, slots = place.shape[0], row_ids.shape[2]
    n_row, n_col = col_ids.shape[0], row_ids.shape[0]
    row, col = lax.axis_index("row"), lax.axis_index("col")
    base = (row * n_col + col) * per_device
    lane = lax.broadcasted_iota(jnp.int32, (8, slots), 1)
    cluster = lax.broadcasted_iota(jnp.int32, (per_device, slots), 0) + base
    for ids, side, sources, mine, start in ((row_ids, 0, n_col, col, 0), (col_ids, 1, n_row, row, slots)):
        size = slots // sources
        owners = jnp.zeros((8, slots), jnp.int32)
        for src in range(sources):
            from_src = jnp.broadcast_to(ids[src, side:side + 1, :], (8, slots))
            shift = lax.rem((src - mine) * size + slots, slots)
            owners = jnp.where(lane // size == src, pltpu.roll(from_src, shift, 1), owners)
        place[:, start:start + slots] = as_one_hot(cluster == owners[0:1, :])


def near_kernel(per_device, pairs, live, row_tiles, col_tiles, far, coupling, parents, all_lifted, row_ids, col_ids,
                out_first, out_second, own_locals, place, row_wide, col_wide, lifted, moved, radius_sq, inv, cube):
    for narrow, wide in ((row_tiles, row_wide), (col_tiles, col_wide)):
        for src in range(narrow.shape[0] // (6 * per_device)):
            for i in range(8):
                if i < 6:
                    start = (src * 6 + i) * per_device
                    rows = narrow[start:start + per_device, :].astype(jnp.float32)
                else:
                    rows = jnp.full((per_device, narrow.shape[1]), 7.0 - i, jnp.float32)
                for half in range(2):
                    at = pl.ds(src * per_device * 8 + i, per_device, stride=8)
                    wide[half, at, :] = rows[:, half * 128:(half + 1) * 128]

    couple(far, coupling, parents, all_lifted, lifted, moved, own_locals)
    placement(row_ids, col_ids, place)
    row_span = per_device * row_ids.shape[0]
    row_base = lax.axis_index("row") * row_span
    out_first[...] = jnp.zeros_like(out_first)
    out_second[...] = jnp.zeros_like(out_second)
    panels = row_tiles.shape[1]
    count = live[0]
    eps_sq = REG_EPS * REG_EPS
    across = (((1,), (1,)), ((), ()))
    down = (((1,), (0,)), ((), ()))

    sub = lax.broadcasted_iota(jnp.int32, (8, panels), 0)
    ones = jnp.ones((1, panels), jnp.float32)

    def prepare(tile):
        products = [tile * tile[3 + i:4 + i, :] for i in range(3)]
        y_f = products[0][0:1] + products[1][1:2] + products[2][2:3]
        y_y = products[0][3:4] + products[1][4:5] + products[2][5:6]
        blocks = [tile]
        for product in products:
            high = product.astype(jnp.bfloat16).astype(jnp.float32)
            blocks += [high, product - high]
        blocks += split(tile * y_f)
        return jnp.concatenate(blocks, axis=0).astype(jnp.bfloat16), y_y

    def distances(ta, tb, xx, yy, u):
        x_high, x_mid, x_low = split(xx)
        y_high, y_mid, y_low = split(yy + eps_sq)
        left0 = jnp.where(sub == 0, x_high, jnp.where(sub == 1, x_mid, jnp.where(sub == 2, x_low, jnp.where(
            sub < 6, -2.0 * ta, ta))))
        right0 = jnp.where(sub < 3, ones, jnp.where(sub == 6, y_high, tb))
        left1 = jnp.where(sub < 2, ones, 0.0)
        right1 = jnp.where(sub == 0, y_mid, jnp.where(sub == 1, y_low, 0.0))
        left = jnp.concatenate([left0, left1], axis=0).T.astype(jnp.bfloat16)
        right = jnp.concatenate([right0, right1], axis=0).astype(jnp.bfloat16)
        radius_sq[u] = jnp.dot(left, right, preferred_element_type=jnp.float32)

    def combine(near_inv, near_cube, tile):
        x = tile[3:6]
        s = near_cube[0:3]
        value = near_inv[0:3] + eps_sq * s
        last = near_cube[56:64] + near_cube[64:72] + near_cube[72:80]
        dotted = jnp.sum(x * s, axis=0, keepdims=True) - last[6:7]
        value = value + (x * dotted + last[3:6])
        cross = [jnp.sum(x * (near_cube[8 + 16 * i:11 + 16 * i] + near_cube[16 + 16 * i:19 + 16 * i]), axis=0,
                         keepdims=True) for i in range(3)]
        return [(value[i:i + 1] - cross[i]) * STOKES_SCALE for i in range(3)]

    def fetch(wide, local):
        at = pl.ds(pl.multiple_of(local * 8, 8), 8)
        return jnp.concatenate([wide[0, at, :], wide[1, at, :]], axis=1)

    def begin(slot, u):
        b = pairs[1, slot]
        ta = fetch(row_wide, pairs[0, slot] - row_base)
        tb = fetch(col_wide, b // row_span * per_device + b % per_device)
        ra, xx = prepare(ta)
        rb, yy = prepare(tb)
        distances(ta, tb, xx, yy, u)
        return ta, tb, ra, rb

    def finish(slot, u, ta, tb, ra, rb):
        for chunk in range(panels // CHUNK):
            at = slice(chunk * CHUNK, (chunk + 1) * CHUNK)
            inv_dist = lax.rsqrt(radius_sq[u, at, :])
            inv[u, at, :] = inv_dist.astype(jnp.bfloat16)
            cube[u, at, :] = (inv_dist * inv_dist * inv_dist).astype(jnp.bfloat16)
        product = functools.partial(lax.dot_general, preferred_element_type=jnp.float32)
        to_first = combine(product(rb[0:16], inv[u], across), product(rb, cube[u], across), ta)
        to_second = combine(product(ra[0:16], inv[u], down), product(ra, cube[u], down), tb)
        within = slot < count
        keep_second = within & (pairs[0, slot] != pairs[1, slot])
        for i in range(3):
            at = slice(i * panels, (i + 1) * panels)
            out_first[pl.ds(slot, 1), at] = jnp.where(within, to_first[i], 0.0)
            out_second[pl.ds(slot, 1), at] = jnp.where(keep_second, to_second[i], 0.0)

    def group(step, carry):
        held = begin(step * GROUP, 0)
        for u in range(GROUP):
            ahead = begin(step * GROUP + u + 1, u + 1) if u + 1 < GROUP else None
            finish(step * GROUP + u, u, *held)
            held = ahead
        return carry

    lax.fori_loop(0, (count + GROUP - 1) // GROUP, group, 0)


def near(per_device, pairs, live, row_tiles, col_tiles, far, coupling, parents, all_lifted, row_ids, col_ids):
    slots, panels = pairs.shape[1], row_tiles.shape[1]
    rank, clusters = coupling.shape[1], parents.shape[1]
    smem = pl.BlockSpec(memory_space=pltpu.SMEM)
    vmem = pl.BlockSpec(memory_space=pltpu.VMEM)
    shape = jax.ShapeDtypeStruct
    return pl.pallas_call(
        functools.partial(near_kernel, per_device),
        out_shape=[shape((slots, 3 * panels), jnp.float32)] * 2 + [
            shape((clusters // 4, rank), jnp.float32), shape((per_device, 2 * slots), jnp.bfloat16)],
        in_specs=[smem, smem] + [vmem] * 8,
        out_specs=[vmem] * 4,
        scratch_shapes=[
            pltpu.VMEM((2, row_tiles.shape[0] // 6 * 8, 128), jnp.float32),
            pltpu.VMEM((2, col_tiles.shape[0] // 6 * 8, 128), jnp.float32),
            pltpu.VMEM((clusters, 4 * rank), jnp.float32),
            pltpu.VMEM((coupling.shape[0], rank), jnp.float32),
            pltpu.VMEM((GROUP, panels, panels), jnp.float32),
        ] + [pltpu.VMEM((GROUP, panels, panels), jnp.bfloat16)] * 2,
        compiler_params=pltpu.CompilerParams(vmem_limit_bytes=48 * 1024 * 1024),
        name="near",
    )(pairs, live, row_tiles, col_tiles, far, coupling, parents, all_lifted, row_ids, col_ids)


def exchange_kernel(n_row, n_col, parent, out_first, out_second, partial, place, transfer, basis, velocity,
                    got_first, got_second, total, f1, f2, acc, red, parts, coef, far_part, own_sem, s1, r1, s2, r2, s3, r3, sa, ra, sb, rb):
    row, col = lax.axis_index("row"), lax.axis_index("col")
    ca, cb = out_first.shape[0] // n_col, out_second.shape[0] // n_row
    piece = partial.shape[0] // n_col
    own = [
        pltpu.make_async_copy(part(out_first, col, ca), part(got_first, col, ca), own_sem.at[0]),
        pltpu.make_async_copy(part(out_second, row, cb), part(got_second, row, cb), own_sem.at[1]),
    ]
    for copy in own:
        copy.start()
    f1[pl.ds(col, 1)] = partial[pl.ds(pl.multiple_of(col * piece, piece), piece), :][None]
    greet(n_row, n_col, row, col)
    started = []

    def send(src, dst, sends, recvs, slot, mine, device):
        copy = pltpu.make_async_remote_copy(
            src_ref=src, dst_ref=dst, send_sem=sends.at[slot], recv_sem=recvs.at[mine],
            device_id=device, device_id_type=MESH)
        copy.start()
        started.append(copy)

    for k in range(1, n_col):
        peer = lax.rem(col + k, n_col)
        send(part(partial, peer, piece), f1.at[col], s1, r1, peer, col, (row, peer))
    for k in range(1, n_col):
        peer = lax.rem(col + k, n_col)
        send(part(out_first, peer, ca), part(got_first, col, ca), sa, ra, peer, col, (row, peer))
    for k in range(1, n_row):
        peer = lax.rem(row + k, n_row)
        send(part(out_second, peer, cb), part(got_second, row, cb), sb, rb, peer, row, (peer, col))

    for k in range(1, n_col):
        src = lax.rem(col + k, n_col)
        pltpu.make_async_copy(f1.at[src], f1.at[src], r1.at[src]).wait()
    acc[...] = jnp.sum(f1[...], axis=0)
    f2[pl.ds(row, 1)] = acc[...][None]
    for k in range(1, n_row):
        peer = lax.rem(row + k, n_row)
        send(acc, f2.at[row], s2, r2, peer, row, (peer, col))
    for k in range(1, n_row):
        src = lax.rem(row + k, n_row)
        pltpu.make_async_copy(f2.at[src], f2.at[src], r2.at[src]).wait()
    red[...] = jnp.sum(f2[...], axis=0)
    keep = pltpu.make_async_copy(red, part(total, col, piece), own_sem.at[2])
    keep.start()
    for k in range(1, n_col):
        peer = lax.rem(col + k, n_col)
        send(red, part(total, col, piece), s3, r3, peer, col, (row, peer))
    for k in range(1, n_col):
        src = lax.rem(col + k, n_col)
        pltpu.make_async_copy(red, part(total, src, piece), r3.at[src]).wait()
    keep.wait()

    per_device, rank = parts.shape
    base = (row * n_col + col) * per_device
    for c in range(per_device):
        parts[c:c + 1, :] = total[pl.ds(parent[base + c], 1), :]
    turned = parts[...].T
    for c in range(per_device):
        coef[c:c + 1, :] = jnp.sum(transfer[c] * turned[:, c:c + 1], axis=0, keepdims=True)
    turned = coef[...].T
    for c in range(per_device):
        far_part[c:c + 1, :] = jnp.sum(basis[c].astype(jnp.float32) * turned[:, c:c + 1], axis=0, keepdims=True)

    for k in range(1, n_col):
        src = lax.rem(col + k, n_col)
        view = part(got_first, src, ca)
        pltpu.make_async_copy(view, view, ra.at[src]).wait()
    for k in range(1, n_row):
        src = lax.rem(row + k, n_row)
        view = part(got_second, src, cb)
        pltpu.make_async_copy(view, view, rb.at[src]).wait()
    for copy in own:
        copy.wait()
    slots = got_first.shape[0]
    velocity[...] = (far_part[...] + select_rows(place[:, :slots], got_first[...])
                     + select_rows(place[:, slots:], got_second[...]))
    for copy in started:
        copy.wait_send()


def exchange(n_row, n_col, parent, out_first, out_second, partial, place, transfer, basis):
    smem = pl.BlockSpec(memory_space=pltpu.SMEM)
    vmem = pl.BlockSpec(memory_space=pltpu.VMEM)
    dma = pltpu.SemaphoreType.DMA
    piece, rank = partial.shape[0] // n_col, partial.shape[1]
    per_device, width = place.shape[0], out_first.shape[1]
    sizes = [3, n_col, n_col, n_row, n_row, n_col, n_col, n_col, n_col, n_row, n_row]
    buffers = [out_first.shape, out_second.shape, partial.shape, (n_col, piece, rank), (n_row, piece, rank),
               (piece, rank), (piece, rank), (per_device, rank), (per_device, rank), (per_device, width)]
    return pl.pallas_call(
        functools.partial(exchange_kernel, n_row, n_col),
        out_shape=jax.ShapeDtypeStruct((per_device, width), jnp.float32),
        in_specs=[smem] + [vmem] * 6,
        out_specs=vmem,
        scratch_shapes=[pltpu.VMEM(size, jnp.float32) for size in buffers] + [dma((size,)) for size in sizes],
        compiler_params=pltpu.CompilerParams(
            collective_id=2, has_side_effects=True, vmem_limit_bytes=32 * 1024 * 1024),
        name="exchange",
    )(parent, out_first, out_second, partial, place, transfer, basis)


def shards(density, coords, basis, transfer, parent, near_pairs, near_count, far_pairs, coupling):
    highest = lax.Precision.HIGHEST
    per_device, _, panels = density.shape
    n_row, n_col = lax.axis_size("row"), lax.axis_size("col")
    tile = jnp.concatenate([density, coords], axis=1).transpose(1, 0, 2).reshape(6 * per_device, panels)
    flattened = density.reshape(per_device, 3 * panels)
    moments = jnp.einsum("crk,ck->cr", basis, flattened, preferred_element_type=jnp.float32)
    lifted = jnp.einsum("crs,cs->cr", transfer, moments, precision=highest)
    row_tiles, col_tiles, row_ids, col_ids, all_lifted = gather(
        n_row, n_col, tile, near_pairs, lifted.reshape(-1, 128))
    out_first, out_second, own_locals, place = near(
        per_device, near_pairs, near_count, row_tiles, col_tiles, far_pairs, coupling, parent.reshape(1, -1),
        all_lifted, row_ids, col_ids)
    velocity = exchange(n_row, n_col, parent, out_first, out_second, own_locals, place, transfer, basis)
    return velocity.reshape(per_device, 3, panels)


def solution(mesh):
    placed = (
        P(("row", "col"), None, None),
        P(("row", "col"), None, None),
        P(("row", "col"), None, None),
        P(("row", "col"), None, None),
        P(),
        P(None, ("row", "col")),
        P(("row", "col")),
        P(None, ("row", "col")),
        P(("row", "col"), None, None),
    )
    return jax.shard_map(
        shards, mesh=mesh, in_specs=placed, out_specs=P(("row", "col"), None, None), check_vma=False
    )
```

```python
import functools
import math

import jax
import jax.numpy as jnp
from jax import lax
from jax.experimental import pallas as pl
from jax.experimental.pallas import tpu as pltpu
from jax.sharding import PartitionSpec as P

REG_EPS = 0.02
STOKES_SCALE = 1.0 / (8.0 * math.pi)
MESH = pl.DeviceIdType.MESH
GROUP = 4
CHUNK = 16


def greet(n_row, n_col, row, col):
    barrier = pltpu.get_barrier_semaphore()
    for k in range(1, n_col):
        pl.semaphore_signal(barrier, inc=1, device_id=(row, lax.rem(col + k, n_col)), device_id_type=MESH)
    for k in range(1, n_row):
        pl.semaphore_signal(barrier, inc=1, device_id=(lax.rem(row + k, n_row), col), device_id_type=MESH)
    pl.semaphore_wait(barrier, n_col + n_row - 2)


def part(ref, index, size):
    return ref.at[pl.ds(pl.multiple_of(index * size, size), size)]


def lift(tile, basis, transfer, lifted):
    per_device, rank, width = basis.shape
    panels = width // 3
    source = tile[...].astype(jnp.float32)
    lane = lax.broadcasted_iota(jnp.int32, (rank, per_device), 1)
    turned = jnp.zeros((rank, per_device), jnp.float32)
    for c in range(per_device):
        total = sum(basis[c, :, i * panels:(i + 1) * panels].astype(jnp.float32)
                    * source[i * per_device + c:i * per_device + c + 1] for i in range(3))
        turned = jnp.where(lane == c, jnp.sum(total, axis=1, keepdims=True), turned)
    moments = turned.T
    turned = jnp.zeros((rank, per_device), jnp.float32)
    for c in range(per_device):
        total = jnp.sum(transfer[c] * moments[c:c + 1], axis=1, keepdims=True)
        turned = jnp.where(lane == c, total, turned)
    value = turned.T
    group = per_device // 4
    lifted[...] = jnp.concatenate([value[u * group:(u + 1) * group] for u in range(4)], axis=1)


def gather_kernel(n_row, n_col, n_z, tile, ids, basis, transfer, row_tiles, col_tiles, row_ids, col_ids, all_lifted,
                  lifted, own_sem, st, rt, sct, rct, si, ri, sci, rci, sl, rl, scl, rcl):
    row, col = lax.axis_index("row"), lax.axis_index("col")
    n_y = n_col // n_z
    z, y = col // n_y, lax.rem(col, n_y)
    rows, lift_rows = tile.shape[0], lifted.shape[0]
    span = n_col * lift_rows
    own = [
        pltpu.make_async_copy(tile, part(row_tiles, col, rows), own_sem.at[0]),
        pltpu.make_async_copy(tile, part(col_tiles, row, rows), own_sem.at[1]),
        pltpu.make_async_copy(ids, row_ids.at[col], own_sem.at[2]),
        pltpu.make_async_copy(ids, col_ids.at[row], own_sem.at[3]),
        pltpu.make_async_copy(lifted, part(all_lifted, row * n_col + col, lift_rows), own_sem.at[4]),
    ]
    for copy in own[:4]:
        copy.start()
    greet(n_row, n_col, row, col)

    def to_col(src, dst, index, size, sends, recvs, slot, peer):
        return pltpu.make_async_remote_copy(
            src_ref=src, dst_ref=part(dst, index, size), send_sem=sends.at[slot], recv_sem=recvs.at[index],
            device_id=(row, peer), device_id_type=MESH)

    def to_row(src, dst_view, sends, recvs, peer):
        return pltpu.make_async_remote_copy(
            src_ref=src, dst_ref=dst_view, send_sem=sends.at[peer], recv_sem=recvs.at[row],
            device_id=(peer, col), device_id_type=MESH)

    started = []

    def go(copy):
        copy.start()
        started.append(copy)

    for k in range(1, n_z):
        peer = lax.rem(z + k, n_z) * n_y + y
        go(to_col(tile, row_tiles, col, rows, st, rt, k, peer))
    for k in range(1, n_y):
        peer = z * n_y + lax.rem(y + k, n_y)
        go(to_col(tile, row_tiles, col, rows, st, rt, n_z + k, peer))
    for k in range(1, n_row):
        peer = lax.rem(row + k, n_row)
        go(to_row(tile, part(col_tiles, row, rows), sct, rct, peer))
        go(to_row(ids, col_ids.at[row], sci, rci, peer))
    for k in range(1, n_col):
        peer = lax.rem(col + k, n_col)
        go(pltpu.make_async_remote_copy(
            src_ref=ids, dst_ref=row_ids.at[col], send_sem=si.at[peer], recv_sem=ri.at[col],
            device_id=(row, peer), device_id_type=MESH))

    lift(tile, basis, transfer, lifted)
    own[4].start()
    for k in range(1, n_col):
        peer = lax.rem(col + k, n_col)
        go(pltpu.make_async_remote_copy(
            src_ref=lifted, dst_ref=part(all_lifted, row * n_col + col, lift_rows),
            send_sem=sl.at[peer], recv_sem=rl.at[col], device_id=(row, peer), device_id_type=MESH))
    own[4].wait()
    for k in range(1, n_col):
        src = lax.rem(col + k, n_col)
        pltpu.make_async_copy(lifted, part(all_lifted, row * n_col + src, lift_rows), rl.at[src]).wait()
    for k in range(1, n_row):
        peer = lax.rem(row + k, n_row)
        mine = part(all_lifted, row, span)
        go(to_row(mine, mine, scl, rcl, peer))

    for k in range(1, n_z):
        src = lax.rem(z + k, n_z) * n_y + y
        pltpu.make_async_copy(tile, part(row_tiles, src, rows), rt.at[src]).wait()
        for j in range(1, n_y):
            peer = z * n_y + lax.rem(y + j, n_y)
            go(to_col(part(row_tiles, src, rows), row_tiles, src, rows, st, rt, n_z + n_y * k + j, peer))
    for j in range(1, n_y):
        for k in range(n_z):
            src = lax.rem(z + k, n_z) * n_y + lax.rem(y + j, n_y)
            pltpu.make_async_copy(tile, part(row_tiles, src, rows), rt.at[src]).wait()
    for k in range(1, n_col):
        src = lax.rem(col + k, n_col)
        pltpu.make_async_copy(ids, row_ids.at[src], ri.at[src]).wait()
    for k in range(1, n_row):
        src = lax.rem(row + k, n_row)
        pltpu.make_async_copy(tile, part(col_tiles, src, rows), rct.at[src]).wait()
        pltpu.make_async_copy(ids, col_ids.at[src], rci.at[src]).wait()
        view = part(all_lifted, src, span)
        pltpu.make_async_copy(view, view, rcl.at[src]).wait()
    for copy in own[:4]:
        copy.wait()
    for copy in started:
        copy.wait_send()


def gather(n_row, n_col, tile, ids, basis, transfer):
    n_z = 4 if n_col % 4 == 0 else 1
    vmem = pl.BlockSpec(memory_space=pltpu.VMEM)
    dma = pltpu.SemaphoreType.DMA
    sizes = [(5,), (n_z * (n_col // n_z + 1) + n_col,), (n_col,), (n_row,), (n_row,), (n_col,), (n_col,),
             (n_row,), (n_row,), (n_col,), (n_col,), (n_row,), (n_row,)]
    shape = jax.ShapeDtypeStruct
    lift_shape = (basis.shape[0] // 4, 4 * basis.shape[1])
    return pl.pallas_call(
        functools.partial(gather_kernel, n_row, n_col, n_z),
        out_shape=[
            shape((n_col * tile.shape[0], tile.shape[1]), tile.dtype),
            shape((n_row * tile.shape[0], tile.shape[1]), tile.dtype),
            shape((n_col,) + ids.shape, ids.dtype),
            shape((n_row,) + ids.shape, ids.dtype),
            shape((n_row * n_col * lift_shape[0], lift_shape[1]), jnp.float32),
        ],
        in_specs=[vmem] * 4,
        out_specs=[vmem] * 5,
        scratch_shapes=[pltpu.VMEM(lift_shape, jnp.float32)] + [dma(size) for size in sizes],
        compiler_params=pltpu.CompilerParams(
            collective_id=1, has_side_effects=True, vmem_limit_bytes=32 * 1024 * 1024),
        name="gather",
    )(tile, ids, basis, transfer)


def split(wide, terms=3):
    out = []
    for _ in range(terms - 1):
        term = wide.astype(jnp.bfloat16).astype(jnp.float32)
        out.append(term)
        wide = wide - term
    return out + [wide]


def select_rows(one_hot, wide):
    return sum(jnp.dot(one_hot, term.astype(jnp.bfloat16), preferred_element_type=jnp.float32)
               for term in split(wide))


def as_one_hot(where_true):
    return jnp.where(where_true, 1.0, 0.0).astype(jnp.bfloat16)


def couple(far, coupling, parents, all_lifted, lifted, moved, own_locals):
    total, rank = own_locals.shape
    pairs = far.shape[1]
    for u in range(4):
        turned = pltpu.roll(all_lifted[...], (4 - u) % 4 * rank, 1)
        lifted[:, u] = turned.reshape(lifted.shape[0], lifted.shape[2], 4 * rank)
    clusters = parents.shape[1]
    parent_row = lax.broadcasted_iota(jnp.int32, (total, 1), 0)
    moments = select_rows(as_one_hot(parent_row == parents[...]), lifted[...].reshape(clusters, 4 * rank)[:, :rank])
    lane = lax.broadcasted_iota(jnp.int32, (pairs, total), 1).astype(jnp.float32)
    sources = []
    for side in range(2):
        column = jnp.broadcast_to(far[side:side + 1, :].astype(jnp.float32), (8, pairs)).T[:, 0:1]
        sources.append(select_rows(as_one_hot(lane == column), moments))
    turned = sources[0].T
    pair_lane = lax.broadcasted_iota(jnp.int32, (rank, pairs), 1)
    to_first = jnp.zeros((rank, pairs), jnp.float32)
    for k in range(pairs):
        block = coupling[k]
        to_first = jnp.where(pair_lane == k, jnp.sum(block * sources[1][k:k + 1], axis=1, keepdims=True), to_first)
        moved[k:k + 1, :] = jnp.sum(block * turned[:, k:k + 1], axis=0, keepdims=True)
    own_locals[...] = (select_rows(as_one_hot(parent_row == far[0:1, :]), to_first.T)
                       + select_rows(as_one_hot(parent_row == far[1:2, :]), moved[...]))


def placement(row_ids, col_ids, place):
    per_device, slots = place.shape[0], row_ids.shape[2]
    n_row, n_col = col_ids.shape[0], row_ids.shape[0]
    row, col = lax.axis_index("row"), lax.axis_index("col")
    base = (row * n_col + col) * per_device
    lane = lax.broadcasted_iota(jnp.int32, (8, slots), 1)
    cluster = lax.broadcasted_iota(jnp.int32, (per_device, slots), 0) + base
    for ids, side, sources, mine, start in ((row_ids, 0, n_col, col, 0), (col_ids, 1, n_row, row, slots)):
        size = slots // sources
        owners = jnp.zeros((8, slots), jnp.int32)
        for src in range(sources):
            from_src = jnp.broadcast_to(ids[src, side:side + 1, :], (8, slots))
            shift = lax.rem((src - mine) * size + slots, slots)
            owners = jnp.where(lane // size == src, pltpu.roll(from_src, shift, 1), owners)
        place[:, start:start + slots] = as_one_hot(cluster == owners[0:1, :])


def near_kernel(per_device, pairs, live, row_tiles, col_tiles, far, coupling, parents, all_lifted, row_ids, col_ids,
                sent_first, sent_second, own_locals, place, out_first, out_second, row_wide, col_wide, lifted, moved, radius_sq, inv, cube):
    for narrow, wide in ((row_tiles, row_wide), (col_tiles, col_wide)):
        for src in range(narrow.shape[0] // (6 * per_device)):
            for i in range(8):
                if i < 6:
                    start = (src * 6 + i) * per_device
                    rows = narrow[start:start + per_device, :].astype(jnp.float32)
                else:
                    rows = jnp.full((per_device, narrow.shape[1]), 7.0 - i, jnp.float32)
                for half in range(2):
                    at = pl.ds(src * per_device * 8 + i, per_device, stride=8)
                    wide[half, at, :] = rows[:, half * 128:(half + 1) * 128]

    couple(far, coupling, parents, all_lifted, lifted, moved, own_locals)
    placement(row_ids, col_ids, place)
    row_span = per_device * row_ids.shape[0]
    row_base = lax.axis_index("row") * row_span
    out_first[...] = jnp.zeros_like(out_first)
    out_second[...] = jnp.zeros_like(out_second)
    panels = row_tiles.shape[1]
    count = live[0]
    eps_sq = REG_EPS * REG_EPS
    across = (((1,), (1,)), ((), ()))
    down = (((1,), (0,)), ((), ()))

    sub = lax.broadcasted_iota(jnp.int32, (8, panels), 0)
    ones = jnp.ones((1, panels), jnp.float32)

    def prepare(tile):
        products = [tile * tile[3 + i:4 + i, :] for i in range(3)]
        y_f = products[0][0:1] + products[1][1:2] + products[2][2:3]
        y_y = products[0][3:4] + products[1][4:5] + products[2][5:6]
        blocks = [tile]
        for product in products:
            high = product.astype(jnp.bfloat16).astype(jnp.float32)
            blocks += [high, product - high]
        blocks += split(tile * y_f)
        return jnp.concatenate(blocks, axis=0).astype(jnp.bfloat16), y_y

    def distances(ta, tb, xx, yy, u):
        x_high, x_mid, x_low = split(xx)
        y_high, y_mid, y_low = split(yy + eps_sq)
        left0 = jnp.where(sub == 0, x_high, jnp.where(sub == 1, x_mid, jnp.where(sub == 2, x_low, jnp.where(
            sub < 6, -2.0 * ta, ta))))
        right0 = jnp.where(sub < 3, ones, jnp.where(sub == 6, y_high, tb))
        left1 = jnp.where(sub < 2, ones, 0.0)
        right1 = jnp.where(sub == 0, y_mid, jnp.where(sub == 1, y_low, 0.0))
        left = jnp.concatenate([left0, left1], axis=0).T.astype(jnp.bfloat16)
        right = jnp.concatenate([right0, right1], axis=0).astype(jnp.bfloat16)
        radius_sq[u] = jnp.dot(left, right, preferred_element_type=jnp.float32)

    def combine(near_inv, near_cube, tile):
        x = tile[3:6]
        s = near_cube[0:3]
        value = near_inv[0:3] + eps_sq * s
        last = near_cube[56:64] + near_cube[64:72] + near_cube[72:80]
        dotted = jnp.sum(x * s, axis=0, keepdims=True) - last[6:7]
        value = value + (x * dotted + last[3:6])
        cross = [jnp.sum(x * (near_cube[8 + 16 * i:11 + 16 * i] + near_cube[16 + 16 * i:19 + 16 * i]), axis=0,
                         keepdims=True) for i in range(3)]
        return [(value[i:i + 1] - cross[i]) * STOKES_SCALE for i in range(3)]

    def fetch(wide, local):
        at = pl.ds(pl.multiple_of(local * 8, 8), 8)
        return jnp.concatenate([wide[0, at, :], wide[1, at, :]], axis=1)

    def begin(slot, u):
        b = pairs[1, slot]
        ta = fetch(row_wide, pairs[0, slot] - row_base)
        tb = fetch(col_wide, b // row_span * per_device + b % per_device)
        ra, xx = prepare(ta)
        rb, yy = prepare(tb)
        distances(ta, tb, xx, yy, u)
        return ta, tb, ra, rb

    def finish(slot, u, ta, tb, ra, rb):
        for chunk in range(panels // CHUNK):
            at = slice(chunk * CHUNK, (chunk + 1) * CHUNK)
            inv_dist = lax.rsqrt(radius_sq[u, at, :])
            inv[u, at, :] = inv_dist.astype(jnp.bfloat16)
            cube[u, at, :] = (inv_dist * inv_dist * inv_dist).astype(jnp.bfloat16)
        product = functools.partial(lax.dot_general, preferred_element_type=jnp.float32)
        to_first = combine(product(rb[0:16], inv[u], across), product(rb, cube[u], across), ta)
        to_second = combine(product(ra[0:16], inv[u], down), product(ra, cube[u], down), tb)
        within = slot < count
        keep_second = within & (pairs[0, slot] != pairs[1, slot])
        for i in range(3):
            at = slice(i * panels, (i + 1) * panels)
            out_first[pl.ds(slot, 1), at] = jnp.where(within, to_first[i], 0.0)
            out_second[pl.ds(slot, 1), at] = jnp.where(keep_second, to_second[i], 0.0)

    def group(step, carry):
        held = begin(step * GROUP, 0)
        for u in range(GROUP):
            ahead = begin(step * GROUP + u + 1, u + 1) if u + 1 < GROUP else None
            finish(step * GROUP + u, u, *held)
            held = ahead
        return carry

    lax.fori_loop(0, (count + GROUP - 1) // GROUP, group, 0)
    for out, sent in ((out_first, sent_first), (out_second, sent_second)):
        size = sent.shape[1]
        for k in range(sent.shape[0]):
            sent[k] = out[k * size:(k + 1) * size, :].astype(jnp.bfloat16)


def near(per_device, pairs, live, row_tiles, col_tiles, far, coupling, parents, all_lifted, row_ids, col_ids):
    slots, panels = pairs.shape[1], row_tiles.shape[1]
    rank, clusters = coupling.shape[1], parents.shape[1]
    smem = pl.BlockSpec(memory_space=pltpu.SMEM)
    vmem = pl.BlockSpec(memory_space=pltpu.VMEM)
    shape = jax.ShapeDtypeStruct
    return pl.pallas_call(
        functools.partial(near_kernel, per_device),
        out_shape=[shape((n, slots // n, 3 * panels), jnp.bfloat16) for n in (row_ids.shape[0], col_ids.shape[0])] + [
            shape((clusters // 4, rank), jnp.float32), shape((per_device, 2 * slots), jnp.bfloat16)],
        in_specs=[smem, smem] + [vmem] * 8,
        out_specs=[vmem] * 4,
        scratch_shapes=[pltpu.VMEM((slots, 3 * panels), jnp.float32)] * 2 + [
            pltpu.VMEM((2, row_tiles.shape[0] // 6 * 8, 128), jnp.float32),
            pltpu.VMEM((2, col_tiles.shape[0] // 6 * 8, 128), jnp.float32),
            pltpu.VMEM((clusters // per_device, 4, per_device // 4, 4 * rank), jnp.float32),
            pltpu.VMEM((coupling.shape[0], rank), jnp.float32),
            pltpu.VMEM((GROUP, panels, panels), jnp.float32),
        ] + [pltpu.VMEM((GROUP, panels, panels), jnp.bfloat16)] * 2,
        compiler_params=pltpu.CompilerParams(vmem_limit_bytes=48 * 1024 * 1024),
        name="near",
    )(pairs, live, row_tiles, col_tiles, far, coupling, parents, all_lifted, row_ids, col_ids)


def exchange_kernel(n_row, n_col, parent, out_first, out_second, partial, place, transfer, basis, velocity,
                    got_first, got_second, total, f1, f2, acc, red, parts, coef, far_part, own_sem, s1, r1, s2, r2, s3, r3, sa, ra, sb, rb):
    row, col = lax.axis_index("row"), lax.axis_index("col")
    piece = partial.shape[0] // n_col
    own = [
        pltpu.make_async_copy(out_first.at[col], got_first.at[col], own_sem.at[0]),
        pltpu.make_async_copy(out_second.at[row], got_second.at[row], own_sem.at[1]),
    ]
    for copy in own:
        copy.start()
    f1[pl.ds(col, 1)] = partial[pl.ds(pl.multiple_of(col * piece, piece), piece), :][None]
    greet(n_row, n_col, row, col)
    started = []

    def send(src, dst, sends, recvs, slot, mine, device):
        copy = pltpu.make_async_remote_copy(
            src_ref=src, dst_ref=dst, send_sem=sends.at[slot], recv_sem=recvs.at[mine],
            device_id=device, device_id_type=MESH)
        copy.start()
        started.append(copy)

    for k in range(1, n_col):
        peer = lax.rem(col + k, n_col)
        send(part(partial, peer, piece), f1.at[col], s1, r1, peer, col, (row, peer))
    for k in range(1, n_col):
        peer = lax.rem(col + k, n_col)
        send(out_first.at[peer], got_first.at[col], sa, ra, peer, col, (row, peer))
    for k in range(1, n_row):
        peer = lax.rem(row + k, n_row)
        send(out_second.at[peer], got_second.at[row], sb, rb, peer, row, (peer, col))

    for k in range(1, n_col):
        src = lax.rem(col + k, n_col)
        pltpu.make_async_copy(f1.at[src], f1.at[src], r1.at[src]).wait()
    acc[...] = jnp.sum(f1[...], axis=0)
    f2[pl.ds(row, 1)] = acc[...][None]
    for k in range(1, n_row):
        peer = lax.rem(row + k, n_row)
        send(acc, f2.at[row], s2, r2, peer, row, (peer, col))
    for k in range(1, n_row):
        src = lax.rem(row + k, n_row)
        pltpu.make_async_copy(f2.at[src], f2.at[src], r2.at[src]).wait()
    red[...] = jnp.sum(f2[...], axis=0)
    keep = pltpu.make_async_copy(red, part(total, col, piece), own_sem.at[2])
    keep.start()
    for k in range(1, n_col):
        peer = lax.rem(col + k, n_col)
        send(red, part(total, col, piece), s3, r3, peer, col, (row, peer))
    for k in range(1, n_col):
        src = lax.rem(col + k, n_col)
        pltpu.make_async_copy(red, part(total, src, piece), r3.at[src]).wait()
    keep.wait()

    per_device, rank = parts.shape
    base = (row * n_col + col) * per_device
    for c in range(per_device):
        parts[c:c + 1, :] = total[pl.ds(parent[base + c], 1), :]
    turned = parts[...].T
    for c in range(per_device):
        coef[c:c + 1, :] = jnp.sum(transfer[c] * turned[:, c:c + 1], axis=0, keepdims=True)
    turned = coef[...].T
    for c in range(per_device):
        far_part[c:c + 1, :] = jnp.sum(basis[c].astype(jnp.float32) * turned[:, c:c + 1], axis=0, keepdims=True)

    for k in range(1, n_col):
        src = lax.rem(col + k, n_col)
        view = got_first.at[src]
        pltpu.make_async_copy(view, view, ra.at[src]).wait()
    for k in range(1, n_row):
        src = lax.rem(row + k, n_row)
        view = got_second.at[src]
        pltpu.make_async_copy(view, view, rb.at[src]).wait()
    for copy in own:
        copy.wait()
    slots = place.shape[1] // 2
    value = far_part[...]
    for got, start in ((got_first, 0), (got_second, slots)):
        rows = got[...].astype(jnp.float32).reshape(slots, got.shape[2]).astype(jnp.bfloat16)
        value = value + jnp.dot(place[:, start:start + slots], rows, preferred_element_type=jnp.float32)
    velocity[...] = value
    for copy in started:
        copy.wait_send()


def exchange(n_row, n_col, parent, out_first, out_second, partial, place, transfer, basis):
    smem = pl.BlockSpec(memory_space=pltpu.SMEM)
    vmem = pl.BlockSpec(memory_space=pltpu.VMEM)
    dma = pltpu.SemaphoreType.DMA
    piece, rank = partial.shape[0] // n_col, partial.shape[1]
    per_device, width = place.shape[0], out_first.shape[2]
    sizes = [3, n_col, n_col, n_row, n_row, n_col, n_col, n_col, n_col, n_row, n_row]
    buffers = [partial.shape, (n_col, piece, rank), (n_row, piece, rank),
               (piece, rank), (piece, rank), (per_device, rank), (per_device, rank), (per_device, width)]
    return pl.pallas_call(
        functools.partial(exchange_kernel, n_row, n_col),
        out_shape=jax.ShapeDtypeStruct((per_device, width), jnp.float32),
        in_specs=[smem] + [vmem] * 6,
        out_specs=vmem,
        scratch_shapes=[pltpu.VMEM(out_first.shape, jnp.bfloat16), pltpu.VMEM(out_second.shape, jnp.bfloat16)] + [
            pltpu.VMEM(size, jnp.float32) for size in buffers] + [dma((size,)) for size in sizes],
        compiler_params=pltpu.CompilerParams(
            collective_id=2, has_side_effects=True, vmem_limit_bytes=32 * 1024 * 1024),
        name="exchange",
    )(parent, out_first, out_second, partial, place, transfer, basis)


def shards(density, coords, basis, transfer, parent, near_pairs, near_count, far_pairs, coupling):
    per_device, _, panels = density.shape
    n_row, n_col = lax.axis_size("row"), lax.axis_size("col")
    tile = jnp.concatenate([density, coords], axis=1).transpose(1, 0, 2).reshape(6 * per_device, panels)
    row_tiles, col_tiles, row_ids, col_ids, all_lifted = gather(
        n_row, n_col, tile, near_pairs, basis, transfer)
    out_first, out_second, own_locals, place = near(
        per_device, near_pairs, near_count, row_tiles, col_tiles, far_pairs, coupling, parent.reshape(1, -1),
        all_lifted, row_ids, col_ids)
    velocity = exchange(n_row, n_col, parent, out_first, out_second, own_locals, place, transfer, basis)
    return velocity.reshape(per_device, 3, panels)


def solution(mesh):
    placed = (
        P(("row", "col"), None, None),
        P(("row", "col"), None, None),
        P(("row", "col"), None, None),
        P(("row", "col"), None, None),
        P(),
        P(None, ("row", "col")),
        P(("row", "col")),
        P(None, ("row", "col")),
        P(("row", "col"), None, None),
    )
    return jax.shard_map(
        shards, mesh=mesh, in_specs=placed, out_specs=P(("row", "col"), None, None), check_vma=False
    )
```

```python
import functools
import math

import jax
import jax.numpy as jnp
from jax import lax
from jax.experimental import pallas as pl
from jax.experimental.pallas import tpu as pltpu
from jax.sharding import PartitionSpec as P

REG_EPS = 0.02
STOKES_SCALE = 1.0 / (8.0 * math.pi)
MESH = pl.DeviceIdType.MESH
GROUP = 4
CHUNK = 16


def greet(n_row, n_col, row, col):
    barrier = pltpu.get_barrier_semaphore()
    for k in range(1, n_col):
        pl.semaphore_signal(barrier, inc=1, device_id=(row, lax.rem(col + k, n_col)), device_id_type=MESH)
    for k in range(1, n_row):
        pl.semaphore_signal(barrier, inc=1, device_id=(lax.rem(row + k, n_row), col), device_id_type=MESH)


def meet(n_row, n_col):
    pl.semaphore_wait(pltpu.get_barrier_semaphore(), n_col + n_row - 2)


def part(ref, index, size):
    return ref.at[pl.ds(pl.multiple_of(index * size, size), size)]


def split(wide, terms=3):
    out = []
    for _ in range(terms - 1):
        term = wide.astype(jnp.bfloat16).astype(jnp.float32)
        out.append(term)
        wide = wide - term
    return out + [wide]


def select_rows(one_hot, wide):
    return sum(jnp.dot(one_hot, term.astype(jnp.bfloat16), preferred_element_type=jnp.float32)
               for term in split(wide))


def as_one_hot(where_true):
    return jnp.where(where_true, 1.0, 0.0).astype(jnp.bfloat16)


def couple(far, coupling, parents, all_lifted, lifted, moved, own_locals):
    total, rank = own_locals.shape
    pairs = far.shape[1]
    for u in range(4):
        turned = pltpu.roll(all_lifted[...], (4 - u) % 4 * rank, 1)
        lifted[:, u] = turned.reshape(lifted.shape[0], lifted.shape[2], 4 * rank)
    clusters = parents.shape[1]
    parent_row = lax.broadcasted_iota(jnp.int32, (total, 1), 0)
    moments = select_rows(as_one_hot(parent_row == parents[...]), lifted[...].reshape(clusters, 4 * rank)[:, :rank])
    lane = lax.broadcasted_iota(jnp.int32, (pairs, total), 1).astype(jnp.float32)
    sources = []
    for side in range(2):
        column = jnp.broadcast_to(far[side:side + 1, :].astype(jnp.float32), (8, pairs)).T[:, 0:1]
        sources.append(select_rows(as_one_hot(lane == column), moments))
    turned = sources[0].T
    pair_lane = lax.broadcasted_iota(jnp.int32, (rank, pairs), 1)
    to_first = jnp.zeros((rank, pairs), jnp.float32)
    for k in range(pairs):
        block = coupling[k]
        to_first = jnp.where(pair_lane == k, jnp.sum(block * sources[1][k:k + 1], axis=1, keepdims=True), to_first)
        moved[k:k + 1, :] = jnp.sum(block * turned[:, k:k + 1], axis=0, keepdims=True)
    own_locals[...] = (select_rows(as_one_hot(parent_row == far[0:1, :]), to_first.T)
                       + select_rows(as_one_hot(parent_row == far[1:2, :]), moved[...]))


def lift(tile, basis, transfer, lifted):
    per_device, rank, width = basis.shape
    panels = width // 3
    source = tile[...].astype(jnp.float32)
    lane = lax.broadcasted_iota(jnp.int32, (rank, per_device), 1)
    turned = jnp.zeros((rank, per_device), jnp.float32)
    for c in range(per_device):
        total = sum(basis[c, :, i * panels:(i + 1) * panels].astype(jnp.float32)
                    * source[i * per_device + c:i * per_device + c + 1] for i in range(3))
        turned = jnp.where(lane == c, jnp.sum(total, axis=1, keepdims=True), turned)
    moments = turned.T
    turned = jnp.zeros((rank, per_device), jnp.float32)
    for c in range(per_device):
        total = jnp.sum(transfer[c] * moments[c:c + 1], axis=1, keepdims=True)
        turned = jnp.where(lane == c, total, turned)
    value = turned.T
    group = per_device // 4
    lifted[...] = jnp.concatenate([value[u * group:(u + 1) * group] for u in range(4)], axis=1)


def gather_kernel(n_row, n_col, n_z, tile, ids, far, parents, basis, transfer, coupling,
                  row_tiles, col_tiles, row_ids, col_ids, total,
                  basis_in, transfer_in, coupling_in, lifted, all_lifted, natural, moved, partial, f1, f2, acc, red,
                  own_sem, in_sem, st, rt, sct, rct, si, ri, sci, rci, sl, rl, scl, rcl, s1, r1, s2, r2, s3, r3):
    row, col = lax.axis_index("row"), lax.axis_index("col")
    n_y = n_col // n_z
    z, y = col // n_y, lax.rem(col, n_y)
    rows, lift_rows = tile.shape[0], lifted.shape[0]
    piece = partial.shape[0] // n_col
    span = n_col * lift_rows
    loads = [
        pltpu.make_async_copy(basis, basis_in, in_sem.at[0]),
        pltpu.make_async_copy(transfer, transfer_in, in_sem.at[1]),
        pltpu.make_async_copy(coupling, coupling_in, in_sem.at[2]),
    ]
    for copy in loads:
        copy.start()
    greet(n_row, n_col, row, col)
    own = [
        pltpu.make_async_copy(tile, part(row_tiles, col, rows), own_sem.at[0]),
        pltpu.make_async_copy(tile, part(col_tiles, row, rows), own_sem.at[1]),
        pltpu.make_async_copy(ids, row_ids.at[col], own_sem.at[2]),
        pltpu.make_async_copy(ids, col_ids.at[row], own_sem.at[3]),
    ]
    for copy in own:
        copy.start()
    loads[0].wait()
    loads[1].wait()
    lift(tile, basis_in, transfer_in, lifted)
    mine = pltpu.make_async_copy(lifted, part(all_lifted, row * n_col + col, lift_rows), own_sem.at[4])
    mine.start()
    meet(n_row, n_col)
    started = []

    def send(src, dst, sends, slot, recvs, index, device):
        copy = pltpu.make_async_remote_copy(
            src_ref=src, dst_ref=dst, send_sem=sends.at[slot], recv_sem=recvs.at[index],
            device_id=device, device_id_type=MESH)
        copy.start()
        started.append(copy)

    def arrive(view, sem):
        pltpu.make_async_copy(view, view, sem).wait()

    col_peers = [lax.rem(col + k, n_col) for k in range(1, n_col)]
    row_peers = [lax.rem(row + k, n_row) for k in range(1, n_row)]

    def forward(k):
        src = lax.rem(z + k, n_z) * n_y + y
        view = part(row_tiles, src, rows)
        arrive(view, rt.at[src])
        for j in range(1, n_y):
            send(view, view, st, n_z + n_y * k + j, rt, src, (row, z * n_y + lax.rem(y + j, n_y)))

    for peer in col_peers:
        send(lifted, part(all_lifted, row * n_col + col, lift_rows), sl, peer, rl, col, (row, peer))
    for k in range(1, n_z):
        send(tile, part(row_tiles, col, rows), st, k, rt, col, (row, lax.rem(z + k, n_z) * n_y + y))
    for k in range(1, n_y):
        send(tile, part(row_tiles, col, rows), st, n_z + k, rt, col, (row, z * n_y + lax.rem(y + k, n_y)))
    for peer in row_peers:
        send(tile, part(col_tiles, row, rows), sct, peer, rct, row, (peer, col))
        send(ids, col_ids.at[row], sci, peer, rci, row, (peer, col))
    for peer in col_peers:
        send(ids, row_ids.at[col], si, peer, ri, col, (row, peer))

    mine.wait()
    for src in col_peers:
        arrive(part(all_lifted, row * n_col + src, lift_rows), rl.at[src])
    for peer in row_peers:
        send(part(all_lifted, row, span), part(all_lifted, row, span), scl, peer, rcl, row, (peer, col))
    loads[2].wait()
    for src in row_peers:
        arrive(part(all_lifted, src, span), rcl.at[src])
    forward(1)
    couple(far, coupling_in, parents, all_lifted, natural, moved, partial)
    f1[pl.ds(col, 1)] = partial[pl.ds(pl.multiple_of(col * piece, piece), piece), :][None]
    for peer in col_peers:
        send(part(partial, peer, piece), f1.at[col], s1, peer, r1, col, (row, peer))
    for k in range(2, n_z):
        forward(k)

    for src in col_peers:
        arrive(f1.at[src], r1.at[src])
    acc[...] = jnp.sum(f1[...], axis=0)
    f2[pl.ds(row, 1)] = acc[...][None]
    for peer in row_peers:
        send(acc, f2.at[row], s2, peer, r2, row, (peer, col))
    for src in row_peers:
        arrive(f2.at[src], r2.at[src])
    red[...] = jnp.sum(f2[...], axis=0)
    keep = pltpu.make_async_copy(red, part(total, col, piece), own_sem.at[5])
    keep.start()
    for peer in col_peers:
        send(red, part(total, col, piece), s3, peer, r3, col, (row, peer))

    for j in range(1, n_y):
        for k in range(n_z):
            src = lax.rem(z + k, n_z) * n_y + lax.rem(y + j, n_y)
            arrive(part(row_tiles, src, rows), rt.at[src])
    for src in col_peers:
        arrive(row_ids.at[src], ri.at[src])
        arrive(part(total, src, piece), r3.at[src])
    for src in row_peers:
        arrive(part(col_tiles, src, rows), rct.at[src])
        arrive(col_ids.at[src], rci.at[src])
    keep.wait()
    for copy in own:
        copy.wait()
    for copy in started:
        copy.wait_send()


def gather(n_row, n_col, tile, ids, far, parents, basis, transfer, coupling):
    n_z = 4 if n_col % 4 == 0 else 1
    vmem = pl.BlockSpec(memory_space=pltpu.VMEM)
    any_space = pl.BlockSpec(memory_space=pl.ANY)
    per_device, rank = basis.shape[:2]
    clusters, parent_total = parents.shape[1], parents.shape[1] // 4
    piece = parent_total // n_col
    steps = n_z * (n_col // n_z + 1) + n_col
    sizes = [6, 3, steps, n_col, n_row, n_row, n_col, n_col, n_row, n_row, n_col, n_col, n_row, n_row,
             n_col, n_col, n_row, n_row, n_col, n_col]
    shape = jax.ShapeDtypeStruct
    group = per_device // 4
    buffers = [transfer.shape, coupling.shape, (group, 4 * rank), (clusters // 4, 4 * rank),
               (clusters // per_device, 4, group, 4 * rank), (coupling.shape[0], rank), (parent_total, rank),
               (n_col, piece, rank), (n_row, piece, rank), (piece, rank), (piece, rank)]
    return pl.pallas_call(
        functools.partial(gather_kernel, n_row, n_col, n_z),
        out_shape=[
            shape((n_col * tile.shape[0], tile.shape[1]), tile.dtype),
            shape((n_row * tile.shape[0], tile.shape[1]), tile.dtype),
            shape((n_col,) + ids.shape, ids.dtype),
            shape((n_row,) + ids.shape, ids.dtype),
            shape((parent_total, rank), jnp.float32),
        ],
        in_specs=[vmem] * 4 + [any_space] * 3,
        out_specs=[vmem] * 5,
        scratch_shapes=[pltpu.VMEM(basis.shape, basis.dtype)] + [pltpu.VMEM(size, jnp.float32) for size in buffers]
        + [pltpu.SemaphoreType.DMA((size,)) for size in sizes],
        compiler_params=pltpu.CompilerParams(
            collective_id=1, has_side_effects=True, vmem_limit_bytes=32 * 1024 * 1024),
        name="gather",
    )(tile, ids, far, parents, basis, transfer, coupling)


def placement(row_ids, col_ids, place):
    per_device, slots = place.shape[0], row_ids.shape[2]
    n_row, n_col = col_ids.shape[0], row_ids.shape[0]
    row, col = lax.axis_index("row"), lax.axis_index("col")
    base = (row * n_col + col) * per_device
    lane = lax.broadcasted_iota(jnp.int32, (8, slots), 1)
    cluster = lax.broadcasted_iota(jnp.int32, (per_device, slots), 0) + base
    for ids, side, sources, mine, start in ((row_ids, 0, n_col, col, 0), (col_ids, 1, n_row, row, slots)):
        size = slots // sources
        owners = jnp.zeros((8, slots), jnp.int32)
        for src in range(sources):
            from_src = jnp.broadcast_to(ids[src, side:side + 1, :], (8, slots))
            shift = lax.rem((src - mine) * size + slots, slots)
            owners = jnp.where(lane // size == src, pltpu.roll(from_src, shift, 1), owners)
        place[:, start:start + slots] = as_one_hot(cluster == owners[0:1, :])


def near_kernel(per_device, pairs, live, row_tiles, col_tiles, row_ids, col_ids,
                sent_first, sent_second, place, out_first, out_second, row_wide, col_wide, radius_sq, inv, cube):
    for narrow, wide in ((row_tiles, row_wide), (col_tiles, col_wide)):
        for src in range(narrow.shape[0] // (6 * per_device)):
            for i in range(8):
                if i < 6:
                    start = (src * 6 + i) * per_device
                    rows = narrow[start:start + per_device, :].astype(jnp.float32)
                else:
                    rows = jnp.full((per_device, narrow.shape[1]), 7.0 - i, jnp.float32)
                for half in range(2):
                    at = pl.ds(src * per_device * 8 + i, per_device, stride=8)
                    wide[half, at, :] = rows[:, half * 128:(half + 1) * 128]

    placement(row_ids, col_ids, place)
    row_span = per_device * row_ids.shape[0]
    row_base = lax.axis_index("row") * row_span
    out_first[...] = jnp.zeros_like(out_first)
    out_second[...] = jnp.zeros_like(out_second)
    panels = row_tiles.shape[1]
    count = live[0]
    eps_sq = REG_EPS * REG_EPS
    across = (((1,), (1,)), ((), ()))
    down = (((1,), (0,)), ((), ()))

    sub = lax.broadcasted_iota(jnp.int32, (8, panels), 0)
    ones = jnp.ones((1, panels), jnp.float32)

    def prepare(tile):
        products = [tile * tile[3 + i:4 + i, :] for i in range(3)]
        y_f = products[0][0:1] + products[1][1:2] + products[2][2:3]
        y_y = products[0][3:4] + products[1][4:5] + products[2][5:6]
        blocks = [tile]
        for product in products:
            high = product.astype(jnp.bfloat16).astype(jnp.float32)
            blocks += [high, product - high]
        blocks += split(tile * y_f)
        return jnp.concatenate(blocks, axis=0).astype(jnp.bfloat16), y_y

    def distances(ta, tb, xx, yy, u):
        x_high, x_mid, x_low = split(xx)
        y_high, y_mid, y_low = split(yy + eps_sq)
        left0 = jnp.where(sub == 0, x_high, jnp.where(sub == 1, x_mid, jnp.where(sub == 2, x_low, jnp.where(
            sub < 6, -2.0 * ta, ta))))
        right0 = jnp.where(sub < 3, ones, jnp.where(sub == 6, y_high, tb))
        left1 = jnp.where(sub < 2, ones, 0.0)
        right1 = jnp.where(sub == 0, y_mid, jnp.where(sub == 1, y_low, 0.0))
        left = jnp.concatenate([left0, left1], axis=0).T.astype(jnp.bfloat16)
        right = jnp.concatenate([right0, right1], axis=0).astype(jnp.bfloat16)
        radius_sq[u] = jnp.dot(left, right, preferred_element_type=jnp.float32)

    def combine(near_inv, near_cube, tile):
        x = tile[3:6]
        s = near_cube[0:3]
        value = near_inv[0:3] + eps_sq * s
        last = near_cube[56:64] + near_cube[64:72] + near_cube[72:80]
        dotted = jnp.sum(x * s, axis=0, keepdims=True) - last[6:7]
        value = value + (x * dotted + last[3:6])
        cross = [jnp.sum(x * (near_cube[8 + 16 * i:11 + 16 * i] + near_cube[16 + 16 * i:19 + 16 * i]), axis=0,
                         keepdims=True) for i in range(3)]
        return [(value[i:i + 1] - cross[i]) * STOKES_SCALE for i in range(3)]

    def fetch(wide, local):
        at = pl.ds(pl.multiple_of(local * 8, 8), 8)
        return jnp.concatenate([wide[0, at, :], wide[1, at, :]], axis=1)

    def begin(slot, u):
        b = pairs[1, slot]
        ta = fetch(row_wide, pairs[0, slot] - row_base)
        tb = fetch(col_wide, b // row_span * per_device + b % per_device)
        ra, xx = prepare(ta)
        rb, yy = prepare(tb)
        distances(ta, tb, xx, yy, u)
        return ta, tb, ra, rb

    def finish(slot, u, ta, tb, ra, rb):
        for chunk in range(panels // CHUNK):
            at = slice(chunk * CHUNK, (chunk + 1) * CHUNK)
            inv_dist = lax.rsqrt(radius_sq[u, at, :])
            inv[u, at, :] = inv_dist.astype(jnp.bfloat16)
            cube[u, at, :] = (inv_dist * inv_dist * inv_dist).astype(jnp.bfloat16)
        product = functools.partial(lax.dot_general, preferred_element_type=jnp.float32)
        to_first = combine(product(rb[0:16], inv[u], across), product(rb, cube[u], across), ta)
        to_second = combine(product(ra[0:16], inv[u], down), product(ra, cube[u], down), tb)
        within = slot < count
        keep_second = within & (pairs[0, slot] != pairs[1, slot])
        for i in range(3):
            at = slice(i * panels, (i + 1) * panels)
            out_first[pl.ds(slot, 1), at] = jnp.where(within, to_first[i], 0.0)
            out_second[pl.ds(slot, 1), at] = jnp.where(keep_second, to_second[i], 0.0)

    def group(step, carry):
        held = begin(step * GROUP, 0)
        for u in range(GROUP):
            ahead = begin(step * GROUP + u + 1, u + 1) if u + 1 < GROUP else None
            finish(step * GROUP + u, u, *held)
            held = ahead
        return carry

    lax.fori_loop(0, (count + GROUP - 1) // GROUP, group, 0)
    for out, sent in ((out_first, sent_first), (out_second, sent_second)):
        size = sent.shape[1]
        for k in range(sent.shape[0]):
            sent[k] = out[k * size:(k + 1) * size, :].astype(sent.dtype)


def near(per_device, pairs, live, row_tiles, col_tiles, row_ids, col_ids):
    slots, panels = pairs.shape[1], row_tiles.shape[1]
    n_col, n_row = row_ids.shape[0], col_ids.shape[0]
    smem = pl.BlockSpec(memory_space=pltpu.SMEM)
    vmem = pl.BlockSpec(memory_space=pltpu.VMEM)
    shape = jax.ShapeDtypeStruct
    return pl.pallas_call(
        functools.partial(near_kernel, per_device),
        out_shape=[shape((n_col, slots // n_col, 3 * panels), jnp.bfloat16),
                   shape((n_row, slots // n_row, 3 * panels), jnp.float32),
                   shape((per_device, 2 * slots), jnp.bfloat16)],
        in_specs=[smem, smem] + [vmem] * 4,
        out_specs=[vmem] * 3,
        scratch_shapes=[pltpu.VMEM((slots, 3 * panels), jnp.float32)] * 2 + [
            pltpu.VMEM((2, row_tiles.shape[0] // 6 * 8, 128), jnp.float32),
            pltpu.VMEM((2, col_tiles.shape[0] // 6 * 8, 128), jnp.float32),
            pltpu.VMEM((GROUP, panels, panels), jnp.float32),
        ] + [pltpu.VMEM((GROUP, panels, panels), jnp.bfloat16)] * 2,
        compiler_params=pltpu.CompilerParams(vmem_limit_bytes=48 * 1024 * 1024),
        name="near",
    )(pairs, live, row_tiles, col_tiles, row_ids, col_ids)


def exchange_kernel(n_row, n_col, parent, out_first, out_second, total, place, transfer, basis, velocity,
                    got_first, got_second, parts, coef, far_part, transfer_in, basis_in, own_sem, sa, ra, sb, rb):
    row, col = lax.axis_index("row"), lax.axis_index("col")
    own = [
        pltpu.make_async_copy(out_first.at[col], got_first.at[col], own_sem.at[0]),
        pltpu.make_async_copy(out_second.at[row], got_second.at[row], own_sem.at[1]),
        pltpu.make_async_copy(transfer, transfer_in, own_sem.at[2]),
        pltpu.make_async_copy(basis, basis_in, own_sem.at[3]),
    ]
    greet(n_row, n_col, row, col)
    for copy in own:
        copy.start()
    meet(n_row, n_col)
    started = []

    def send(src, dst, sends, recvs, slot, mine, device):
        copy = pltpu.make_async_remote_copy(
            src_ref=src, dst_ref=dst, send_sem=sends.at[slot], recv_sem=recvs.at[mine],
            device_id=device, device_id_type=MESH)
        copy.start()
        started.append(copy)

    for k in range(1, n_col):
        peer = lax.rem(col + k, n_col)
        send(out_first.at[peer], got_first.at[col], sa, ra, peer, col, (row, peer))
    for k in range(1, n_row):
        peer = lax.rem(row + k, n_row)
        send(out_second.at[peer], got_second.at[row], sb, rb, peer, row, (peer, col))
    for copy in own:
        copy.wait()

    per_device, rank = parts.shape
    base = (row * n_col + col) * per_device
    for c in range(per_device):
        parts[c:c + 1, :] = total[pl.ds(parent[base + c], 1), :]
    turned = parts[...].T
    for c in range(per_device):
        coef[c:c + 1, :] = jnp.sum(transfer_in[c] * turned[:, c:c + 1], axis=0, keepdims=True)
    turned = coef[...].T
    for c in range(per_device):
        far_part[c:c + 1, :] = jnp.sum(basis_in[c].astype(jnp.float32) * turned[:, c:c + 1], axis=0, keepdims=True)

    for k in range(1, n_row):
        src = lax.rem(row + k, n_row)
        view = got_second.at[src]
        pltpu.make_async_copy(view, view, rb.at[src]).wait()
    for k in range(1, n_col):
        src = lax.rem(col + k, n_col)
        view = got_first.at[src]
        pltpu.make_async_copy(view, view, ra.at[src]).wait()
    slots = place.shape[1] // 2
    first = got_first[...].astype(jnp.float32).reshape(slots, got_first.shape[2]).astype(jnp.bfloat16)
    second = got_second[...].reshape(slots, got_second.shape[2])
    velocity[...] = (far_part[...] + jnp.dot(place[:, :slots], first, preferred_element_type=jnp.float32)
                     + select_rows(place[:, slots:], second))
    for copy in started:
        copy.wait_send()


def exchange(n_row, n_col, parent, out_first, out_second, total, place, transfer, basis):
    smem = pl.BlockSpec(memory_space=pltpu.SMEM)
    vmem = pl.BlockSpec(memory_space=pltpu.VMEM)
    any_space = pl.BlockSpec(memory_space=pl.ANY)
    per_device, width, rank = place.shape[0], out_first.shape[2], total.shape[1]
    return pl.pallas_call(
        functools.partial(exchange_kernel, n_row, n_col),
        out_shape=jax.ShapeDtypeStruct((per_device, width), jnp.float32),
        in_specs=[smem] + [vmem] * 4 + [any_space] * 2,
        out_specs=vmem,
        scratch_shapes=[
            pltpu.VMEM(out_first.shape, out_first.dtype), pltpu.VMEM(out_second.shape, out_second.dtype),
            pltpu.VMEM((per_device, rank), jnp.float32), pltpu.VMEM((per_device, rank), jnp.float32),
            pltpu.VMEM((per_device, width), jnp.float32), pltpu.VMEM(transfer.shape, transfer.dtype),
            pltpu.VMEM(basis.shape, basis.dtype),
        ] + [pltpu.SemaphoreType.DMA((size,)) for size in (4, n_col, n_col, n_row, n_row)],
        compiler_params=pltpu.CompilerParams(
            collective_id=2, has_side_effects=True, vmem_limit_bytes=32 * 1024 * 1024),
        name="exchange",
    )(parent, out_first, out_second, total, place, transfer, basis)


def shards(density, coords, basis, transfer, parent, near_pairs, near_count, far_pairs, coupling):
    per_device, _, panels = density.shape
    n_row, n_col = lax.axis_size("row"), lax.axis_size("col")
    tile = jnp.concatenate([density, coords], axis=1).transpose(1, 0, 2).reshape(6 * per_device, panels)
    row_tiles, col_tiles, row_ids, col_ids, total = gather(
        n_row, n_col, tile, near_pairs, far_pairs, parent.reshape(1, -1), basis, transfer, coupling)
    out_first, out_second, place = near(
        per_device, near_pairs, near_count, row_tiles, col_tiles, row_ids, col_ids)
    velocity = exchange(n_row, n_col, parent, out_first, out_second, total, place, transfer, basis)
    return velocity.reshape(per_device, 3, panels)


def solution(mesh):
    placed = (
        P(("row", "col"), None, None),
        P(("row", "col"), None, None),
        P(("row", "col"), None, None),
        P(("row", "col"), None, None),
        P(),
        P(None, ("row", "col")),
        P(("row", "col")),
        P(None, ("row", "col")),
        P(("row", "col"), None, None),
    )
    return jax.shard_map(
        shards, mesh=mesh, in_specs=placed, out_specs=P(("row", "col"), None, None), check_vma=False
    )
```

```python
import functools
import math

import jax
import jax.numpy as jnp
from jax import lax
from jax.experimental import pallas as pl
from jax.experimental.pallas import tpu as pltpu
from jax.sharding import PartitionSpec as P

REG_EPS = 0.02
STOKES_SCALE = 1.0 / (8.0 * math.pi)
MESH = pl.DeviceIdType.MESH
GROUP = 4
CHUNK = 16


def greet(n_row, n_col, row, col):
    barrier = pltpu.get_barrier_semaphore()
    for k in range(1, n_col):
        pl.semaphore_signal(barrier, inc=1, device_id=(row, lax.rem(col + k, n_col)), device_id_type=MESH)
    for k in range(1, n_row):
        pl.semaphore_signal(barrier, inc=1, device_id=(lax.rem(row + k, n_row), col), device_id_type=MESH)


def meet(n_row, n_col):
    pl.semaphore_wait(pltpu.get_barrier_semaphore(), n_col + n_row - 2)


def part(ref, index, size):
    return ref.at[pl.ds(pl.multiple_of(index * size, size), size)]


def split(wide, terms=3):
    out = []
    for _ in range(terms - 1):
        term = wide.astype(jnp.bfloat16).astype(jnp.float32)
        out.append(term)
        wide = wide - term
    return out + [wide]


def select_rows(one_hot, wide):
    return sum(jnp.dot(one_hot, term.astype(jnp.bfloat16), preferred_element_type=jnp.float32)
               for term in split(wide))


def as_one_hot(where_true):
    return jnp.where(where_true, 1.0, 0.0).astype(jnp.bfloat16)


def couple(far, coupling, parents, all_lifted, lifted, moved, own_locals):
    rank, total = moved.shape[1], parents.shape[1] // 4
    pairs = far.shape[1]
    for u in range(4):
        turned = pltpu.roll(all_lifted[...], (4 - u) % 4 * rank, 1)
        lifted[:, u] = turned.reshape(lifted.shape[0], lifted.shape[2], 4 * rank)
    clusters = parents.shape[1]
    parent_row = lax.broadcasted_iota(jnp.int32, (total, 1), 0)
    moments = select_rows(as_one_hot(parent_row == parents[...]), lifted[...].reshape(clusters, 4 * rank)[:, :rank])
    lane = lax.broadcasted_iota(jnp.int32, (pairs, total), 1).astype(jnp.float32)
    sources = []
    for side in range(2):
        column = jnp.broadcast_to(far[side:side + 1, :].astype(jnp.float32), (8, pairs)).T[:, 0:1]
        sources.append(select_rows(as_one_hot(lane == column), moments))
    turned = sources[0].T
    pair_lane = lax.broadcasted_iota(jnp.int32, (rank, pairs), 1)
    to_first = jnp.zeros((rank, pairs), jnp.float32)
    for k in range(pairs):
        block = coupling[k]
        to_first = jnp.where(pair_lane == k, jnp.sum(block * sources[1][k:k + 1], axis=1, keepdims=True), to_first)
        moved[k:k + 1, :] = jnp.sum(block * turned[:, k:k + 1], axis=0, keepdims=True)
    value = (select_rows(as_one_hot(parent_row == far[0:1, :]), to_first.T)
             + select_rows(as_one_hot(parent_row == far[1:2, :]), moved[...]))
    group = own_locals.shape[0]
    own_locals[...] = jnp.concatenate([value[u * group:(u + 1) * group] for u in range(4)], axis=1)


def lift(tile, basis, transfer, lifted):
    per_device, rank, width = basis.shape
    panels = width // 3
    source = tile[...].astype(jnp.float32)
    lane = lax.broadcasted_iota(jnp.int32, (rank, per_device), 1)
    turned = jnp.zeros((rank, per_device), jnp.float32)
    for c in range(per_device):
        total = sum(basis[c, :, i * panels:(i + 1) * panels].astype(jnp.float32)
                    * source[i * per_device + c:i * per_device + c + 1] for i in range(3))
        turned = jnp.where(lane == c, jnp.sum(total, axis=1, keepdims=True), turned)
    moments = turned.T
    turned = jnp.zeros((rank, per_device), jnp.float32)
    for c in range(per_device):
        total = jnp.sum(transfer[c] * moments[c:c + 1], axis=1, keepdims=True)
        turned = jnp.where(lane == c, total, turned)
    value = turned.T
    group = per_device // 4
    lifted[...] = jnp.concatenate([value[u * group:(u + 1) * group] for u in range(4)], axis=1)


def gather_kernel(n_row, n_col, n_z, tile, ids, far, parents, basis, transfer, coupling,
                  row_tiles, col_tiles, row_ids, col_ids, reduced,
                  basis_in, transfer_in, coupling_in, lifted, all_lifted, natural, moved, partial, f1, f2, acc,
                  own_sem, in_sem, st, rt, sct, rct, si, ri, sci, rci, sl, rl, scl, rcl, s1, r1, s2, r2):
    row, col = lax.axis_index("row"), lax.axis_index("col")
    n_y = n_col // n_z
    z, y = col // n_y, lax.rem(col, n_y)
    rows, lift_rows = tile.shape[0], lifted.shape[0]
    piece = partial.shape[0] // n_col
    span = n_col * lift_rows
    loads = [
        pltpu.make_async_copy(basis, basis_in, in_sem.at[0]),
        pltpu.make_async_copy(transfer, transfer_in, in_sem.at[1]),
        pltpu.make_async_copy(coupling, coupling_in, in_sem.at[2]),
    ]
    for copy in loads:
        copy.start()
    greet(n_row, n_col, row, col)
    own = [
        pltpu.make_async_copy(tile, part(row_tiles, col, rows), own_sem.at[0]),
        pltpu.make_async_copy(tile, part(col_tiles, row, rows), own_sem.at[1]),
        pltpu.make_async_copy(ids, row_ids.at[col], own_sem.at[2]),
        pltpu.make_async_copy(ids, col_ids.at[row], own_sem.at[3]),
    ]
    for copy in own:
        copy.start()
    loads[0].wait()
    loads[1].wait()
    lift(tile, basis_in, transfer_in, lifted)
    mine = pltpu.make_async_copy(lifted, part(all_lifted, row * n_col + col, lift_rows), own_sem.at[4])
    mine.start()
    meet(n_row, n_col)
    started = []

    def send(src, dst, sends, slot, recvs, index, device):
        copy = pltpu.make_async_remote_copy(
            src_ref=src, dst_ref=dst, send_sem=sends.at[slot], recv_sem=recvs.at[index],
            device_id=device, device_id_type=MESH)
        copy.start()
        started.append(copy)

    def arrive(view, sem):
        pltpu.make_async_copy(view, view, sem).wait()

    col_peers = [lax.rem(col + k, n_col) for k in range(1, n_col)]
    row_peers = [lax.rem(row + k, n_row) for k in range(1, n_row)]

    def forward(k):
        src = lax.rem(z + k, n_z) * n_y + y
        view = part(row_tiles, src, rows)
        arrive(view, rt.at[src])
        for j in range(1, n_y):
            send(view, view, st, n_z + n_y * k + j, rt, src, (row, z * n_y + lax.rem(y + j, n_y)))

    for peer in col_peers:
        send(lifted, part(all_lifted, row * n_col + col, lift_rows), sl, peer, rl, col, (row, peer))
    for k in range(1, n_z):
        send(tile, part(row_tiles, col, rows), st, k, rt, col, (row, lax.rem(z + k, n_z) * n_y + y))
    for k in range(1, n_y):
        send(tile, part(row_tiles, col, rows), st, n_z + k, rt, col, (row, z * n_y + lax.rem(y + k, n_y)))
    for peer in row_peers:
        send(tile, part(col_tiles, row, rows), sct, peer, rct, row, (peer, col))
        send(ids, col_ids.at[row], sci, peer, rci, row, (peer, col))
    for peer in col_peers:
        send(ids, row_ids.at[col], si, peer, ri, col, (row, peer))

    mine.wait()
    for src in col_peers:
        arrive(part(all_lifted, row * n_col + src, lift_rows), rl.at[src])
    for peer in row_peers:
        send(part(all_lifted, row, span), part(all_lifted, row, span), scl, peer, rcl, row, (peer, col))
    loads[2].wait()
    for src in row_peers:
        arrive(part(all_lifted, src, span), rcl.at[src])
    couple(far, coupling_in, parents, all_lifted, natural, moved, partial)
    f1[pl.ds(col, 1)] = partial[pl.ds(pl.multiple_of(col * piece, piece), piece), :][None]
    for peer in col_peers:
        send(part(partial, peer, piece), f1.at[col], s1, peer, r1, col, (row, peer))
    for k in range(1, n_z):
        forward(k)

    for src in col_peers:
        arrive(f1.at[src], r1.at[src])
    acc[...] = jnp.sum(f1[...], axis=0)
    f2[pl.ds(row, 1)] = acc[...][None]
    for peer in row_peers:
        send(acc, f2.at[row], s2, peer, r2, row, (peer, col))
    for src in row_peers:
        arrive(f2.at[src], r2.at[src])
    reduced[...] = jnp.sum(f2[...], axis=0)

    for j in range(1, n_y):
        for k in range(n_z):
            src = lax.rem(z + k, n_z) * n_y + lax.rem(y + j, n_y)
            arrive(part(row_tiles, src, rows), rt.at[src])
    for src in col_peers:
        arrive(row_ids.at[src], ri.at[src])
    for src in row_peers:
        arrive(part(col_tiles, src, rows), rct.at[src])
        arrive(col_ids.at[src], rci.at[src])
    for copy in own:
        copy.wait()
    for copy in started:
        copy.wait_send()


def gather(n_row, n_col, tile, ids, far, parents, basis, transfer, coupling):
    n_z = 4 if n_col % 4 == 0 else 1
    vmem = pl.BlockSpec(memory_space=pltpu.VMEM)
    any_space = pl.BlockSpec(memory_space=pl.ANY)
    per_device, rank = basis.shape[:2]
    clusters, parent_total = parents.shape[1], parents.shape[1] // 4
    piece = parent_total // 4 // n_col
    steps = n_z * (n_col // n_z + 1) + n_col
    sizes = [6, 3, steps, n_col, n_row, n_row, n_col, n_col, n_row, n_row, n_col, n_col, n_row, n_row,
             n_col, n_col, n_row, n_row]
    shape = jax.ShapeDtypeStruct
    group = per_device // 4
    buffers = [transfer.shape, coupling.shape, (group, 4 * rank), (clusters // 4, 4 * rank),
               (clusters // per_device, 4, group, 4 * rank), (coupling.shape[0], rank),
               (parent_total // 4, 4 * rank), (n_col, piece, 4 * rank), (n_row, piece, 4 * rank), (piece, 4 * rank)]
    return pl.pallas_call(
        functools.partial(gather_kernel, n_row, n_col, n_z),
        out_shape=[
            shape((n_col * tile.shape[0], tile.shape[1]), tile.dtype),
            shape((n_row * tile.shape[0], tile.shape[1]), tile.dtype),
            shape((n_col,) + ids.shape, ids.dtype),
            shape((n_row,) + ids.shape, ids.dtype),
            shape((piece, 4 * rank), jnp.float32),
        ],
        in_specs=[vmem] * 4 + [any_space] * 3,
        out_specs=[vmem] * 5,
        scratch_shapes=[pltpu.VMEM(basis.shape, basis.dtype)] + [pltpu.VMEM(size, jnp.float32) for size in buffers]
        + [pltpu.SemaphoreType.DMA((size,)) for size in sizes],
        compiler_params=pltpu.CompilerParams(
            collective_id=1, has_side_effects=True, vmem_limit_bytes=32 * 1024 * 1024),
        name="gather",
    )(tile, ids, far, parents, basis, transfer, coupling)


def placement(row_ids, col_ids, place):
    per_device, slots = place.shape[0], row_ids.shape[2]
    n_row, n_col = col_ids.shape[0], row_ids.shape[0]
    row, col = lax.axis_index("row"), lax.axis_index("col")
    base = (row * n_col + col) * per_device
    lane = lax.broadcasted_iota(jnp.int32, (8, slots), 1)
    cluster = lax.broadcasted_iota(jnp.int32, (per_device, slots), 0) + base
    for ids, side, sources, mine, start in ((row_ids, 0, n_col, col, 0), (col_ids, 1, n_row, row, slots)):
        size = slots // sources
        owners = jnp.zeros((8, slots), jnp.int32)
        for src in range(sources):
            from_src = jnp.broadcast_to(ids[src, side:side + 1, :], (8, slots))
            shift = lax.rem((src - mine) * size + slots, slots)
            owners = jnp.where(lane // size == src, pltpu.roll(from_src, shift, 1), owners)
        place[:, start:start + slots] = as_one_hot(cluster == owners[0:1, :])


def near_kernel(per_device, pairs, live, row_tiles, col_tiles, row_ids, col_ids,
                sent_first, sent_second, place, out_first, out_second, row_wide, col_wide, radius_sq, inv, cube):
    for narrow, wide in ((row_tiles, row_wide), (col_tiles, col_wide)):
        for src in range(narrow.shape[0] // (6 * per_device)):
            for i in range(8):
                if i < 6:
                    start = (src * 6 + i) * per_device
                    rows = narrow[start:start + per_device, :].astype(jnp.float32)
                else:
                    rows = jnp.full((per_device, narrow.shape[1]), 7.0 - i, jnp.float32)
                for half in range(2):
                    at = pl.ds(src * per_device * 8 + i, per_device, stride=8)
                    wide[half, at, :] = rows[:, half * 128:(half + 1) * 128]

    placement(row_ids, col_ids, place)
    row_span = per_device * row_ids.shape[0]
    row_base = lax.axis_index("row") * row_span
    out_first[...] = jnp.zeros_like(out_first)
    out_second[...] = jnp.zeros_like(out_second)
    panels = row_tiles.shape[1]
    count = live[0]
    eps_sq = REG_EPS * REG_EPS
    across = (((1,), (1,)), ((), ()))
    down = (((1,), (0,)), ((), ()))

    sub = lax.broadcasted_iota(jnp.int32, (8, panels), 0)
    ones = jnp.ones((1, panels), jnp.float32)

    def prepare(tile):
        products = [tile * tile[3 + i:4 + i, :] for i in range(3)]
        y_f = products[0][0:1] + products[1][1:2] + products[2][2:3]
        y_y = products[0][3:4] + products[1][4:5] + products[2][5:6]
        blocks = [tile]
        for product in products:
            high = product.astype(jnp.bfloat16).astype(jnp.float32)
            blocks += [high, product - high]
        blocks += split(tile * y_f)
        return jnp.concatenate(blocks, axis=0).astype(jnp.bfloat16), y_y

    def distances(ta, tb, xx, yy, u):
        x_high, x_mid, x_low = split(xx)
        y_high, y_mid, y_low = split(yy + eps_sq)
        left0 = jnp.where(sub == 0, x_high, jnp.where(sub == 1, x_mid, jnp.where(sub == 2, x_low, jnp.where(
            sub < 6, -2.0 * ta, ta))))
        right0 = jnp.where(sub < 3, ones, jnp.where(sub == 6, y_high, tb))
        left1 = jnp.where(sub < 2, ones, 0.0)
        right1 = jnp.where(sub == 0, y_mid, jnp.where(sub == 1, y_low, 0.0))
        left = jnp.concatenate([left0, left1], axis=0).T.astype(jnp.bfloat16)
        right = jnp.concatenate([right0, right1], axis=0).astype(jnp.bfloat16)
        radius_sq[u] = jnp.dot(left, right, preferred_element_type=jnp.float32)

    def combine(near_inv, near_cube, tile):
        x = tile[3:6]
        s = near_cube[0:3]
        value = near_inv[0:3] + eps_sq * s
        last = near_cube[56:64] + near_cube[64:72] + near_cube[72:80]
        dotted = jnp.sum(x * s, axis=0, keepdims=True) - last[6:7]
        value = value + (x * dotted + last[3:6])
        cross = [jnp.sum(x * (near_cube[8 + 16 * i:11 + 16 * i] + near_cube[16 + 16 * i:19 + 16 * i]), axis=0,
                         keepdims=True) for i in range(3)]
        return [(value[i:i + 1] - cross[i]) * STOKES_SCALE for i in range(3)]

    def fetch(wide, local):
        at = pl.ds(pl.multiple_of(local * 8, 8), 8)
        return jnp.concatenate([wide[0, at, :], wide[1, at, :]], axis=1)

    def begin(slot, u):
        b = pairs[1, slot]
        ta = fetch(row_wide, pairs[0, slot] - row_base)
        tb = fetch(col_wide, b // row_span * per_device + b % per_device)
        ra, xx = prepare(ta)
        rb, yy = prepare(tb)
        distances(ta, tb, xx, yy, u)
        return ta, tb, ra, rb

    def finish(slot, u, ta, tb, ra, rb):
        for chunk in range(panels // CHUNK):
            at = slice(chunk * CHUNK, (chunk + 1) * CHUNK)
            inv_dist = lax.rsqrt(radius_sq[u, at, :])
            inv[u, at, :] = inv_dist.astype(jnp.bfloat16)
            cube[u, at, :] = (inv_dist * inv_dist * inv_dist).astype(jnp.bfloat16)
        product = functools.partial(lax.dot_general, preferred_element_type=jnp.float32)
        to_first = combine(product(rb[0:16], inv[u], across), product(rb, cube[u], across), ta)
        to_second = combine(product(ra[0:16], inv[u], down), product(ra, cube[u], down), tb)
        within = slot < count
        keep_second = within & (pairs[0, slot] != pairs[1, slot])
        for i in range(3):
            at = slice(i * panels, (i + 1) * panels)
            out_first[pl.ds(slot, 1), at] = jnp.where(within, to_first[i], 0.0)
            out_second[pl.ds(slot, 1), at] = jnp.where(keep_second, to_second[i], 0.0)

    def group(step, carry):
        held = begin(step * GROUP, 0)
        for u in range(GROUP):
            ahead = begin(step * GROUP + u + 1, u + 1) if u + 1 < GROUP else None
            finish(step * GROUP + u, u, *held)
            held = ahead
        return carry

    lax.fori_loop(0, (count + GROUP - 1) // GROUP, group, 0)
    for out, sent in ((out_first, sent_first), (out_second, sent_second)):
        size = sent.shape[1]
        for k in range(sent.shape[0]):
            sent[k] = out[k * size:(k + 1) * size, :].astype(sent.dtype)


def near(per_device, pairs, live, row_tiles, col_tiles, row_ids, col_ids):
    slots, panels = pairs.shape[1], row_tiles.shape[1]
    n_col, n_row = row_ids.shape[0], col_ids.shape[0]
    smem = pl.BlockSpec(memory_space=pltpu.SMEM)
    vmem = pl.BlockSpec(memory_space=pltpu.VMEM)
    shape = jax.ShapeDtypeStruct
    return pl.pallas_call(
        functools.partial(near_kernel, per_device),
        out_shape=[shape((n_col, slots // n_col, 3 * panels), jnp.bfloat16),
                   shape((n_row, slots // n_row, 3 * panels), jnp.float32),
                   shape((per_device, 2 * slots), jnp.bfloat16)],
        in_specs=[smem, smem] + [vmem] * 4,
        out_specs=[vmem] * 3,
        scratch_shapes=[pltpu.VMEM((slots, 3 * panels), jnp.float32)] * 2 + [
            pltpu.VMEM((2, row_tiles.shape[0] // 6 * 8, 128), jnp.float32),
            pltpu.VMEM((2, col_tiles.shape[0] // 6 * 8, 128), jnp.float32),
            pltpu.VMEM((GROUP, panels, panels), jnp.float32),
        ] + [pltpu.VMEM((GROUP, panels, panels), jnp.bfloat16)] * 2,
        compiler_params=pltpu.CompilerParams(vmem_limit_bytes=48 * 1024 * 1024),
        name="near",
    )(pairs, live, row_tiles, col_tiles, row_ids, col_ids)


def exchange_kernel(n_row, n_col, parent, out_first, out_second, reduced, place, transfer, basis, velocity,
                    got_first, got_second, total, parts, coef, far_part, transfer_in, basis_in, own_sem, sa, ra, sb, rb, s3, r3):
    row, col = lax.axis_index("row"), lax.axis_index("col")
    own = [
        pltpu.make_async_copy(out_first.at[col], got_first.at[col], own_sem.at[0]),
        pltpu.make_async_copy(out_second.at[row], got_second.at[row], own_sem.at[1]),
        pltpu.make_async_copy(transfer, transfer_in, own_sem.at[2]),
        pltpu.make_async_copy(basis, basis_in, own_sem.at[3]),
        pltpu.make_async_copy(reduced, total.at[col], own_sem.at[4]),
    ]
    greet(n_row, n_col, row, col)
    for copy in own:
        copy.start()
    meet(n_row, n_col)
    started = []

    def send(src, dst, sends, recvs, slot, mine, device):
        copy = pltpu.make_async_remote_copy(
            src_ref=src, dst_ref=dst, send_sem=sends.at[slot], recv_sem=recvs.at[mine],
            device_id=device, device_id_type=MESH)
        copy.start()
        started.append(copy)

    for k in range(1, n_col):
        peer = lax.rem(col + k, n_col)
        send(reduced, total.at[col], s3, r3, peer, col, (row, peer))
    for k in range(1, n_col):
        peer = lax.rem(col + k, n_col)
        send(out_first.at[peer], got_first.at[col], sa, ra, peer, col, (row, peer))
    for k in range(1, n_row):
        peer = lax.rem(row + k, n_row)
        send(out_second.at[peer], got_second.at[row], sb, rb, peer, row, (peer, col))
    for copy in own:
        copy.wait()
    for k in range(1, n_col):
        src = lax.rem(col + k, n_col)
        pltpu.make_async_copy(total.at[src], total.at[src], r3.at[src]).wait()

    per_device, rank = coef.shape
    base = (row * n_col + col) * per_device
    piece, group = reduced.shape[0], reduced.shape[0] * n_col
    block = lax.broadcasted_iota(jnp.int32, (1, 4 * rank), 1) // rank
    for c in range(per_device):
        p = parent[base + c]
        q = lax.rem(p, group)
        found = total[q // piece, pl.ds(lax.rem(q, piece), 1), :]
        parts[c:c + 1, :] = jnp.where(block == p // group, found, 0.0)
    wide = parts[...]
    turned = sum(wide[:, u * rank:(u + 1) * rank] for u in range(4)).T
    for c in range(per_device):
        coef[c:c + 1, :] = jnp.sum(transfer_in[c] * turned[:, c:c + 1], axis=0, keepdims=True)
    turned = coef[...].T
    for c in range(per_device):
        far_part[c:c + 1, :] = jnp.sum(basis_in[c].astype(jnp.float32) * turned[:, c:c + 1], axis=0, keepdims=True)

    for k in range(1, n_row):
        src = lax.rem(row + k, n_row)
        view = got_second.at[src]
        pltpu.make_async_copy(view, view, rb.at[src]).wait()
    for k in range(1, n_col):
        src = lax.rem(col + k, n_col)
        view = got_first.at[src]
        pltpu.make_async_copy(view, view, ra.at[src]).wait()
    slots = place.shape[1] // 2
    first = got_first[...].astype(jnp.float32).reshape(slots, got_first.shape[2]).astype(jnp.bfloat16)
    second = got_second[...].reshape(slots, got_second.shape[2])
    velocity[...] = (far_part[...] + jnp.dot(place[:, :slots], first, preferred_element_type=jnp.float32)
                     + select_rows(place[:, slots:], second))
    for copy in started:
        copy.wait_send()


def exchange(n_row, n_col, parent, out_first, out_second, reduced, place, transfer, basis):
    smem = pl.BlockSpec(memory_space=pltpu.SMEM)
    vmem = pl.BlockSpec(memory_space=pltpu.VMEM)
    any_space = pl.BlockSpec(memory_space=pl.ANY)
    per_device, width, rank = place.shape[0], out_first.shape[2], transfer.shape[1]
    return pl.pallas_call(
        functools.partial(exchange_kernel, n_row, n_col),
        out_shape=jax.ShapeDtypeStruct((per_device, width), jnp.float32),
        in_specs=[smem] + [vmem] * 4 + [any_space] * 2,
        out_specs=vmem,
        scratch_shapes=[
            pltpu.VMEM(out_first.shape, out_first.dtype), pltpu.VMEM(out_second.shape, out_second.dtype),
            pltpu.VMEM((n_col,) + reduced.shape, jnp.float32), pltpu.VMEM((per_device, 4 * rank), jnp.float32),
            pltpu.VMEM((per_device, rank), jnp.float32),
            pltpu.VMEM((per_device, width), jnp.float32), pltpu.VMEM(transfer.shape, transfer.dtype),
            pltpu.VMEM(basis.shape, basis.dtype),
        ] + [pltpu.SemaphoreType.DMA((size,)) for size in (5, n_col, n_col, n_row, n_row, n_col, n_col)],
        compiler_params=pltpu.CompilerParams(
            collective_id=2, has_side_effects=True, vmem_limit_bytes=32 * 1024 * 1024),
        name="exchange",
    )(parent, out_first, out_second, reduced, place, transfer, basis)


def shards(density, coords, basis, transfer, parent, near_pairs, near_count, far_pairs, coupling):
    per_device, _, panels = density.shape
    n_row, n_col = lax.axis_size("row"), lax.axis_size("col")
    tile = jnp.concatenate([density, coords], axis=1).transpose(1, 0, 2).reshape(6 * per_device, panels)
    row_tiles, col_tiles, row_ids, col_ids, reduced = gather(
        n_row, n_col, tile, near_pairs, far_pairs, parent.reshape(1, -1), basis, transfer, coupling)
    out_first, out_second, place = near(
        per_device, near_pairs, near_count, row_tiles, col_tiles, row_ids, col_ids)
    velocity = exchange(n_row, n_col, parent, out_first, out_second, reduced, place, transfer, basis)
    return velocity.reshape(per_device, 3, panels)


def solution(mesh):
    placed = (
        P(("row", "col"), None, None),
        P(("row", "col"), None, None),
        P(("row", "col"), None, None),
        P(("row", "col"), None, None),
        P(),
        P(None, ("row", "col")),
        P(("row", "col")),
        P(None, ("row", "col")),
        P(("row", "col"), None, None),
    )
    return jax.shard_map(
        shards, mesh=mesh, in_specs=placed, out_specs=P(("row", "col"), None, None), check_vma=False
    )
```

```python
import functools
import math

import jax
import jax.numpy as jnp
from jax import lax
from jax.experimental import pallas as pl
from jax.experimental.pallas import tpu as pltpu
from jax.sharding import PartitionSpec as P

REG_EPS = 0.02
STOKES_SCALE = 1.0 / (8.0 * math.pi)
MESH = pl.DeviceIdType.MESH
GROUP = 4
CHUNK = 16


def greet(n_row, n_col, row, col):
    barrier = pltpu.get_barrier_semaphore()
    for k in range(1, n_col):
        pl.semaphore_signal(barrier, inc=1, device_id=(row, lax.rem(col + k, n_col)), device_id_type=MESH)
    for k in range(1, n_row):
        pl.semaphore_signal(barrier, inc=1, device_id=(lax.rem(row + k, n_row), col), device_id_type=MESH)


def meet(n_row, n_col):
    pl.semaphore_wait(pltpu.get_barrier_semaphore(), n_col + n_row - 2)


def part(ref, index, size):
    return ref.at[pl.ds(pl.multiple_of(index * size, size), size)]


def split(wide, terms=3):
    out = []
    for _ in range(terms - 1):
        term = wide.astype(jnp.bfloat16).astype(jnp.float32)
        out.append(term)
        wide = wide - term
    return out + [wide]


def select_rows(one_hot, wide):
    return sum(jnp.dot(one_hot, term.astype(jnp.bfloat16), preferred_element_type=jnp.float32)
               for term in split(wide))


def as_one_hot(where_true):
    return jnp.where(where_true, 1.0, 0.0).astype(jnp.bfloat16)


def couple(far, coupling, parents, all_lifted, lifted, moved, own_locals):
    rank, total = moved.shape[0], parents.shape[1] // 4
    pairs = far.shape[1]
    for u in range(4):
        turned = pltpu.roll(all_lifted[...], (4 - u) % 4 * rank, 1)
        lifted[:, u] = turned.reshape(lifted.shape[0], lifted.shape[2], 4 * rank)
    clusters = parents.shape[1]
    parent_row = lax.broadcasted_iota(jnp.int32, (total, 1), 0)
    moments = select_rows(as_one_hot(parent_row == parents[...]), lifted[...].reshape(clusters, 4 * rank)[:, :rank])
    lane = lax.broadcasted_iota(jnp.int32, (pairs, total), 1).astype(jnp.float32)
    sources = []
    for side in range(2):
        column = jnp.broadcast_to(far[side:side + 1, :].astype(jnp.float32), (8, pairs)).T[:, 0:1]
        sources.append(select_rows(as_one_hot(lane == column), moments))
    turned = [source.T for source in sources]
    to_second = jnp.zeros((rank, pairs), jnp.float32)
    for r in range(rank):
        block = coupling[r]
        moved[r:r + 1, :] = jnp.sum(block * turned[1], axis=0, keepdims=True)
        to_second = to_second + block * turned[0][r:r + 1]
    value = (select_rows(as_one_hot(parent_row == far[0:1, :]), moved[...].T)
             + select_rows(as_one_hot(parent_row == far[1:2, :]), to_second.T))
    group = own_locals.shape[0]
    own_locals[...] = jnp.concatenate([value[u * group:(u + 1) * group] for u in range(4)], axis=1)


def lift(tile, basis, transfer, lifted):
    per_device, rank, width = basis.shape
    panels = width // 3
    source = tile[...].astype(jnp.float32)
    lane = lax.broadcasted_iota(jnp.int32, (rank, per_device), 1)
    turned = jnp.zeros((rank, per_device), jnp.float32)
    for c in range(per_device):
        total = sum(basis[c, :, i * panels:(i + 1) * panels].astype(jnp.float32)
                    * source[i * per_device + c:i * per_device + c + 1] for i in range(3))
        turned = jnp.where(lane == c, jnp.sum(total, axis=1, keepdims=True), turned)
    moments = turned.T
    turned = jnp.zeros((rank, per_device), jnp.float32)
    for c in range(per_device):
        total = jnp.sum(transfer[c] * moments[c:c + 1], axis=1, keepdims=True)
        turned = jnp.where(lane == c, total, turned)
    value = turned.T
    group = per_device // 4
    lifted[...] = jnp.concatenate([value[u * group:(u + 1) * group] for u in range(4)], axis=1)


def gather_kernel(n_row, n_col, n_z, tile, ids, far, parents, basis, transfer, coupling,
                  row_tiles, col_tiles, row_ids, col_ids, reduced,
                  coupling_in, lifted, all_lifted, natural, moved, partial, f1, f2, acc,
                  own_sem, in_sem, st, rt, sct, rct, si, ri, sci, rci, sl, rl, scl, rcl, s1, r1, s2, r2):
    row, col = lax.axis_index("row"), lax.axis_index("col")
    n_y = n_col // n_z
    z, y = col // n_y, lax.rem(col, n_y)
    rows, lift_rows = tile.shape[0], lifted.shape[0]
    piece = partial.shape[0] // n_col
    span = n_col * lift_rows
    load = pltpu.make_async_copy(coupling, coupling_in, in_sem.at[0])
    load.start()
    greet(n_row, n_col, row, col)
    own = [
        pltpu.make_async_copy(tile, part(row_tiles, col, rows), own_sem.at[0]),
        pltpu.make_async_copy(tile, part(col_tiles, row, rows), own_sem.at[1]),
        pltpu.make_async_copy(ids, row_ids.at[col], own_sem.at[2]),
        pltpu.make_async_copy(ids, col_ids.at[row], own_sem.at[3]),
    ]
    for copy in own:
        copy.start()
    lift(tile, basis, transfer, lifted)
    mine = pltpu.make_async_copy(lifted, part(all_lifted, row * n_col + col, lift_rows), own_sem.at[4])
    mine.start()
    meet(n_row, n_col)
    started = []

    def send(src, dst, sends, slot, recvs, index, device):
        copy = pltpu.make_async_remote_copy(
            src_ref=src, dst_ref=dst, send_sem=sends.at[slot], recv_sem=recvs.at[index],
            device_id=device, device_id_type=MESH)
        copy.start()
        started.append(copy)

    def arrive(view, sem):
        pltpu.make_async_copy(view, view, sem).wait()

    col_peers = [lax.rem(col + k, n_col) for k in range(1, n_col)]
    row_peers = [lax.rem(row + k, n_row) for k in range(1, n_row)]

    def forward(k):
        src = lax.rem(z + k, n_z) * n_y + y
        view = part(row_tiles, src, rows)
        arrive(view, rt.at[src])
        for j in range(1, n_y):
            send(view, view, st, n_z + n_y * k + j, rt, src, (row, z * n_y + lax.rem(y + j, n_y)))

    for peer in col_peers:
        send(lifted, part(all_lifted, row * n_col + col, lift_rows), sl, peer, rl, col, (row, peer))
    for k in range(1, n_z):
        send(tile, part(row_tiles, col, rows), st, k, rt, col, (row, lax.rem(z + k, n_z) * n_y + y))
    for k in range(1, n_y):
        send(tile, part(row_tiles, col, rows), st, n_z + k, rt, col, (row, z * n_y + lax.rem(y + k, n_y)))
    for peer in row_peers:
        send(tile, part(col_tiles, row, rows), sct, peer, rct, row, (peer, col))
        send(ids, col_ids.at[row], sci, peer, rci, row, (peer, col))
    for peer in col_peers:
        send(ids, row_ids.at[col], si, peer, ri, col, (row, peer))

    mine.wait()
    for src in col_peers:
        arrive(part(all_lifted, row * n_col + src, lift_rows), rl.at[src])
    for peer in row_peers:
        send(part(all_lifted, row, span), part(all_lifted, row, span), scl, peer, rcl, row, (peer, col))
    load.wait()
    for src in row_peers:
        arrive(part(all_lifted, src, span), rcl.at[src])
    couple(far, coupling_in, parents, all_lifted, natural, moved, partial)
    f1[pl.ds(col, 1)] = partial[pl.ds(pl.multiple_of(col * piece, piece), piece), :][None]
    for peer in col_peers:
        send(part(partial, peer, piece), f1.at[col], s1, peer, r1, col, (row, peer))
    for k in range(1, n_z):
        forward(k)

    for src in col_peers:
        arrive(f1.at[src], r1.at[src])
    acc[...] = jnp.sum(f1[...], axis=0)
    f2[pl.ds(row, 1)] = acc[...][None]
    for peer in row_peers:
        send(acc, f2.at[row], s2, peer, r2, row, (peer, col))
    for src in row_peers:
        arrive(f2.at[src], r2.at[src])
    reduced[...] = jnp.sum(f2[...], axis=0)

    for j in range(1, n_y):
        for k in range(n_z):
            src = lax.rem(z + k, n_z) * n_y + lax.rem(y + j, n_y)
            arrive(part(row_tiles, src, rows), rt.at[src])
    for src in col_peers:
        arrive(row_ids.at[src], ri.at[src])
    for src in row_peers:
        arrive(part(col_tiles, src, rows), rct.at[src])
        arrive(col_ids.at[src], rci.at[src])
    for copy in own:
        copy.wait()
    for copy in started:
        copy.wait_send()


def gather(n_row, n_col, tile, ids, far, parents, basis, transfer, coupling):
    n_z = 4 if n_col % 4 == 0 else 1
    vmem = pl.BlockSpec(memory_space=pltpu.VMEM)
    any_space = pl.BlockSpec(memory_space=pl.ANY)
    per_device, rank = basis.shape[:2]
    clusters, parent_total = parents.shape[1], parents.shape[1] // 4
    piece = parent_total // 4 // n_col
    steps = n_z * (n_col // n_z + 1) + n_col
    sizes = [5, 1, steps, n_col, n_row, n_row, n_col, n_col, n_row, n_row, n_col, n_col, n_row, n_row,
             n_col, n_col, n_row, n_row]
    shape = jax.ShapeDtypeStruct
    group = per_device // 4
    buffers = [coupling.shape, (group, 4 * rank), (clusters // 4, 4 * rank),
               (clusters // per_device, 4, group, 4 * rank), (rank, coupling.shape[2]),
               (parent_total // 4, 4 * rank), (n_col, piece, 4 * rank), (n_row, piece, 4 * rank), (piece, 4 * rank)]
    return pl.pallas_call(
        functools.partial(gather_kernel, n_row, n_col, n_z),
        out_shape=[
            shape((n_col * tile.shape[0], tile.shape[1]), tile.dtype),
            shape((n_row * tile.shape[0], tile.shape[1]), tile.dtype),
            shape((n_col,) + ids.shape, ids.dtype),
            shape((n_row,) + ids.shape, ids.dtype),
            shape((piece, 4 * rank), jnp.float32),
        ],
        in_specs=[vmem] * 6 + [any_space],
        out_specs=[vmem] * 5,
        scratch_shapes=[pltpu.VMEM(size, jnp.float32) for size in buffers]
        + [pltpu.SemaphoreType.DMA((size,)) for size in sizes],
        compiler_params=pltpu.CompilerParams(
            collective_id=1, has_side_effects=True, vmem_limit_bytes=32 * 1024 * 1024),
        name="gather",
    )(tile, ids, far, parents, basis, transfer, coupling)


def placement(row_ids, col_ids, place):
    per_device, slots = place.shape[0], row_ids.shape[2]
    n_row, n_col = col_ids.shape[0], row_ids.shape[0]
    row, col = lax.axis_index("row"), lax.axis_index("col")
    base = (row * n_col + col) * per_device
    lane = lax.broadcasted_iota(jnp.int32, (8, slots), 1)
    cluster = lax.broadcasted_iota(jnp.int32, (per_device, slots), 0) + base
    for ids, side, sources, mine, start in ((row_ids, 0, n_col, col, 0), (col_ids, 1, n_row, row, slots)):
        size = slots // sources
        owners = jnp.zeros((8, slots), jnp.int32)
        for src in range(sources):
            from_src = jnp.broadcast_to(ids[src, side:side + 1, :], (8, slots))
            shift = lax.rem((src - mine) * size + slots, slots)
            owners = jnp.where(lane // size == src, pltpu.roll(from_src, shift, 1), owners)
        place[:, start:start + slots] = as_one_hot(cluster == owners[0:1, :])


def near_kernel(per_device, pairs, live, row_tiles, col_tiles, row_ids, col_ids,
                sent_first, sent_second, place, out_first, out_second, row_wide, col_wide, radius_sq, inv, cube):
    for narrow, wide in ((row_tiles, row_wide), (col_tiles, col_wide)):
        for src in range(narrow.shape[0] // (6 * per_device)):
            for i in range(8):
                if i < 6:
                    start = (src * 6 + i) * per_device
                    rows = narrow[start:start + per_device, :].astype(jnp.float32)
                else:
                    rows = jnp.full((per_device, narrow.shape[1]), 7.0 - i, jnp.float32)
                for half in range(2):
                    at = pl.ds(src * per_device * 8 + i, per_device, stride=8)
                    wide[half, at, :] = rows[:, half * 128:(half + 1) * 128]

    placement(row_ids, col_ids, place)
    row_span = per_device * row_ids.shape[0]
    row_base = lax.axis_index("row") * row_span
    out_first[...] = jnp.zeros_like(out_first)
    out_second[...] = jnp.zeros_like(out_second)
    panels = row_tiles.shape[1]
    count = live[0]
    eps_sq = REG_EPS * REG_EPS
    across = (((1,), (1,)), ((), ()))
    down = (((1,), (0,)), ((), ()))

    sub = lax.broadcasted_iota(jnp.int32, (8, panels), 0)
    ones = jnp.ones((1, panels), jnp.float32)

    def prepare(tile):
        products = [tile * tile[3 + i:4 + i, :] for i in range(3)]
        y_f = products[0][0:1] + products[1][1:2] + products[2][2:3]
        y_y = products[0][3:4] + products[1][4:5] + products[2][5:6]
        blocks = [tile]
        for product in products:
            high = product.astype(jnp.bfloat16).astype(jnp.float32)
            blocks += [high, product - high]
        blocks += split(tile * y_f)
        return jnp.concatenate(blocks, axis=0).astype(jnp.bfloat16), y_y

    def distances(ta, tb, xx, yy, u):
        x_high, x_mid, x_low = split(xx)
        y_high, y_mid, y_low = split(yy + eps_sq)
        left0 = jnp.where(sub == 0, x_high, jnp.where(sub == 1, x_mid, jnp.where(sub == 2, x_low, jnp.where(
            sub < 6, -2.0 * ta, ta))))
        right0 = jnp.where(sub < 3, ones, jnp.where(sub == 6, y_high, tb))
        left1 = jnp.where(sub < 2, ones, 0.0)
        right1 = jnp.where(sub == 0, y_mid, jnp.where(sub == 1, y_low, 0.0))
        left = jnp.concatenate([left0, left1], axis=0).T.astype(jnp.bfloat16)
        right = jnp.concatenate([right0, right1], axis=0).astype(jnp.bfloat16)
        radius_sq[u] = jnp.dot(left, right, preferred_element_type=jnp.float32)

    def combine(near_inv, near_cube, tile):
        x = tile[3:6]
        s = near_cube[0:3]
        value = near_inv[0:3] + eps_sq * s
        last = near_cube[56:64] + near_cube[64:72] + near_cube[72:80]
        dotted = jnp.sum(x * s, axis=0, keepdims=True) - last[6:7]
        value = value + (x * dotted + last[3:6])
        cross = [jnp.sum(x * (near_cube[8 + 16 * i:11 + 16 * i] + near_cube[16 + 16 * i:19 + 16 * i]), axis=0,
                         keepdims=True) for i in range(3)]
        return [(value[i:i + 1] - cross[i]) * STOKES_SCALE for i in range(3)]

    def fetch(wide, local):
        at = pl.ds(pl.multiple_of(local * 8, 8), 8)
        return jnp.concatenate([wide[0, at, :], wide[1, at, :]], axis=1)

    def begin(slot, u):
        b = pairs[1, slot]
        ta = fetch(row_wide, pairs[0, slot] - row_base)
        tb = fetch(col_wide, b // row_span * per_device + b % per_device)
        ra, xx = prepare(ta)
        rb, yy = prepare(tb)
        distances(ta, tb, xx, yy, u)
        return ta, tb, ra, rb

    def finish(slot, u, ta, tb, ra, rb):
        for chunk in range(panels // CHUNK):
            at = slice(chunk * CHUNK, (chunk + 1) * CHUNK)
            inv_dist = lax.rsqrt(radius_sq[u, at, :])
            inv[u, at, :] = inv_dist.astype(jnp.bfloat16)
            cube[u, at, :] = (inv_dist * inv_dist * inv_dist).astype(jnp.bfloat16)
        product = functools.partial(lax.dot_general, preferred_element_type=jnp.float32)
        to_first = combine(product(rb[0:16], inv[u], across), product(rb, cube[u], across), ta)
        to_second = combine(product(ra[0:16], inv[u], down), product(ra, cube[u], down), tb)
        within = slot < count
        keep_second = within & (pairs[0, slot] != pairs[1, slot])
        for i in range(3):
            at = slice(i * panels, (i + 1) * panels)
            out_first[pl.ds(slot, 1), at] = jnp.where(within, to_first[i], 0.0)
            out_second[pl.ds(slot, 1), at] = jnp.where(keep_second, to_second[i], 0.0)

    def group(step, carry):
        held = begin(step * GROUP, 0)
        for u in range(GROUP):
            ahead = begin(step * GROUP + u + 1, u + 1) if u + 1 < GROUP else None
            finish(step * GROUP + u, u, *held)
            held = ahead
        return carry

    lax.fori_loop(0, (count + GROUP - 1) // GROUP, group, 0)
    for out, sent in ((out_first, sent_first), (out_second, sent_second)):
        size = sent.shape[1]
        for k in range(sent.shape[0]):
            sent[k] = out[k * size:(k + 1) * size, :].astype(sent.dtype)


def near(per_device, pairs, live, row_tiles, col_tiles, row_ids, col_ids):
    slots, panels = pairs.shape[1], row_tiles.shape[1]
    n_col, n_row = row_ids.shape[0], col_ids.shape[0]
    smem = pl.BlockSpec(memory_space=pltpu.SMEM)
    vmem = pl.BlockSpec(memory_space=pltpu.VMEM)
    shape = jax.ShapeDtypeStruct
    return pl.pallas_call(
        functools.partial(near_kernel, per_device),
        out_shape=[shape((n_col, slots // n_col, 3 * panels), jnp.bfloat16),
                   shape((n_row, slots // n_row, 3 * panels), jnp.float32),
                   shape((per_device, 2 * slots), jnp.bfloat16)],
        in_specs=[smem, smem] + [vmem] * 4,
        out_specs=[vmem] * 3,
        scratch_shapes=[pltpu.VMEM((slots, 3 * panels), jnp.float32)] * 2 + [
            pltpu.VMEM((2, row_tiles.shape[0] // 6 * 8, 128), jnp.float32),
            pltpu.VMEM((2, col_tiles.shape[0] // 6 * 8, 128), jnp.float32),
            pltpu.VMEM((GROUP, panels, panels), jnp.float32),
        ] + [pltpu.VMEM((GROUP, panels, panels), jnp.bfloat16)] * 2,
        compiler_params=pltpu.CompilerParams(vmem_limit_bytes=48 * 1024 * 1024),
        name="near",
    )(pairs, live, row_tiles, col_tiles, row_ids, col_ids)


def exchange_kernel(n_row, n_col, parent, out_first, out_second, reduced, place, transfer, basis, velocity,
                    got_first, got_second, total, parts, coef, far_part, transfer_in, basis_in, own_sem, sa, ra, sb, rb, s3, r3):
    row, col = lax.axis_index("row"), lax.axis_index("col")
    own = [
        pltpu.make_async_copy(out_first.at[col], got_first.at[col], own_sem.at[0]),
        pltpu.make_async_copy(out_second.at[row], got_second.at[row], own_sem.at[1]),
        pltpu.make_async_copy(transfer, transfer_in, own_sem.at[2]),
        pltpu.make_async_copy(basis, basis_in, own_sem.at[3]),
        pltpu.make_async_copy(reduced, total.at[col], own_sem.at[4]),
    ]
    greet(n_row, n_col, row, col)
    for copy in own:
        copy.start()
    meet(n_row, n_col)
    started = []

    def send(src, dst, sends, recvs, slot, mine, device):
        copy = pltpu.make_async_remote_copy(
            src_ref=src, dst_ref=dst, send_sem=sends.at[slot], recv_sem=recvs.at[mine],
            device_id=device, device_id_type=MESH)
        copy.start()
        started.append(copy)

    for k in range(1, n_col):
        peer = lax.rem(col + k, n_col)
        send(reduced, total.at[col], s3, r3, peer, col, (row, peer))
    for k in range(1, n_col):
        peer = lax.rem(col + k, n_col)
        send(out_first.at[peer], got_first.at[col], sa, ra, peer, col, (row, peer))
    for k in range(1, n_row):
        peer = lax.rem(row + k, n_row)
        send(out_second.at[peer], got_second.at[row], sb, rb, peer, row, (peer, col))
    for copy in own:
        copy.wait()
    for k in range(1, n_col):
        src = lax.rem(col + k, n_col)
        pltpu.make_async_copy(total.at[src], total.at[src], r3.at[src]).wait()

    per_device, rank = coef.shape
    base = (row * n_col + col) * per_device
    piece, group = reduced.shape[0], reduced.shape[0] * n_col
    block = lax.broadcasted_iota(jnp.int32, (1, 4 * rank), 1) // rank
    for c in range(per_device):
        p = parent[base + c]
        q = lax.rem(p, group)
        found = total[q // piece, pl.ds(lax.rem(q, piece), 1), :]
        parts[c:c + 1, :] = jnp.where(block == p // group, found, 0.0)
    wide = parts[...]
    turned = sum(wide[:, u * rank:(u + 1) * rank] for u in range(4)).T
    for c in range(per_device):
        coef[c:c + 1, :] = jnp.sum(transfer_in[c] * turned[:, c:c + 1], axis=0, keepdims=True)
    turned = coef[...].T
    for c in range(per_device):
        far_part[c:c + 1, :] = jnp.sum(basis_in[c].astype(jnp.float32) * turned[:, c:c + 1], axis=0, keepdims=True)

    for k in range(1, n_row):
        src = lax.rem(row + k, n_row)
        view = got_second.at[src]
        pltpu.make_async_copy(view, view, rb.at[src]).wait()
    for k in range(1, n_col):
        src = lax.rem(col + k, n_col)
        view = got_first.at[src]
        pltpu.make_async_copy(view, view, ra.at[src]).wait()
    slots = place.shape[1] // 2
    first = got_first[...].astype(jnp.float32).reshape(slots, got_first.shape[2]).astype(jnp.bfloat16)
    second = got_second[...].reshape(slots, got_second.shape[2])
    velocity[...] = (far_part[...] + jnp.dot(place[:, :slots], first, preferred_element_type=jnp.float32)
                     + select_rows(place[:, slots:], second))
    for copy in started:
        copy.wait_send()


def exchange(n_row, n_col, parent, out_first, out_second, reduced, place, transfer, basis):
    smem = pl.BlockSpec(memory_space=pltpu.SMEM)
    vmem = pl.BlockSpec(memory_space=pltpu.VMEM)
    any_space = pl.BlockSpec(memory_space=pl.ANY)
    per_device, width, rank = place.shape[0], out_first.shape[2], transfer.shape[1]
    return pl.pallas_call(
        functools.partial(exchange_kernel, n_row, n_col),
        out_shape=jax.ShapeDtypeStruct((per_device, width), jnp.float32),
        in_specs=[smem] + [vmem] * 4 + [any_space] * 2,
        out_specs=vmem,
        scratch_shapes=[
            pltpu.VMEM(out_first.shape, out_first.dtype), pltpu.VMEM(out_second.shape, out_second.dtype),
            pltpu.VMEM((n_col,) + reduced.shape, jnp.float32), pltpu.VMEM((per_device, 4 * rank), jnp.float32),
            pltpu.VMEM((per_device, rank), jnp.float32),
            pltpu.VMEM((per_device, width), jnp.float32), pltpu.VMEM(transfer.shape, transfer.dtype),
            pltpu.VMEM(basis.shape, basis.dtype),
        ] + [pltpu.SemaphoreType.DMA((size,)) for size in (5, n_col, n_col, n_row, n_row, n_col, n_col)],
        compiler_params=pltpu.CompilerParams(
            collective_id=2, has_side_effects=True, vmem_limit_bytes=32 * 1024 * 1024),
        name="exchange",
    )(parent, out_first, out_second, reduced, place, transfer, basis)


def shards(density, coords, basis, transfer, parent, near_pairs, near_count, far_pairs, coupling):
    per_device, _, panels = density.shape
    n_row, n_col = lax.axis_size("row"), lax.axis_size("col")
    tile = jnp.concatenate([density, coords], axis=1).transpose(1, 0, 2).reshape(6 * per_device, panels)
    row_tiles, col_tiles, row_ids, col_ids, reduced = gather(
        n_row, n_col, tile, near_pairs, far_pairs, parent.reshape(1, -1), basis, transfer, coupling.transpose(1, 2, 0))
    out_first, out_second, place = near(
        per_device, near_pairs, near_count, row_tiles, col_tiles, row_ids, col_ids)
    velocity = exchange(n_row, n_col, parent, out_first, out_second, reduced, place, transfer, basis)
    return velocity.reshape(per_device, 3, panels)


def solution(mesh):
    placed = (
        P(("row", "col"), None, None),
        P(("row", "col"), None, None),
        P(("row", "col"), None, None),
        P(("row", "col"), None, None),
        P(),
        P(None, ("row", "col")),
        P(("row", "col")),
        P(None, ("row", "col")),
        P(("row", "col"), None, None),
    )
    return jax.shard_map(
        shards, mesh=mesh, in_specs=placed, out_specs=P(("row", "col"), None, None), check_vma=False
    )
```

```python
import functools
import math

import jax
import jax.numpy as jnp
from jax import lax
from jax.experimental import pallas as pl
from jax.experimental.pallas import tpu as pltpu
from jax.sharding import PartitionSpec as P

REG_EPS = 0.02
STOKES_SCALE = 1.0 / (8.0 * math.pi)
MESH = pl.DeviceIdType.MESH
GROUP = 4
CHUNK = 16


def greet(n_row, n_col, row, col):
    barrier = pltpu.get_barrier_semaphore()
    for k in range(1, n_col):
        pl.semaphore_signal(barrier, inc=1, device_id=(row, lax.rem(col + k, n_col)), device_id_type=MESH)
    for k in range(1, n_row):
        pl.semaphore_signal(barrier, inc=1, device_id=(lax.rem(row + k, n_row), col), device_id_type=MESH)


def meet(n_row, n_col):
    pl.semaphore_wait(pltpu.get_barrier_semaphore(), n_col + n_row - 2)


def part(ref, index, size):
    return ref.at[pl.ds(pl.multiple_of(index * size, size), size)]


def split(wide, terms=3):
    out = []
    for _ in range(terms - 1):
        term = wide.astype(jnp.bfloat16).astype(jnp.float32)
        out.append(term)
        wide = wide - term
    return out + [wide]


def select_rows(one_hot, wide):
    return sum(jnp.dot(one_hot, term.astype(jnp.bfloat16), preferred_element_type=jnp.float32)
               for term in split(wide))


def as_one_hot(where_true):
    return jnp.where(where_true, 1.0, 0.0).astype(jnp.bfloat16)


def couple(far, coupling, parents, all_lifted, lifted, moved, own_locals):
    rank, total = moved.shape[0], parents.shape[1] // 4
    pairs = far.shape[1]
    for u in range(4):
        turned = pltpu.roll(all_lifted[...], (4 - u) % 4 * rank, 1)
        lifted[:, u] = turned.reshape(lifted.shape[0], lifted.shape[2], 4 * rank)
    clusters = parents.shape[1]
    parent_row = lax.broadcasted_iota(jnp.int32, (total, 1), 0)
    moments = select_rows(as_one_hot(parent_row == parents[...]), lifted[...].reshape(clusters, 4 * rank)[:, :rank])
    lane = lax.broadcasted_iota(jnp.int32, (pairs, total), 1).astype(jnp.float32)
    sources = []
    for side in range(2):
        column = jnp.broadcast_to(far[side:side + 1, :].astype(jnp.float32), (8, pairs)).T[:, 0:1]
        sources.append(select_rows(as_one_hot(lane == column), moments))
    turned = [source.T for source in sources]
    to_second = jnp.zeros((rank, pairs), jnp.float32)
    for r in range(rank):
        block = coupling[r]
        moved[r:r + 1, :] = jnp.sum(block * turned[1], axis=0, keepdims=True)
        to_second = to_second + block * turned[0][r:r + 1]
    value = (select_rows(as_one_hot(parent_row == far[0:1, :]), moved[...].T)
             + select_rows(as_one_hot(parent_row == far[1:2, :]), to_second.T))
    group = own_locals.shape[0]
    own_locals[...] = jnp.concatenate([value[u * group:(u + 1) * group] for u in range(4)], axis=1)


def lift(tile, basis, transfer, lifted):
    per_device, rank, width = basis.shape
    panels = width // 3
    source = tile[...].astype(jnp.float32)
    lane = lax.broadcasted_iota(jnp.int32, (rank, per_device), 1)
    turned = jnp.zeros((rank, per_device), jnp.float32)
    for c in range(per_device):
        total = sum(basis[c, :, i * panels:(i + 1) * panels].astype(jnp.float32)
                    * source[i * per_device + c:i * per_device + c + 1] for i in range(3))
        turned = jnp.where(lane == c, jnp.sum(total, axis=1, keepdims=True), turned)
    moments = turned.T
    turned = jnp.zeros((rank, per_device), jnp.float32)
    for c in range(per_device):
        total = jnp.sum(transfer[c] * moments[c:c + 1], axis=1, keepdims=True)
        turned = jnp.where(lane == c, total, turned)
    value = turned.T
    group = per_device // 4
    lifted[...] = jnp.concatenate([value[u * group:(u + 1) * group] for u in range(4)], axis=1)


def gather_kernel(n_row, n_col, n_z, tile, ids, far, parents, basis, transfer, coupling,
                  row_tiles, col_tiles, row_ids, col_ids, reduced,
                  basis_in, transfer_in, coupling_in, lifted, all_lifted, natural, moved, partial, f1, f2, acc,
                  own_sem, in_sem, st, rt, sct, rct, si, ri, sci, rci, sl, rl, scl, rcl, s1, r1, s2, r2):
    row, col = lax.axis_index("row"), lax.axis_index("col")
    n_y = n_col // n_z
    z, y = col // n_y, lax.rem(col, n_y)
    rows, lift_rows = tile.shape[0], lifted.shape[0]
    piece = partial.shape[0] // n_col
    span = n_col * lift_rows
    loads = [
        pltpu.make_async_copy(basis, basis_in, in_sem.at[0]),
        pltpu.make_async_copy(transfer, transfer_in, in_sem.at[1]),
        pltpu.make_async_copy(coupling, coupling_in, in_sem.at[2]),
    ]
    for copy in loads:
        copy.start()
    greet(n_row, n_col, row, col)
    own = [
        pltpu.make_async_copy(tile, part(row_tiles, col, rows), own_sem.at[0]),
        pltpu.make_async_copy(tile, part(col_tiles, row, rows), own_sem.at[1]),
        pltpu.make_async_copy(ids, row_ids.at[col], own_sem.at[2]),
        pltpu.make_async_copy(ids, col_ids.at[row], own_sem.at[3]),
    ]
    for copy in own:
        copy.start()
    loads[0].wait()
    loads[1].wait()
    lift(tile, basis_in, transfer_in, lifted)
    mine = pltpu.make_async_copy(lifted, part(all_lifted, row * n_col + col, lift_rows), own_sem.at[4])
    mine.start()
    meet(n_row, n_col)
    started = []

    def send(src, dst, sends, slot, recvs, index, device):
        copy = pltpu.make_async_remote_copy(
            src_ref=src, dst_ref=dst, send_sem=sends.at[slot], recv_sem=recvs.at[index],
            device_id=device, device_id_type=MESH)
        copy.start()
        started.append(copy)

    def arrive(view, sem):
        pltpu.make_async_copy(view, view, sem).wait()

    col_peers = [lax.rem(col + k, n_col) for k in range(1, n_col)]
    row_peers = [lax.rem(row + k, n_row) for k in range(1, n_row)]

    def forward(k):
        src = lax.rem(z + k, n_z) * n_y + y
        view = part(row_tiles, src, rows)
        arrive(view, rt.at[src])
        for j in range(1, n_y):
            send(view, view, st, n_z + n_y * k + j, rt, src, (row, z * n_y + lax.rem(y + j, n_y)))

    for peer in col_peers:
        send(lifted, part(all_lifted, row * n_col + col, lift_rows), sl, peer, rl, col, (row, peer))
    for k in range(1, n_z):
        send(tile, part(row_tiles, col, rows), st, k, rt, col, (row, lax.rem(z + k, n_z) * n_y + y))
    for k in range(1, n_y):
        send(tile, part(row_tiles, col, rows), st, n_z + k, rt, col, (row, z * n_y + lax.rem(y + k, n_y)))
    for peer in row_peers:
        send(tile, part(col_tiles, row, rows), sct, peer, rct, row, (peer, col))
        send(ids, col_ids.at[row], sci, peer, rci, row, (peer, col))
    for peer in col_peers:
        send(ids, row_ids.at[col], si, peer, ri, col, (row, peer))

    mine.wait()
    for src in col_peers:
        arrive(part(all_lifted, row * n_col + src, lift_rows), rl.at[src])
    for peer in row_peers:
        send(part(all_lifted, row, span), part(all_lifted, row, span), scl, peer, rcl, row, (peer, col))
    loads[2].wait()
    for src in row_peers:
        arrive(part(all_lifted, src, span), rcl.at[src])
    couple(far, coupling_in, parents, all_lifted, natural, moved, partial)
    f1[pl.ds(col, 1)] = partial[pl.ds(pl.multiple_of(col * piece, piece), piece), :][None]
    for peer in col_peers:
        send(part(partial, peer, piece), f1.at[col], s1, peer, r1, col, (row, peer))
    for k in range(1, n_z):
        forward(k)

    for src in col_peers:
        arrive(f1.at[src], r1.at[src])
    acc[...] = jnp.sum(f1[...], axis=0)
    f2[pl.ds(row, 1)] = acc[...][None]
    for peer in row_peers:
        send(acc, f2.at[row], s2, peer, r2, row, (peer, col))
    for src in row_peers:
        arrive(f2.at[src], r2.at[src])
    reduced[...] = jnp.sum(f2[...], axis=0)

    for j in range(1, n_y):
        for k in range(n_z):
            src = lax.rem(z + k, n_z) * n_y + lax.rem(y + j, n_y)
            arrive(part(row_tiles, src, rows), rt.at[src])
    for src in col_peers:
        arrive(row_ids.at[src], ri.at[src])
    for src in row_peers:
        arrive(part(col_tiles, src, rows), rct.at[src])
        arrive(col_ids.at[src], rci.at[src])
    for copy in own:
        copy.wait()
    for copy in started:
        copy.wait_send()


def gather(n_row, n_col, tile, ids, far, parents, basis, transfer, coupling):
    n_z = 4 if n_col % 4 == 0 else 1
    vmem = pl.BlockSpec(memory_space=pltpu.VMEM)
    any_space = pl.BlockSpec(memory_space=pl.ANY)
    per_device, rank = basis.shape[:2]
    clusters, parent_total = parents.shape[1], parents.shape[1] // 4
    piece = parent_total // 4 // n_col
    steps = n_z * (n_col // n_z + 1) + n_col
    sizes = [5, 3, steps, n_col, n_row, n_row, n_col, n_col, n_row, n_row, n_col, n_col, n_row, n_row,
             n_col, n_col, n_row, n_row]
    shape = jax.ShapeDtypeStruct
    group = per_device // 4
    buffers = [transfer.shape, coupling.shape, (group, 4 * rank), (clusters // 4, 4 * rank),
               (clusters // per_device, 4, group, 4 * rank), (rank, coupling.shape[2]),
               (parent_total // 4, 4 * rank), (n_col, piece, 4 * rank), (n_row, piece, 4 * rank), (piece, 4 * rank)]
    return pl.pallas_call(
        functools.partial(gather_kernel, n_row, n_col, n_z),
        out_shape=[
            shape((n_col * tile.shape[0], tile.shape[1]), tile.dtype),
            shape((n_row * tile.shape[0], tile.shape[1]), tile.dtype),
            shape((n_col,) + ids.shape, ids.dtype),
            shape((n_row,) + ids.shape, ids.dtype),
            shape((piece, 4 * rank), jnp.float32),
        ],
        in_specs=[vmem] * 4 + [any_space] * 3,
        out_specs=[vmem] * 5,
        scratch_shapes=[pltpu.VMEM(basis.shape, basis.dtype)] + [pltpu.VMEM(size, jnp.float32) for size in buffers]
        + [pltpu.SemaphoreType.DMA((size,)) for size in sizes],
        compiler_params=pltpu.CompilerParams(
            collective_id=1, has_side_effects=True, vmem_limit_bytes=32 * 1024 * 1024),
        name="gather",
    )(tile, ids, far, parents, basis, transfer, coupling)


def placement(row_ids, col_ids, place):
    per_device, slots = place.shape[0], row_ids.shape[2]
    n_row, n_col = col_ids.shape[0], row_ids.shape[0]
    row, col = lax.axis_index("row"), lax.axis_index("col")
    base = (row * n_col + col) * per_device
    lane = lax.broadcasted_iota(jnp.int32, (8, slots), 1)
    cluster = lax.broadcasted_iota(jnp.int32, (per_device, slots), 0) + base
    for ids, side, sources, mine, start in ((row_ids, 0, n_col, col, 0), (col_ids, 1, n_row, row, slots)):
        size = slots // sources
        owners = jnp.zeros((8, slots), jnp.int32)
        for src in range(sources):
            from_src = jnp.broadcast_to(ids[src, side:side + 1, :], (8, slots))
            shift = lax.rem((src - mine) * size + slots, slots)
            owners = jnp.where(lane // size == src, pltpu.roll(from_src, shift, 1), owners)
        place[:, start:start + slots] = as_one_hot(cluster == owners[0:1, :])


def near_kernel(per_device, pairs, live, row_tiles, col_tiles, row_ids, col_ids,
                sent_first, sent_second, place, out_first, out_second, row_wide, col_wide, radius_sq, inv, cube):
    for narrow, wide in ((row_tiles, row_wide), (col_tiles, col_wide)):
        for src in range(narrow.shape[0] // (6 * per_device)):
            for i in range(8):
                if i < 6:
                    start = (src * 6 + i) * per_device
                    rows = narrow[start:start + per_device, :].astype(jnp.float32)
                else:
                    rows = jnp.full((per_device, narrow.shape[1]), 7.0 - i, jnp.float32)
                for half in range(2):
                    at = pl.ds(src * per_device * 8 + i, per_device, stride=8)
                    wide[half, at, :] = rows[:, half * 128:(half + 1) * 128]

    placement(row_ids, col_ids, place)
    row_span = per_device * row_ids.shape[0]
    row_base = lax.axis_index("row") * row_span
    out_first[...] = jnp.zeros_like(out_first)
    out_second[...] = jnp.zeros_like(out_second)
    panels = row_tiles.shape[1]
    count = live[0]
    eps_sq = REG_EPS * REG_EPS
    across = (((1,), (1,)), ((), ()))
    down = (((1,), (0,)), ((), ()))

    sub = lax.broadcasted_iota(jnp.int32, (8, panels), 0)
    ones = jnp.ones((1, panels), jnp.float32)

    def prepare(tile):
        products = [tile * tile[3 + i:4 + i, :] for i in range(3)]
        y_f = products[0][0:1] + products[1][1:2] + products[2][2:3]
        y_y = products[0][3:4] + products[1][4:5] + products[2][5:6]
        blocks = [tile]
        for product in products:
            high = product.astype(jnp.bfloat16).astype(jnp.float32)
            blocks += [high, product - high]
        blocks += split(tile * y_f)
        return jnp.concatenate(blocks, axis=0).astype(jnp.bfloat16), y_y

    def distances(ta, tb, xx, yy, u):
        x_high, x_mid, x_low = split(xx)
        y_high, y_mid, y_low = split(yy + eps_sq)
        left0 = jnp.where(sub == 0, x_high, jnp.where(sub == 1, x_mid, jnp.where(sub == 2, x_low, jnp.where(
            sub < 6, -2.0 * ta, ta))))
        right0 = jnp.where(sub < 3, ones, jnp.where(sub == 6, y_high, tb))
        left1 = jnp.where(sub < 2, ones, 0.0)
        right1 = jnp.where(sub == 0, y_mid, jnp.where(sub == 1, y_low, 0.0))
        left = jnp.concatenate([left0, left1], axis=0).T.astype(jnp.bfloat16)
        right = jnp.concatenate([right0, right1], axis=0).astype(jnp.bfloat16)
        radius_sq[u] = jnp.dot(left, right, preferred_element_type=jnp.float32)

    def combine(near_inv, near_cube, tile):
        x = tile[3:6]
        s = near_cube[0:3]
        value = near_inv[0:3] + eps_sq * s
        last = near_cube[56:64] + near_cube[64:72] + near_cube[72:80]
        dotted = jnp.sum(x * s, axis=0, keepdims=True) - last[6:7]
        value = value + (x * dotted + last[3:6])
        cross = [jnp.sum(x * (near_cube[8 + 16 * i:11 + 16 * i] + near_cube[16 + 16 * i:19 + 16 * i]), axis=0,
                         keepdims=True) for i in range(3)]
        return [(value[i:i + 1] - cross[i]) * STOKES_SCALE for i in range(3)]

    def fetch(wide, local):
        at = pl.ds(pl.multiple_of(local * 8, 8), 8)
        return jnp.concatenate([wide[0, at, :], wide[1, at, :]], axis=1)

    def begin(slot, u):
        b = pairs[1, slot]
        ta = fetch(row_wide, pairs[0, slot] - row_base)
        tb = fetch(col_wide, b // row_span * per_device + b % per_device)
        ra, xx = prepare(ta)
        rb, yy = prepare(tb)
        distances(ta, tb, xx, yy, u)
        return ta, tb, ra, rb

    def finish(slot, u, ta, tb, ra, rb):
        for chunk in range(panels // CHUNK):
            at = slice(chunk * CHUNK, (chunk + 1) * CHUNK)
            inv_dist = lax.rsqrt(radius_sq[u, at, :])
            inv[u, at, :] = inv_dist.astype(jnp.bfloat16)
            cube[u, at, :] = (inv_dist * inv_dist * inv_dist).astype(jnp.bfloat16)
        product = functools.partial(lax.dot_general, preferred_element_type=jnp.float32)
        to_first = combine(product(rb[0:16], inv[u], across), product(rb, cube[u], across), ta)
        to_second = combine(product(ra[0:16], inv[u], down), product(ra, cube[u], down), tb)
        within = slot < count
        keep_second = within & (pairs[0, slot] != pairs[1, slot])
        for i in range(3):
            at = slice(i * panels, (i + 1) * panels)
            out_first[pl.ds(slot, 1), at] = jnp.where(within, to_first[i], 0.0)
            out_second[pl.ds(slot, 1), at] = jnp.where(keep_second, to_second[i], 0.0)

    def group(step, carry):
        held = begin(step * GROUP, 0)
        for u in range(GROUP):
            ahead = begin(step * GROUP + u + 1, u + 1) if u + 1 < GROUP else None
            finish(step * GROUP + u, u, *held)
            held = ahead
        return carry

    lax.fori_loop(0, (count + GROUP - 1) // GROUP, group, 0)
    for out, sent in ((out_first, sent_first), (out_second, sent_second)):
        size = sent.shape[1]
        for k in range(sent.shape[0]):
            sent[k] = out[k * size:(k + 1) * size, :].astype(sent.dtype)


def near(per_device, pairs, live, row_tiles, col_tiles, row_ids, col_ids):
    slots, panels = pairs.shape[1], row_tiles.shape[1]
    n_col, n_row = row_ids.shape[0], col_ids.shape[0]
    smem = pl.BlockSpec(memory_space=pltpu.SMEM)
    vmem = pl.BlockSpec(memory_space=pltpu.VMEM)
    shape = jax.ShapeDtypeStruct
    return pl.pallas_call(
        functools.partial(near_kernel, per_device),
        out_shape=[shape((n_col, slots // n_col, 3 * panels), jnp.bfloat16),
                   shape((n_row, slots // n_row, 3 * panels), jnp.float32),
                   shape((per_device, 2 * slots), jnp.bfloat16)],
        in_specs=[smem, smem] + [vmem] * 4,
        out_specs=[vmem] * 3,
        scratch_shapes=[pltpu.VMEM((slots, 3 * panels), jnp.float32)] * 2 + [
            pltpu.VMEM((2, row_tiles.shape[0] // 6 * 8, 128), jnp.float32),
            pltpu.VMEM((2, col_tiles.shape[0] // 6 * 8, 128), jnp.float32),
            pltpu.VMEM((GROUP, panels, panels), jnp.float32),
        ] + [pltpu.VMEM((GROUP, panels, panels), jnp.bfloat16)] * 2,
        compiler_params=pltpu.CompilerParams(vmem_limit_bytes=48 * 1024 * 1024),
        name="near",
    )(pairs, live, row_tiles, col_tiles, row_ids, col_ids)


def exchange_kernel(n_row, n_col, parent, out_first, out_second, reduced, place, transfer, basis, velocity,
                    got_first, got_second, total, parts, coef, far_part, transfer_in, basis_in, own_sem, sa, ra, sb, rb, s3, r3):
    row, col = lax.axis_index("row"), lax.axis_index("col")
    own = [
        pltpu.make_async_copy(out_first.at[col], got_first.at[col], own_sem.at[0]),
        pltpu.make_async_copy(out_second.at[row], got_second.at[row], own_sem.at[1]),
        pltpu.make_async_copy(transfer, transfer_in, own_sem.at[2]),
        pltpu.make_async_copy(basis, basis_in, own_sem.at[3]),
        pltpu.make_async_copy(reduced, total.at[col], own_sem.at[4]),
    ]
    greet(n_row, n_col, row, col)
    for copy in own:
        copy.start()
    meet(n_row, n_col)
    started = []

    def send(src, dst, sends, recvs, slot, mine, device):
        copy = pltpu.make_async_remote_copy(
            src_ref=src, dst_ref=dst, send_sem=sends.at[slot], recv_sem=recvs.at[mine],
            device_id=device, device_id_type=MESH)
        copy.start()
        started.append(copy)

    for k in range(1, n_col):
        peer = lax.rem(col + k, n_col)
        send(reduced, total.at[col], s3, r3, peer, col, (row, peer))
    for k in range(1, n_col):
        peer = lax.rem(col + k, n_col)
        send(out_first.at[peer], got_first.at[col], sa, ra, peer, col, (row, peer))
    for k in range(1, n_row):
        peer = lax.rem(row + k, n_row)
        send(out_second.at[peer], got_second.at[row], sb, rb, peer, row, (peer, col))
    for copy in own:
        copy.wait()
    for k in range(1, n_col):
        src = lax.rem(col + k, n_col)
        pltpu.make_async_copy(total.at[src], total.at[src], r3.at[src]).wait()

    per_device, rank = coef.shape
    base = (row * n_col + col) * per_device
    piece, group = reduced.shape[0], reduced.shape[0] * n_col
    block = lax.broadcasted_iota(jnp.int32, (1, 4 * rank), 1) // rank
    for c in range(per_device):
        p = parent[base + c]
        q = lax.rem(p, group)
        found = total[q // piece, pl.ds(lax.rem(q, piece), 1), :]
        parts[c:c + 1, :] = jnp.where(block == p // group, found, 0.0)
    wide = parts[...]
    turned = sum(wide[:, u * rank:(u + 1) * rank] for u in range(4)).T
    for c in range(per_device):
        coef[c:c + 1, :] = jnp.sum(transfer_in[c] * turned[:, c:c + 1], axis=0, keepdims=True)
    turned = coef[...].T
    for c in range(per_device):
        far_part[c:c + 1, :] = jnp.sum(basis_in[c].astype(jnp.float32) * turned[:, c:c + 1], axis=0, keepdims=True)

    for k in range(1, n_row):
        src = lax.rem(row + k, n_row)
        view = got_second.at[src]
        pltpu.make_async_copy(view, view, rb.at[src]).wait()
    for k in range(1, n_col):
        src = lax.rem(col + k, n_col)
        view = got_first.at[src]
        pltpu.make_async_copy(view, view, ra.at[src]).wait()
    slots = place.shape[1] // 2
    first = got_first[...].astype(jnp.float32).reshape(slots, got_first.shape[2]).astype(jnp.bfloat16)
    second = got_second[...].reshape(slots, got_second.shape[2])
    velocity[...] = (far_part[...] + jnp.dot(place[:, :slots], first, preferred_element_type=jnp.float32)
                     + select_rows(place[:, slots:], second))
    for copy in started:
        copy.wait_send()


def exchange(n_row, n_col, parent, out_first, out_second, reduced, place, transfer, basis):
    smem = pl.BlockSpec(memory_space=pltpu.SMEM)
    vmem = pl.BlockSpec(memory_space=pltpu.VMEM)
    any_space = pl.BlockSpec(memory_space=pl.ANY)
    per_device, width, rank = place.shape[0], out_first.shape[2], transfer.shape[1]
    return pl.pallas_call(
        functools.partial(exchange_kernel, n_row, n_col),
        out_shape=jax.ShapeDtypeStruct((per_device, width), jnp.float32),
        in_specs=[smem] + [vmem] * 4 + [any_space] * 2,
        out_specs=vmem,
        scratch_shapes=[
            pltpu.VMEM(out_first.shape, out_first.dtype), pltpu.VMEM(out_second.shape, out_second.dtype),
            pltpu.VMEM((n_col,) + reduced.shape, jnp.float32), pltpu.VMEM((per_device, 4 * rank), jnp.float32),
            pltpu.VMEM((per_device, rank), jnp.float32),
            pltpu.VMEM((per_device, width), jnp.float32), pltpu.VMEM(transfer.shape, transfer.dtype),
            pltpu.VMEM(basis.shape, basis.dtype),
        ] + [pltpu.SemaphoreType.DMA((size,)) for size in (5, n_col, n_col, n_row, n_row, n_col, n_col)],
        compiler_params=pltpu.CompilerParams(
            collective_id=2, has_side_effects=True, vmem_limit_bytes=32 * 1024 * 1024),
        name="exchange",
    )(parent, out_first, out_second, reduced, place, transfer, basis)


def shards(density, coords, basis, transfer, parent, near_pairs, near_count, far_pairs, coupling):
    per_device, _, panels = density.shape
    n_row, n_col = lax.axis_size("row"), lax.axis_size("col")
    tile = jnp.concatenate([density, coords], axis=1).transpose(1, 0, 2).reshape(6 * per_device, panels)
    row_tiles, col_tiles, row_ids, col_ids, reduced = gather(
        n_row, n_col, tile, near_pairs, far_pairs, parent.reshape(1, -1), basis, transfer, coupling.transpose(1, 2, 0))
    out_first, out_second, place = near(
        per_device, near_pairs, near_count, row_tiles, col_tiles, row_ids, col_ids)
    velocity = exchange(n_row, n_col, parent, out_first, out_second, reduced, place, transfer, basis)
    return velocity.reshape(per_device, 3, panels)


def solution(mesh):
    placed = (
        P(("row", "col"), None, None),
        P(("row", "col"), None, None),
        P(("row", "col"), None, None),
        P(("row", "col"), None, None),
        P(),
        P(None, ("row", "col")),
        P(("row", "col")),
        P(None, ("row", "col")),
        P(("row", "col"), None, None),
    )
    return jax.shard_map(
        shards, mesh=mesh, in_specs=placed, out_specs=P(("row", "col"), None, None), check_vma=False
    )
```
